128 devices in a mesh: row: 8 (over z, core), col: 16 (over y, x).
Axes of the slice: x: 4, y: 4, z: 4, core: 2. Of those that a mesh axis runs over, the one named last changes fastest.
Arguments:
- volume: float32 [1280, 16, 256], P(('row', 'col')), may hold values from 0 to 1
- velocity: float32 [3, 1280, 16, 256], P(None, ('row', 'col')), may hold values from -4 to 4
- source: float32 [1280, 16, 256], P(('row', 'col')), may hold values from -6 to 6
- pressure_prev: float32 [1280, 16, 256], P(('row', 'col')), may hold values from -6 to 6
- neighbours: int32 [1024, 6], replicated, may hold values from -1 to 1023, as said below
- levels: int32 [1024], replicated, may hold values from 0 to 2
- refine: int32 [1024], replicated, may hold values 0 or 1
- bounds_old: int32 [129], replicated, may hold values from 0 to 1024, as said below
- bounds_new: int32 [129], replicated, may hold values from 0 to 1024, as said below
Outputs:
- vof_new: float32 [1280, 16, 256], P(('row', 'col'))
- pressure: float32 [1280, 16, 256], P(('row', 'col'))
The draws below stay inside these ranges and needn't reach their ends.
Inputs may be any that keep to these rules, and one draw needn't show every extreme that they name: The grid is a forest of two octrees side by side along i: tiles below 512 form the first tree, the others the second; within a tree, local index g mod (512) gives local coordinates from its bits (bit b is bit b // 3 of coordinate b mod 3), and the second tree's i runs mirrored, so that its tile with local i coordinate q sits at global i = 2 E - 1 - q, E being a tree's extent along i; neighbours[g, f] is the tile one step across face f in global coordinates, or -1 at the grid's boundary and where the face is closed by a wall; faces between the two trees are open; neighbours[g, 2a + 1] = p >= 0 exactly when neighbours[p, 2a] = g. `bounds_old`: entry 0 is 0, the last entry is 1024, and every entry d differs from d * 8 by at most 1; on some device both its first entry is 1 below and its next entry 1 above the even place. `bounds_new`: entry 0 is 0, the last entry is 1024, and every entry d differs from d * 8 by at most 1; on some device both its first entry is 1 below and its next entry 1 above the even place.
All inputs are finite; a program needn't handle non-finite values.
Results may differ from the reference program's by a relative error of at most 0.0003.
Values sent between devices are 32-bit elements; how exact they have to be, the bound alone decides.
No kernel may reach another device: no remote copies, remote signals or barrier semaphores. Data moves between devices by JAX's collectives and lax.ppermute only.
A program may use at most 64 MiB of HBM per device.

```python
import jax
import jax.numpy as jnp
from jax import lax

TILE = 16
TILES_DEV = 8
SWEEPS = 4
SHIFT = 1
NT = 1024
SLOTS = 1280


def draw_bounds(base_key, chosen):
    device_count = NT // TILES_DEV
    offsets = jax.random.randint(base_key, (device_count + 1,), -SHIFT, SHIFT + 1)
    places = jnp.arange(device_count + 1, dtype=jnp.int32)
    offsets = jnp.where(places == chosen, -SHIFT, offsets)
    offsets = jnp.where(places == chosen + 1, SHIFT, offsets)
    offsets = jnp.where((places == 0) | (places == device_count), 0, offsets)
    return (places * TILES_DEV + offsets).astype(jnp.int32)


def draw_bounds_old(key, part):
    key = jax.random.fold_in(key, 11)
    device_count = NT // TILES_DEV
    chosen = jax.random.randint(jax.random.fold_in(key, 7), (), 1, device_count - 1)
    return draw_bounds(key, chosen)


def draw_bounds_new(key, part):
    key = jax.random.fold_in(key, 23)
    return draw_bounds(key, 1)


def encode_tiles(coord_list, bit_count):
    tile_code = jnp.zeros_like(coord_list[0])
    for bit_index in range(bit_count):
        coord_one = coord_list[bit_index % 3]
        tile_code = tile_code + coord_one // 2 ** (bit_index // 3) % 2 * 2 ** bit_index
    return tile_code.astype(jnp.int32)


def encode_forest(coord_list, local_bits, first_extent):
    upper_tree = coord_list[0] >= first_extent
    local_first = jnp.where(upper_tree, 2 * first_extent - 1 - coord_list[0], coord_list[0])
    local_code = encode_tiles([local_first, coord_list[1], coord_list[2]], local_bits)
    return (local_code + upper_tree.astype(jnp.int32) * 2 ** local_bits).astype(jnp.int32)


def draw_neighbours(key, part):
    key = jax.random.fold_in(key, 41)
    local_bits = int(NT).bit_length() - 2
    half_count = NT // 2
    tile_ids = jnp.arange(NT, dtype=jnp.int32)
    upper_tree = tile_ids >= half_count
    local_ids = tile_ids % half_count
    local_coords = [jnp.zeros((NT,), jnp.int32), jnp.zeros((NT,), jnp.int32), jnp.zeros((NT,), jnp.int32)]
    extent_list = [1, 1, 1]
    for bit_index in range(local_bits):
        axis_id = bit_index % 3
        local_coords[axis_id] = local_coords[axis_id] + local_ids // 2 ** bit_index % 2 * 2 ** (bit_index // 3)
        extent_list[axis_id] = extent_list[axis_id] * 2
    first_extent = extent_list[0]
    coord_list = [jnp.where(upper_tree, 2 * first_extent - 1 - local_coords[0], local_coords[0]), local_coords[1], local_coords[2]]
    global_extent = [2 * first_extent, extent_list[1], extent_list[2]]
    closed_draw = jax.random.randint(key, (NT, 3), 0, 8) == 0
    columns = []
    for axis_id in range(3):
        raised = list(coord_list)
        raised[axis_id] = coord_list[axis_id] + 1
        has_above = coord_list[axis_id] + 1 < global_extent[axis_id]
        above_tile = encode_forest([jnp.minimum(raised[0], global_extent[0] - 1), jnp.minimum(raised[1], global_extent[1] - 1), jnp.minimum(raised[2], global_extent[2] - 1)], local_bits, first_extent)
        safe_above = jnp.where(has_above, above_tile, 0)
        kept_open = (tile_ids < 2 * TILES_DEV) & (safe_above < 2 * TILES_DEV)
        if axis_id == 0:
            kept_open = kept_open | (coord_list[0] == first_extent - 1)
        high_open = has_above & jnp.logical_not(closed_draw[:, axis_id] & jnp.logical_not(kept_open))
        sunken = list(coord_list)
        sunken[axis_id] = coord_list[axis_id] - 1
        has_below = coord_list[axis_id] >= 1
        below_tile = encode_forest([jnp.maximum(entry, 0) for entry in sunken], local_bits, first_extent)
        safe_below = jnp.where(has_below, below_tile, 0)
        low_open = has_below & high_open[safe_below]
        columns.append(jnp.where(low_open, safe_below, -1))
        columns.append(jnp.where(high_open, safe_above, -1))
    return jnp.stack(columns, axis=1).astype(jnp.int32)


def set_ends(values, key, low, top_value):
    longest = values.shape.index(max(values.shape))
    spots = []
    for shift in (0, 1):
        where = [jax.random.randint(jax.random.fold_in(key, axis), (), 0, length) for axis, length in enumerate(values.shape)]
        where[longest] = (where[longest] + shift) % values.shape[longest]
        spots.append(tuple(where))
    return values.at[spots[0]].set(low).at[spots[1]].set(top_value)


def level_of(key, shape, pieces, smallest, top_value):
    def one(dim, shards_of):
        steps = jax.random.uniform(jax.random.fold_in(jax.random.fold_in(key, 6), dim), (shards_of,), jnp.float32, smallest / len(pieces), top_value / len(pieces))
        return jnp.repeat(jnp.exp(steps), shape[dim] // shards_of).reshape((-1,) + (1,) * (len(shape) - dim - 1))

    factor_of = one(*pieces[0])
    for cut in pieces[1:]:
        factor_of = factor_of * one(*cut)
    return factor_of


def bell_draw(stream_key, extent, scale, bound, shards=(), kind=jnp.bfloat16):
    entries = scale * jax.random.normal(stream_key, extent, jnp.float32)
    if shards:
        entries = entries * level_of(stream_key, extent, shards, -0.22, 0.18)
    return jnp.clip(entries, -bound, bound).astype(kind)


def setup_inputs(seed: int = 0) -> dict:
    key_list = jax.random.split(jax.random.key(seed), 10)
    volume = jnp.clip(1.0 * jax.random.uniform(key_list[0], (SLOTS, TILE, TILE * TILE), jnp.float32) ** level_of(key_list[0], (SLOTS, TILE, TILE * TILE), ((0, 128),), -0.2, 0.2), 0.0, 1.0)
    velocity = bell_draw(key_list[1], (3, SLOTS, TILE, TILE * TILE), 1.0, 4.0, ((1, 128),), jnp.float32)
    source = bell_draw(key_list[2], (SLOTS, TILE, TILE * TILE), 1.0, 6.0, ((0, 128),), jnp.float32)
    pressure_prev = bell_draw(key_list[3], (SLOTS, TILE, TILE * TILE), 1.0, 6.0, ((0, 128),), jnp.float32)
    neighbours = draw_neighbours(jax.random.fold_in(key_list[9], 71), 0)
    levels = set_ends(jax.random.randint(key_list[5], (NT,), 0, 3), jax.random.fold_in(key_list[5], 1), 0, 2).astype(jnp.int32)
    refine = set_ends((jax.random.randint(key_list[6], (NT,), 0, 3) < 1).astype(jnp.int32), jax.random.fold_in(key_list[6], 1), 0, 1)
    bounds_old = draw_bounds_old(jax.random.fold_in(key_list[9], 71), 0)
    bounds_new = draw_bounds_new(jax.random.fold_in(key_list[9], 71), 0)
    return dict(volume=volume, velocity=velocity, source=source, pressure_prev=pressure_prev, neighbours=neighbours, levels=levels, refine=refine, bounds_old=bounds_old, bounds_new=bounds_new)


CFL = 0.4
SIGMA = 0.05
RHO_GAS = 0.05
RHO_LIQ = 1.0

def line_up(field_in, direction):
    tile_count, tile_edge, plane_size = field_in.shape
    cube = field_in.reshape(tile_count, tile_edge, tile_edge, tile_edge)
    if direction == 1:
        cube = cube.transpose(0, 2, 1, 3)
    if direction == 2:
        cube = cube.transpose(0, 3, 1, 2)
    return cube.reshape(tile_count, tile_edge, plane_size)

def line_back(field_in, direction):
    tile_count, tile_edge, plane_size = field_in.shape
    cube = field_in.reshape(tile_count, tile_edge, tile_edge, tile_edge)
    if direction == 1:
        cube = cube.transpose(0, 2, 1, 3)
    if direction == 2:
        cube = cube.transpose(0, 2, 3, 1)
    return cube.reshape(tile_count, tile_edge, plane_size)

def opposite_faces(face_count):
    face_ids = jnp.arange(face_count, dtype=jnp.int32)
    return face_ids + 1 - 2 * (face_ids % 2)

def advect_planes(volume, velocity):
    tile_edge = volume.shape[1]
    planes = []
    for direction in range(3):
        vol_line = line_up(volume, direction)
        vel_line = line_up(velocity[direction], direction)
        planes.append(jnp.concatenate([vol_line[:, :2], vel_line[:, :1]], axis=1))
        planes.append(jnp.concatenate([vol_line[:, tile_edge - 2:], vel_line[:, tile_edge - 1:]], axis=1))
    return jnp.stack(planes, axis=1)

def rim_planes(field_in, face_count):
    tile_edge = field_in.shape[1]
    planes = []
    for direction in range(face_count // 2):
        line_view = line_up(field_in, direction)
        planes.append(line_view[:, :1])
        planes.append(line_view[:, tile_edge - 1:])
    return jnp.stack(planes, axis=1)

def advect(volume, velocity, ghosts, spacing, time_step):
    change = jnp.zeros_like(volume)
    for direction in range(3):
        low_side = ghosts[:, 2 * direction]
        high_side = ghosts[:, 2 * direction + 1]
        vol_ext = jnp.concatenate([low_side[:, :2], line_up(volume, direction), high_side[:, :2]], axis=1)
        vel_ext = jnp.concatenate([low_side[:, 2:], line_up(velocity[direction], direction), high_side[:, 2:]], axis=1)
        upper_diff = vol_ext[:, 2:] - vol_ext[:, 1:-1]
        lower_diff = vol_ext[:, 1:-1] - vol_ext[:, :-2]
        slopes = 0.5 * (jnp.sign(upper_diff) + jnp.sign(lower_diff)) * jnp.minimum(jnp.abs(upper_diff), jnp.abs(lower_diff))
        centre = vol_ext[:, 1:-1]
        left_state = centre[:, :-1] + 0.5 * slopes[:, :-1]
        right_state = centre[:, 1:] - 0.5 * slopes[:, 1:]
        face_vel = 0.5 * (vel_ext[:, :-1] + vel_ext[:, 1:])
        fluxes = jnp.maximum(face_vel, 0.0) * left_state + jnp.minimum(face_vel, 0.0) * right_state
        change = change + line_back(fluxes[:, 1:] - fluxes[:, :-1], direction)
    return jnp.clip(volume - (time_step / spacing)[:, None, None] * change, 0.0, 1.0)

def heights(volume, ghosts):
    tile_edge = volume.shape[1]
    vol_ext = jnp.concatenate([ghosts[:, 4, :2], line_up(volume, 2), ghosts[:, 5, :2]], axis=1)
    running = vol_ext[:, 0:tile_edge]
    for layer_shift in range(1, 5):
        running = running + vol_ext[:, layer_shift:layer_shift + tile_edge]
    return line_back(running, 2)

def curvature(height, ghosts, spacing):
    grads = []
    seconds = []
    for direction in range(2):
        extended = jnp.concatenate([ghosts[:, 2 * direction], line_up(height, direction), ghosts[:, 2 * direction + 1]], axis=1)
        grads.append(line_back(0.5 * (extended[:, 2:] - extended[:, :-2]), direction))
        seconds.append(line_back(extended[:, 2:] - 2.0 * extended[:, 1:-1] + extended[:, :-2], direction))
    grad_x, grad_y = grads
    second_x, second_y = seconds
    slope_sq = 1.0 + grad_x * grad_x + grad_y * grad_y
    upper_part = second_x * (1.0 + grad_y * grad_y) + second_y * (1.0 + grad_x * grad_x)
    return -upper_part / (spacing[:, None, None] * slope_sq * jnp.sqrt(slope_sq))

def jacobi_weights(mobility, ghosts, spacing, face_spacing):
    tile_count, tile_edge = (mobility.shape[0], mobility.shape[1])
    inside = jnp.ones((tile_count, tile_edge - 1), jnp.float32)
    weights = []
    diagonal = jnp.zeros_like(mobility)
    for direction in range(3):
        extended = jnp.concatenate([ghosts[:, 2 * direction], line_up(mobility, direction), ghosts[:, 2 * direction + 1]], axis=1)
        low_scale = (spacing / face_spacing[:, 2 * direction])[:, None]
        high_scale = (spacing / face_spacing[:, 2 * direction + 1])[:, None]
        end_scale = jnp.concatenate([low_scale, inside, high_scale], axis=1) / (spacing * spacing)[:, None]
        face_weight = 0.5 * (extended[:, :-1] + extended[:, 1:]) * end_scale[:, :, None]
        weights.append(face_weight)
        diagonal = diagonal + line_back(face_weight[:, :-1] + face_weight[:, 1:], direction)
    return (weights, diagonal)

def relax_sweep(pressure, ghosts, weights, diagonal, right_side):
    running = -right_side
    for direction in range(3):
        extended = jnp.concatenate([ghosts[:, 2 * direction], line_up(pressure, direction), ghosts[:, 2 * direction + 1]], axis=1)
        face_weight = weights[direction]
        running = running + line_back(face_weight[:, :-1] * extended[:, :-2] + face_weight[:, 1:] * extended[:, 2:], direction)
    return running / diagonal

def global_ghosts(planes, partner):
    face_count = planes.shape[1]
    safe_partner = jnp.maximum(partner, 0)
    gathered = planes[safe_partner, opposite_faces(face_count)[None, :]]
    return jnp.where((partner >= 0)[:, :, None, None], gathered, 0.0)

def reference(volume, velocity, source, pressure_prev, neighbours, levels, refine, bounds_old, bounds_new):
    device_count = bounds_old.shape[0] - 1
    slot_total = volume.shape[0]
    slot_count = slot_total // device_count
    tile_total = neighbours.shape[0]
    tile_ids = jnp.arange(tile_total, dtype=jnp.int32)
    owner = lax.optimization_barrier(jnp.sum((bounds_old[None, 1:device_count] <= tile_ids[:, None]).astype(jnp.int32), axis=1))
    old_rows = (owner * slot_count + tile_ids - bounds_old[owner]).astype(jnp.int32)
    tile_volume = volume[old_rows]
    tile_velocity = velocity[:, old_rows]
    tile_source = source[old_rows]
    tile_prev = pressure_prev[old_rows]
    spacing = jnp.exp2(-levels.astype(jnp.float32))
    speed_ratio = (jnp.abs(tile_velocity[0]) + jnp.abs(tile_velocity[1]) + jnp.abs(tile_velocity[2])) / spacing[:, None, None]
    time_step = CFL / jnp.max(speed_ratio)
    ghosts = global_ghosts(advect_planes(tile_volume, tile_velocity), neighbours)
    volume_adv = advect(tile_volume, tile_velocity, ghosts, spacing, time_step)
    height = heights(tile_volume, ghosts)
    height_ghosts = global_ghosts(rim_planes(height, 4), neighbours[:, :4])
    bending = curvature(height, height_ghosts, spacing)
    right_side = tile_source + SIGMA * bending * volume_adv
    new_spacing = jnp.exp2(-(levels + refine).astype(jnp.float32))
    partner_spacing = jnp.where(neighbours >= 0, new_spacing[jnp.maximum(neighbours, 0)], new_spacing[:, None])
    face_spacing = 0.5 * (new_spacing[:, None] + partner_spacing)
    mobility = 1.0 / (RHO_GAS + (RHO_LIQ - RHO_GAS) * volume_adv)
    mobility_ghosts = global_ghosts(rim_planes(mobility, 6), neighbours)
    weights, diagonal = jacobi_weights(mobility, mobility_ghosts, new_spacing, face_spacing)
    pressure_tiles = tile_prev
    for sweep_index in range(SWEEPS):
        pressure_ghosts = global_ghosts(rim_planes(pressure_tiles, 6), neighbours)
        pressure_tiles = relax_sweep(pressure_tiles, pressure_ghosts, weights, diagonal, right_side)
    slot_ids = jnp.arange(slot_total, dtype=jnp.int32)
    device_of = slot_ids // slot_count
    tile_of = bounds_new[device_of] + slot_ids % slot_count
    live_slot = tile_of < bounds_new[device_of + 1]
    safe_tile = jnp.minimum(tile_of, tile_total - 1).astype(jnp.int32)
    vof_new = jnp.where(live_slot[:, None, None], volume_adv[safe_tile], 0.0)
    pressure = jnp.where(live_slot[:, None, None], pressure_tiles[safe_tile], 0.0)
    return (vof_new, pressure)
```

```python
import jax
import jax.numpy as jnp
from jax import lax
from jax.experimental import pallas as pl
from jax.experimental.pallas import tpu as pltpu
from jax.sharding import PartitionSpec as P

SWEEPS = 4
CFL = 0.4
SIGMA = 0.05
RHO_GAS = 0.05
RHO_LIQ = 1.0
AXES = ("row", "col")
DEVS = 128
F32 = jnp.float32


def block_coords(d):
    tree, low = d >> 6, d & 63
    i = (low & 1) | (((low >> 3) & 1) << 1)
    j = ((low >> 1) & 1) | (((low >> 4) & 1) << 1)
    k = ((low >> 2) & 1) | (((low >> 5) & 1) << 1)
    return (7 - i if tree else i), j, k


PLACE = {block_coords(d): d for d in range(DEVS)}


def axis_pairs(axis, odd):
    count = (8, 4, 4)[axis]
    pairs = []
    for d in range(DEVS):
        c = list(block_coords(d))
        step = 1 if (c[axis] % 2 == 0) != bool(odd) else -1
        c[axis] = (c[axis] + step) % count
        pairs.append((d, PLACE[tuple(c)]))
    return pairs


def flip_pairs(bits):
    return [(d, d ^ bits) for d in range(DEVS)]


EVEN_PAIRS = flip_pairs(1)
ODD_PAIRS = [(d, d + 1 if d % 2 else d - 1) for d in range(1, DEVS - 1)]


def send(x, pairs):
    return lax.ppermute(x, AXES, pairs)


def where_am_i():
    d = lax.axis_index("row") * 16 + lax.axis_index("col")
    tree = d >> 6
    i = (d & 1) | (((d >> 3) & 1) << 1)
    gi = jnp.where(tree == 1, 7 - i, i)
    gj = ((d >> 1) & 1) | (((d >> 4) & 1) << 1)
    gk = ((d >> 2) & 1) | (((d >> 5) & 1) << 1)
    return d, tree, gi, gj, gk


def iotas():
    sub = lax.broadcasted_iota(jnp.int32, (8, 128), 0)
    lane = lax.broadcasted_iota(jnp.int32, (8, 128), 1)
    return sub, lane


def rl(x, shift):
    return pltpu.roll(x, shift % 128, 1)


def rs(x, shift):
    n = x.shape[0]
    return pltpu.roll(x, shift % n, 0)


def halves(h):
    return pl.ds(128 * h, 128)


def old_slice(fields, f, slot, start, count, h):
    vol, vel, src, prev = fields
    rows = pl.ds(pl.multiple_of(start, 8), count)
    if f == 0:
        return vol[slot, rows, halves(h)]
    if f < 4:
        return vel[f - 1, slot, rows, halves(h)]
    return (src if f == 4 else prev)[slot, rows, halves(h)]


def slab_groups(get, high, sub):
    nat = (sub >= 4) == high
    return (
        get(0),
        get(1),
        jnp.where(nat, get(2), rs(get(3), 4)),
        jnp.where(nat, get(5), rs(get(4), 4)),
    )


def first_kernel(vol, vel, src, prev, levels, bounds, ra, rb, peak):
    d, tree, gi, gj, gk = where_am_i()
    sub, lane = iotas()
    fields = (vol, vel, src, prev)
    start = bounds[d]
    count = bounds[d + 1] - start
    off = 8 * d - start
    even = d % 2 == 0
    slot_a = jnp.where(even, 8 + off, 0)
    slot_b = jnp.where(even, 0, 8 + off)
    for f in range(6):
        for r in range(2):
            for h in range(2):
                ra[f * 4 + r * 2 + h] = old_slice(fields, f, slot_a, 8 * r, 8, h)
                rb[f * 4 + r * 2 + h] = old_slice(fields, f, slot_b, 8 * r, 8, h)
    high = gi % 2 == 0
    row0 = jnp.where(high, 8, 0)
    bit = jnp.where(even, 1, 0)
    for q in range(4):
        slot = jnp.clip(bit + 2 * q + off, 0, 9)
        for h in range(2):
            groups = slab_groups(
                lambda f: old_slice(fields, f, slot, row0, 8, h), high, sub
            )
            for g in range(4):
                ra[24 + (g * 4 + q) * 2 + h] = groups[g]
    top = jnp.zeros((8, 128), F32)
    for s in range(10):
        level = levels[jnp.minimum(start + s, 1023)]
        inv = jnp.where(s < count, jnp.left_shift(1, level), 0).astype(F32)
        part = jnp.zeros((8, 128), F32)
        for r in range(2):
            for h in range(2):
                u = [jnp.abs(vel[a, s, pl.ds(8 * r, 8), halves(h)]) for a in range(3)]
                part = jnp.maximum(part, u[0] + u[1] + u[2])
        top = jnp.maximum(top, part * inv)
    ra[56] = top
    peak[0] = top


def second_kernel(vol, vel, src, prev, bounds, peak, ra, rb, x8, x9, ib, peak_out):
    d, tree, gi, gj, gk = where_am_i()
    sub, lane = iotas()
    fields = (vol, vel, src, prev)
    off = 8 * d - bounds[d]
    even = d % 2 == 0
    missing_first = bounds[d] == 8 * d + 1
    missing_last = bounds[d + 1] == 8 * d + 7
    high = gi % 2 == 1
    row0 = jnp.where(high, 8, 0)
    block = jnp.where(high, 2, 0)
    bit = jnp.where(even, 0, 1)
    for q in range(4):
        slot = jnp.clip(bit + 2 * q + off, 0, 9)
        for h in range(2):

            def get(f):
                x = old_slice(fields, f, slot, row0, 8, h)
                if q == 0:
                    x = jnp.where(even & missing_first, rb[f * 4 + block + h], x)
                if q == 3:
                    x = jnp.where(jnp.logical_not(even) & missing_last, rb[f * 4 + block + h], x)
                return x

            groups = slab_groups(get, high, sub)
            for g in range(4):
                ib[(g * 4 + q) * 2 + h] = groups[g]
    peak_out[0] = jnp.maximum(jnp.maximum(peak[0], ra[56]), jnp.maximum(x8[0], x9[0]))


def gather_kernel(vol, vel, src, prev, bounds, ra, rb, ext, ia):
    d, tree, gi, gj, gk = where_am_i()
    sub, lane = iotas()
    fields = (vol, vel, src, prev)
    off = 8 * d - bounds[d]
    even = d % 2 == 0
    missing_first = bounds[d] == 8 * d + 1
    missing_last = bounds[d + 1] == 8 * d + 7
    for t in range(8):
        slot = jnp.clip(t + off, 0, 9)
        bj, bk = (t >> 1) & 1, (t >> 2) & 1
        row0 = 16 * ((t & 1) ^ tree)
        for f in range(6):
            for r in range(2):
                for h in range(2):
                    x = old_slice(fields, f, slot, 8 * r, 8, h)
                    n = f * 4 + r * 2 + h
                    if t == 0:
                        x = jnp.where(missing_first, jnp.where(even, rb[n], ra[n]), x)
                    if t == 7:
                        x = jnp.where(missing_last, jnp.where(even, ra[n], rb[n]), x)
                    ext[f, 2 * bj + h, bk, pl.ds(pl.multiple_of(row0 + 8 * r, 8), 8), :] = x
    high = gi % 2 == 1
    row0 = jnp.where(high, 8, 0)
    slot_a = jnp.where(even, 8 + off, 0)
    sent_first = even & (bounds[d + 1] == 8 * d + 9)
    sent_last = jnp.logical_not(even) & (bounds[d] == 8 * d - 1)
    for q in range(4):
        for h in range(2):
            if q in (0, 3):
                groups = slab_groups(
                    lambda f: old_slice(fields, f, slot_a, row0, 8, h), high, sub
                )
            for g in range(4):
                n = (g * 4 + q) * 2 + h
                x = ra[24 + n]
                if q == 0:
                    x = jnp.where(sent_first, groups[g], x)
                if q == 3:
                    x = jnp.where(sent_last, groups[g], x)
                ia[n] = x


def make_block(ext, ia, ib, gi, sub):
    first_high = gi % 2 == 0

    def pair(g, jq, kt):
        n = (g * 4 + jq // 2 + 2 * kt) * 2 + jq % 2
        a, b = ia[n], ib[n]
        return jnp.where(first_high, a, b), jnp.where(first_high, b, a)

    def rows(f, jq, kt, b):
        if b < 4:
            return ext[f, jq, kt, pl.ds(8 * b, 8), :]
        if f == 0:
            return pair(0, jq, kt)[b - 4]
        hi, lo = pair((1, 1, 2, 2, 3, 3)[f], jq, kt)
        if f in (3, 4):
            return rs(jnp.where(sub < 4, lo, hi), 4)
        return jnp.where(sub < 4, hi, lo)

    return rows, pair


def third_kernel(ext, ia, ib, peak, xa, xb, xc, ja, jb, peak_out):
    d, tree, gi, gj, gk = where_am_i()
    sub, lane = iotas()
    rows, _ = make_block(ext, ia, ib, gi, sub)
    even = gj % 2 == 0

    def pack(jq, kt, g, b):
        if g == 0:
            return rows(0, jq, kt, b)
        if g == 1:
            return rows(2, jq, kt, b)
        fa, fb = ((1, 3), (5, 4))[g - 2]
        nat = lane < 64 if jq == 0 else lane >= 64
        return jnp.where(nat, rows(fa, jq, kt, b), rl(rows(fb, jq, kt, b), 64))

    for g in range(4):
        for kt in range(2):
            for b in range(6 if g == 0 else 5):
                n = kt * 6 + b if g == 0 else 12 + ((g - 1) * 2 + kt) * 5 + b
                lo, hi = pack(0, kt, g, b), pack(3, kt, g, b)
                ja[n] = jnp.where(even, hi, lo)
                jb[n] = jnp.where(even, lo, hi)
    top = jnp.maximum(jnp.maximum(peak[0], xa[0]), jnp.maximum(xb[0], xc[0]))
    ja[42] = top
    peak_out[0] = top


def make_wide(rows, ja, jb, gj):
    first_high = gj % 2 == 0

    def wide(f, jq, kt, b):
        if jq < 4:
            return rows(f, jq, kt, b)
        if f == 0:
            n = kt * 6 + b
        else:
            n = 12 + ((1, 1, 0, 1, 2, 2)[f] * 2 + kt) * 5 + b
        if jq == 4:
            x = jnp.where(first_high, ja[n], jb[n])
        else:
            x = jnp.where(first_high, jb[n], ja[n])
        return rl(x, 64) if f in (3, 4) else x

    return wide


def fourth_kernel(ext, ia, ib, ja, jb, peak, xa, xb, ka, kb):
    d, tree, gi, gj, gk = where_am_i()
    sub, lane = iotas()
    rows, _ = make_block(ext, ia, ib, gi, sub)
    wide = make_wide(rows, ja, jb, gj)
    even = gk % 2 == 0
    near = lane % 16 < 8
    small = lane % 8 < 4

    def squeeze(f, jt, kt, b):
        first, last = wide(f, 2 * jt, kt, b), wide(f, 2 * jt + 1, kt, b)
        if kt == 0:
            return jnp.where(near, first, rl(last, 8))
        return jnp.where(near, rl(first, -8), last)

    def pack(jt, kt, g, b):
        if g == 0:
            return squeeze(0, jt, kt, b)
        if g == 1:
            return squeeze(3, jt, kt, b)
        fa, fb = ((1, 2), (5, 4))[g - 2]
        one, two = squeeze(fa, jt, kt, b), squeeze(fb, jt, kt, b)
        if kt == 0:
            return jnp.where(small, one, rl(two, 4))
        return jnp.where(small, rl(two, -4), one)

    for g in range(4):
        for jt in range(3):
            for b in range(6 if g == 0 else 5):
                n = jt * 6 + b if g == 0 else 18 + ((g - 1) * 3 + jt) * 5 + b
                lo, hi = pack(jt, 0, g, b), pack(jt, 1, g, b)
                ka[n] = jnp.where(even, hi, lo)
                kb[n] = jnp.where(even, lo, hi)
    ka[63] = jnp.maximum(jnp.maximum(peak[0], ja[42]), jnp.maximum(xa[0], xb[0]))


def coefficient_kernel(neighbours, levels, refine, out, table, ratio):
    d, tree, gi, gj, gk = where_am_i()
    sub, lane = iotas()
    for n in range(7):
        ratio[n] = 2.0 / (1.0 + 2.0 ** (n - 3))

    def one(pos, carry):
        ip, jp, kp = pos >> 4, (pos >> 2) & 3, pos & 3
        x = 2 * gi + jnp.where(ip == 3, -1, ip)
        y = 2 * gj + jnp.where(jp == 3, -1, jp)
        z = 2 * gk + jnp.where(kp == 3, -1, kp)
        inside = (x >= 0) & (x < 16) & (y >= 0) & (y < 8) & (z >= 0) & (z < 8)
        upper = x >= 8
        lx = jnp.where(upper, 15 - x, x)
        code = jnp.where(upper, 512, 0)
        for bit in range(3):
            for axis, v in enumerate((lx, y, z)):
                code = code | (((v >> bit) & 1) << (3 * bit + axis))
        code = jnp.where(inside, code, 0)
        level = levels[code]
        depth = level + refine[code]
        for f in range(6):
            p = neighbours[code * 6 + f]
            opened = inside & (p >= 0)
            safe = jnp.maximum(p, 0)
            other = levels[safe] + refine[safe]
            table[f * 64 + pos] = jnp.where(opened, 1.0, 0.0)
            table[(6 + f) * 64 + pos] = jnp.where(opened, ratio[depth - other + 3], 1.0)
        table[12 * 64 + pos] = jnp.left_shift(1, level).astype(F32)
        table[13 * 64 + pos] = jnp.left_shift(1, 6 - 2 * depth).astype(F32) * (2.0 / 64.0)
        return carry

    lax.fori_loop(0, 64, one, 0)

    def expand(step, carry):
        item, jp = step >> 2, step & 3
        base = item * 64 + jp * 4
        vals = {}
        for ip in range(4):
            v = [jnp.full((8, 128), table[base + ip * 16 + kp], F32) for kp in range(4)]
            vals[ip] = (v[0], v[1], jnp.where(lane % 16 < 8, v[2], v[3]))
        for kt in range(3):
            mixed = jnp.where(sub < 4, vals[2][kt], vals[3][kt])
            for b, v in enumerate((vals[0][kt], vals[0][kt], vals[1][kt], vals[1][kt], mixed)):
                out[item, jp, kt, pl.ds(8 * b, 8), :] = v
        return carry

    lax.fori_loop(0, 56, expand, 0)


def minmod(a, b):
    return jnp.maximum(jnp.minimum(a, b), 0.0) + jnp.minimum(jnp.maximum(a, b), 0.0)


def face_change(c, up1, up2, dn1, dn2, u, u_up, u_dn):
    upper, lower = up1 - c, c - dn1
    half = 0.5 * minmod(upper, lower)
    half_up = 0.5 * minmod(up2 - up1, upper)
    half_dn = 0.5 * minmod(lower, dn1 - dn2)
    w_up, w_dn = 0.5 * (u + u_up), 0.5 * (u_dn + u)
    flux_up = jnp.maximum(w_up, 0.0) * (c + half) + jnp.minimum(w_up, 0.0) * (up1 - half_up)
    flux_dn = jnp.maximum(w_dn, 0.0) * (dn1 + half_dn) + jnp.minimum(w_dn, 0.0) * (c - half)
    return flux_up - flux_dn


def main_kernel(
    ext, ia, ib, ja, jb, ka, kb, peak, coef, bounds,
    vof, pres, send_a, send_b,
    c48, v48, c40, u1, u2, src, p0, p1, adv, mob, hgt, rhs, wts,
):
    d, tree, gi, gj, gk = where_am_i()
    sub, lane = iotas()
    rows, pair = make_block(ext, ia, ib, gi, sub)
    wide = make_wide(rows, ja, jb, gj)
    near = lane % 16 < 8
    k_even = gk % 2 == 0
    dest = {1: v48, 2: u1, 3: u2, 4: src, 5: p0}

    def put(f, jq, kt, b, x):
        if f == 0:
            c48[jq, kt, pl.ds(8 * b, 8), :] = x
            if b < 4:
                c40[jq, kt, pl.ds(8 * b, 8), :] = x
        else:
            dest[f][jq, kt, pl.ds(8 * b, 8), :] = x

    for f in range(6):
        for b in range(6 if f == 0 else 5):
            for jq in range(6):
                for kt in range(2):
                    if f == 1 and b == 4:
                        if jq < 4:
                            hi, lo = pair(1, jq, kt)
                        else:
                            hi = lo = wide(1, jq, kt, 4)
                        put(f, jq, kt, 4, hi)
                        put(f, jq, kt, 5, lo)
                    else:
                        put(f, jq, kt, b, wide(f, jq, kt, b))
            for jt in range(3):
                if f == 0:
                    n = jt * 6 + b
                else:
                    n = 18 + ((1, 1, 1, 0, 2, 2)[f] * 3 + jt) * 5 + b
                a, e = ka[n], kb[n]
                low_pack = jnp.where(k_even, a, e)
                high_pack = jnp.where(k_even, e, a)
                if f in (2, 4):
                    low_pack, high_pack = rl(low_pack, -4), rl(high_pack, 4)
                first = jnp.where(near, low_pack, rl(high_pack, 8))
                last = jnp.where(near, rl(low_pack, -8), high_pack)
                put(f, 2 * jt, 2, b, first)
                put(f, 2 * jt + 1, 2, b, last)
                if f == 1 and b == 4:
                    put(f, 2 * jt, 2, 5, first)
                    put(f, 2 * jt + 1, 2, 5, last)
    for jq in range(6):
        for kt in range(3):
            c40[jq, kt, pl.ds(32, 8), :] = jnp.where(
                sub < 4, c48[jq, kt, pl.ds(32, 8), :], c48[jq, kt, pl.ds(40, 8), :]
            )

    top = jnp.max(jnp.maximum(peak[63], ka[63]), keepdims=True)
    step = jnp.broadcast_to(CFL / top, (8, 128))
    step = jnp.concatenate([step] * 5, axis=0)

    row = lax.broadcasted_iota(jnp.int32, (40, 128), 0)
    lane5 = lax.broadcasted_iota(jnp.int32, (40, 128), 1)
    k16 = lane5 % 16
    i_top1 = (row == 15) | (row == 31) | (row == 39)
    i_top2 = i_top1 | (row == 14) | (row == 30) | (row == 38)
    i_bot1 = (row == 0) | (row == 16) | (row == 32)
    i_bot2 = i_bot1 | (row == 1) | (row == 17) | (row == 33)
    sub4 = sub < 4

    def tile_j(jq):
        return jnp.where(jq < 4, jq >> 1, jq - 2)

    def wrap(x):
        return jnp.concatenate([x[:32], jnp.where(sub4, x[32:40], x[40:48])], axis=0)

    def k_up(x, nxt, n, m):
        return jnp.where(k16 < 16 - n, rl(x, -n), m * rl(nxt, 16 - n))

    def k_dn(x, prv, n, m):
        return jnp.where(k16 >= n, rl(x, n), m * rl(prv, n - 16))

    def j_up(x, nxt, n):
        return rl(jnp.where(lane5 < 16 * n, nxt, x), -16 * n)

    def j_dn(x, prv, n):
        return rl(jnp.where(lane5 >= 128 - 16 * n, prv, x), 16 * n)

    def advance(jq, carry):
        jt = tile_j(jq)
        jn, jp = lax.rem(jq + 1, 6), lax.rem(jq + 5, 6)
        odd = jq % 2 == 1
        for kt in range(3):
            kn, kp = (kt + 1) % 3, (kt + 2) % 3
            c = c40[jq, kt]
            m_dn, m_up = coef[4, jt, kt], coef[5, jt, kt]
            cn, cp = c40[jq, kn], c40[jq, kp]
            up1, up2 = k_up(c, cn, 1, m_up), k_up(c, cn, 2, m_up)
            dn1, dn2 = k_dn(c, cp, 1, m_dn), k_dn(c, cp, 2, m_dn)
            hgt[jq, kt] = dn2 + dn1 + c + up1 + up2
            u = u2[jq, kt]
            change = face_change(
                c, up1, up2, dn1, dn2, u, k_up(u, u2[jq, kn], 1, m_up), k_dn(u, u2[jq, kp], 1, m_dn)
            )
            m_dn = jnp.where(odd, 1.0, coef[2, jt, kt])
            m_up = jnp.where(odd, coef[3, jt, kt], 1.0)
            up_m1 = jnp.where(lane5 >= 112, m_up, 1.0)
            up_m2 = jnp.where(lane5 >= 96, m_up, 1.0)
            dn_m1 = jnp.where(lane5 < 16, m_dn, 1.0)
            dn_m2 = jnp.where(lane5 < 32, m_dn, 1.0)
            cn, cp = c40[jn, kt], c40[jp, kt]
            u = u1[jq, kt]
            change = change + face_change(
                c, j_up(c, cn, 1) * up_m1, j_up(c, cn, 2) * up_m2,
                j_dn(c, cp, 1) * dn_m1, j_dn(c, cp, 2) * dn_m2,
                u, j_up(u, u1[jn, kt], 1) * up_m1, j_dn(u, u1[jp, kt], 1) * dn_m1,
            )
            m_dn, m_up = coef[0, jt, kt], coef[1, jt, kt]
            up_m1, up_m2 = jnp.where(i_top1, m_up, 1.0), jnp.where(i_top2, m_up, 1.0)
            dn_m1, dn_m2 = jnp.where(i_bot1, m_dn, 1.0), jnp.where(i_bot2, m_dn, 1.0)
            cc, uu = c48[jq, kt], v48[jq, kt]
            change = change + face_change(
                c, wrap(rs(cc, -1)) * up_m1, wrap(rs(cc, -2)) * up_m2,
                wrap(rs(cc, 1)) * dn_m1, wrap(rs(cc, 2)) * dn_m2,
                wrap(uu), wrap(rs(uu, -1)) * up_m1, wrap(rs(uu, 1)) * dn_m1,
            )
            a = jnp.clip(c - step * coef[12, jt, kt] * change, 0.0, 1.0)
            adv[jq, kt] = a
            mob[jq, kt] = 1.0 / (RHO_GAS + (RHO_LIQ - RHO_GAS) * a)
        return carry

    lax.fori_loop(0, 6, advance, 0)

    def weigh(jq, carry):
        jt = tile_j(jq)
        jn, jp = lax.rem(jq + 1, 6), lax.rem(jq + 5, 6)
        odd = jq % 2 == 1
        for kt in range(3):
            kn, kp = (kt + 1) % 3, (kt + 2) % 3
            mi_dn = jnp.where(i_bot1, coef[0, jt, kt], 1.0)
            mi_up = jnp.where(i_top1, coef[1, jt, kt], 1.0)
            at_dn = (lane5 < 16) & jnp.logical_not(odd)
            at_up = (lane5 >= 112) & odd
            mj_dn = jnp.where(at_dn, coef[2, jt, kt], 1.0)
            mj_up = jnp.where(at_up, coef[3, jt, kt], 1.0)
            h = hgt[jq, kt]
            h_up, h_dn = rs(h, -1) * mi_up, rs(h, 1) * mi_dn
            gx, sx = 0.5 * (h_up - h_dn), h_up - 2.0 * h + h_dn
            h_up = j_up(h, hgt[jn, kt], 1) * mj_up
            h_dn = j_dn(h, hgt[jp, kt], 1) * mj_dn
            gy, sy = 0.5 * (h_up - h_dn), h_up - 2.0 * h + h_dn
            gx2, gy2 = gx * gx, gy * gy
            root = lax.rsqrt(1.0 + gx2 + gy2)
            bend = (sx * (1.0 + gy2) + sy * (1.0 + gx2)) * coef[12, jt, kt] * (root * root * root)
            right = src[jq, kt] - SIGMA * bend * adv[jq, kt]
            m = mob[jq, kt]
            mk_dn = jnp.where(k16 < 1, coef[4, jt, kt], 1.0)
            mk_up = jnp.where(k16 >= 15, coef[5, jt, kt], 1.0)
            across = (
                rs(m, 1), rs(m, -1),
                j_dn(m, mob[jp, kt], 1), j_up(m, mob[jn, kt], 1),
                k_dn(m, mob[jq, kp], 1, 1.0), k_up(m, mob[jq, kn], 1, 1.0),
            )
            masks = (mi_dn, mi_up, mj_dn, mj_up, mk_dn, mk_up)
            edges = (i_bot1, i_top1, at_dn, at_up, k16 < 1, k16 >= 15)
            diag = jnp.zeros_like(m)
            parts = []
            for f in range(6):
                w = (m + masks[f] * across[f]) * jnp.where(edges[f], coef[6 + f, jt, kt], 1.0)
                diag = diag + w
                parts.append(w * masks[f])
            inv = 1.0 / diag
            for f in range(6):
                wts[f, jq, kt] = parts[f] * inv
            rhs[jq, kt] = right * coef[13, jt, kt] * inv
        return carry

    lax.fori_loop(0, 6, weigh, 0)

    for sweep in range(SWEEPS):
        old, new = (p0, p1) if sweep % 2 == 0 else (p1, p0)
        last = sweep == SWEEPS - 1

        def relax(jq, carry, old=old, new=new, last=last):
            jn, jp = lax.rem(jq + 1, 6), lax.rem(jq + 5, 6)
            for kt in range(2 if last else 3):
                kn, kp = (kt + 1) % 3, (kt + 2) % 3
                p = old[jq, kt]
                total = wts[0, jq, kt] * rs(p, 1) + wts[1, jq, kt] * rs(p, -1)
                total = total + wts[2, jq, kt] * j_dn(p, old[jp, kt], 1)
                total = total + wts[3, jq, kt] * j_up(p, old[jn, kt], 1)
                total = total + wts[4, jq, kt] * k_dn(p, old[jq, kp], 1, 1.0)
                total = total + wts[5, jq, kt] * k_up(p, old[jq, kn], 1, 1.0)
                new[jq, kt] = total - rhs[jq, kt]
            return carry

        lax.fori_loop(0, 4 if last else 6, relax, 0)
    final = p0 if SWEEPS % 2 == 0 else p1

    start = bounds[d]
    count = bounds[d + 1] - start
    off = 8 * d - start
    vof[...] = jnp.zeros_like(vof)
    pres[...] = jnp.zeros_like(pres)
    even = d % 2 == 0

    def tile_half(ref, t, h):
        row0 = pl.multiple_of(16 * ((t & 1) ^ tree), 16)
        return ref[2 * ((t >> 1) & 1) + h, (t >> 2) & 1, pl.ds(row0, 16), :]

    for t in range(8):
        slot = t + off

        @pl.when((slot >= 0) & (slot < count))
        def _(t=t, slot=slot):
            for h in range(2):
                vof[slot, :, halves(h)] = tile_half(adv, t, h)
                pres[slot, :, halves(h)] = tile_half(final, t, h)

    for h in range(2):
        for n, ref in enumerate((adv, final)):
            low, high = tile_half(ref, 0, h), tile_half(ref, 7, h)
            send_a[n, :, halves(h)] = jnp.where(even, high, low)
            send_b[n, :, halves(h)] = jnp.where(even, low, high)


VM = pl.BlockSpec(memory_space=pltpu.VMEM)
SM = pl.BlockSpec(memory_space=pltpu.SMEM)


def blocks(n):
    return jax.ShapeDtypeStruct((n, 8, 128), F32)


def call(kernel, specs, outs, args, scratch=(), cost=1):
    return pl.pallas_call(
        kernel,
        out_shape=outs,
        in_specs=specs,
        out_specs=jax.tree.map(lambda _: VM, outs),
        scratch_shapes=list(scratch),
        compiler_params=pltpu.CompilerParams(vmem_limit_bytes=48 * 1024 * 1024),
        cost_estimate=pl.CostEstimate(
            flops=cost * 1000000, bytes_accessed=cost * 1000000, transcendentals=0
        ),
    )(*args)


def local(volume, velocity, source, pressure_prev, neighbours, levels, refine, bounds_old, bounds_new):
    d = lax.axis_index("row") * 16 + lax.axis_index("col")
    old = (volume, velocity, source, pressure_prev)
    one = blocks(1)
    ra, rb, peak = call(
        first_kernel, [VM] * 4 + [SM] * 2, (blocks(57), blocks(24), one), (*old, levels, bounds_old)
    )
    x8, x9 = send(peak, flip_pairs(8)), send(peak, flip_pairs(9))
    rb, ra = send(rb, ODD_PAIRS), send(ra, EVEN_PAIRS)
    coef = call(
        coefficient_kernel,
        [SM] * 3,
        jax.ShapeDtypeStruct((14, 4, 3, 40, 128), F32),
        (neighbours.reshape(-1), levels, refine),
        [pltpu.SMEM((14 * 64,), F32), pltpu.SMEM((7,), F32)],
        5,
    )
    ib, peak = call(
        second_kernel,
        [VM] * 4 + [SM] + [VM] * 5,
        (blocks(32), one),
        (*old, bounds_old, peak, ra, rb, x8, x9),
    )
    xs = [send(peak, flip_pairs(b)) for b in (16, 64, 80)]
    ib = send(ib, axis_pairs(0, 1))
    ext, ia = call(
        gather_kernel,
        [VM] * 4 + [SM] + [VM] * 2,
        (jax.ShapeDtypeStruct((6, 4, 2, 32, 128), F32), blocks(32)),
        (*old, bounds_old, ra, rb),
    )
    ja, jb, peak = call(
        third_kernel,
        [VM] * 7,
        (blocks(43), blocks(42), one),
        (ext, ia, ib, peak, *xs),
    )
    xs = [send(peak, flip_pairs(b)) for b in (32, 34)]
    ja, jb = send(ja, axis_pairs(1, 0)), send(jb, axis_pairs(1, 1))
    ka, kb = call(
        fourth_kernel,
        [VM] * 8,
        (blocks(64), blocks(63)),
        (ext, ia, ib, ja, jb, peak, *xs),
    )
    peak = ka
    ka, kb = send(ka, axis_pairs(2, 0)), send(kb, axis_pairs(2, 1))
    grid = (6, 3, 40, 128)
    tall = (6, 3, 48, 128)
    vof, pres, sa, sb = call(
        main_kernel,
        [VM] * 9 + [SM],
        (
            jax.ShapeDtypeStruct((10, 16, 256), F32),
            jax.ShapeDtypeStruct((10, 16, 256), F32),
            jax.ShapeDtypeStruct((2, 16, 256), F32),
            jax.ShapeDtypeStruct((2, 16, 256), F32),
        ),
        (ext, ia, ib, ja, jb, ka, kb, peak, coef, bounds_new),
        [pltpu.VMEM(tall, F32)] * 2 + [pltpu.VMEM(grid, F32)] * 10 + [pltpu.VMEM((6, *grid), F32)],
        20,
    )
    sb, sa = send(sb, ODD_PAIRS), send(sa, EVEN_PAIRS)
    even = d % 2 == 0
    low, high = jnp.where(even, sb, sa), jnp.where(even, sa, sb)
    start, stop = bounds_new[d], bounds_new[d + 1]
    slots = jnp.arange(10, dtype=jnp.int32)
    at_low = ((slots == 0) & (start == 8 * d - 1))[:, None, None]
    at_high = ((slots == 8 * d + 8 - start) & (stop == 8 * d + 9))[:, None, None]
    outs = [
        jnp.where(at_low, low[n][None], jnp.where(at_high, high[n][None], x))
        for n, x in enumerate((vof, pres))
    ]
    return tuple(outs)


def solution(mesh):
    in_specs = (
        P(AXES, None, None),
        P(None, AXES, None, None),
        P(AXES, None, None),
        P(AXES, None, None),
        P(),
        P(),
        P(),
        P(),
        P(),
    )
    out_specs = (P(AXES, None, None), P(AXES, None, None))
    return jax.shard_map(local, mesh=mesh, in_specs=in_specs, out_specs=out_specs, check_vma=False)
```

```python
import jax
import jax.numpy as jnp
from jax import lax
from jax.experimental import pallas as pl
from jax.experimental.pallas import tpu as pltpu
from jax.sharding import PartitionSpec as P

SWEEPS = 4
CFL = 0.4
SIGMA = 0.05
RHO_GAS = 0.05
RHO_LIQ = 1.0
AXES = ("row", "col")
DEVS = 128
F32 = jnp.float32


def block_coords(d):
    tree, low = d >> 6, d & 63
    i = (low & 1) | (((low >> 3) & 1) << 1)
    j = ((low >> 1) & 1) | (((low >> 4) & 1) << 1)
    k = ((low >> 2) & 1) | (((low >> 5) & 1) << 1)
    return (7 - i if tree else i), j, k


PLACE = {block_coords(d): d for d in range(DEVS)}


def axis_pairs(axis, odd):
    count = (8, 4, 4)[axis]
    pairs = []
    for d in range(DEVS):
        c = list(block_coords(d))
        step = 1 if (c[axis] % 2 == 0) != bool(odd) else -1
        c[axis] = (c[axis] + step) % count
        pairs.append((d, PLACE[tuple(c)]))
    return pairs


def flip_pairs(bits):
    return [(d, d ^ bits) for d in range(DEVS)]


EVEN_PAIRS = flip_pairs(1)
ODD_PAIRS = [(d, d + 1 if d % 2 else d - 1) for d in range(1, DEVS - 1)]
FAR_PAIRS = [(d, dict(axis_pairs(0, 1))[e]) for d, e in ODD_PAIRS]


def send(x, pairs):
    return lax.ppermute(x, AXES, pairs)


def where_is(d):
    tree = d >> 6
    i = (d & 1) | (((d >> 3) & 1) << 1)
    gi = jnp.where(tree == 1, 7 - i, i)
    gj = ((d >> 1) & 1) | (((d >> 4) & 1) << 1)
    gk = ((d >> 2) & 1) | (((d >> 5) & 1) << 1)
    return tree, gi, gj, gk


def where_am_i():
    d = lax.axis_index("row") * 16 + lax.axis_index("col")
    return d, *where_is(d)


def iotas():
    sub = lax.broadcasted_iota(jnp.int32, (8, 128), 0)
    lane = lax.broadcasted_iota(jnp.int32, (8, 128), 1)
    return sub, lane


def rl(x, shift):
    return pltpu.roll(x, shift % 128, 1)


def rs(x, shift):
    n = x.shape[0]
    return pltpu.roll(x, shift % n, 0)


def halves(h):
    return pl.ds(128 * h, 128)


def old_slice(old, f, slot, start, h):
    return old[f, slot, pl.ds(pl.multiple_of(start, 8), 8), halves(h)]


def slab_groups(get, high, sub):
    nat = (sub >= 4) == high
    return (
        get(0),
        get(1),
        jnp.where(nat, get(2), rs(get(3), 4)),
        jnp.where(nat, get(5), rs(get(4), 4)),
    )


def first_kernel(
    vol, vel, src, prev, levels_in, bounds_in, ra, rb, ib, ic, peak, old, levels, bounds, sems
):
    copies = [
        pltpu.make_async_copy(bounds_in, bounds, sems.at[0]),
        pltpu.make_async_copy(levels_in, levels, sems.at[1]),
        pltpu.make_async_copy(vol, old.at[0], sems.at[2]),
        pltpu.make_async_copy(vel, old.at[pl.ds(1, 3)], sems.at[3]),
        pltpu.make_async_copy(src, old.at[4], sems.at[4]),
        pltpu.make_async_copy(prev, old.at[5], sems.at[5]),
    ]
    for copy in copies:
        copy.start()
    d, tree, gi, gj, gk = where_am_i()
    sub, lane = iotas()
    for copy in copies:
        copy.wait()
    start = bounds[d]
    count = bounds[d + 1] - start
    off = 8 * d - start
    even = d % 2 == 0
    slot_a = jnp.where(even, 8 + off, 0)
    slot_b = jnp.where(even, 0, 8 + off)
    for f in range(6):
        for r in range(2):
            for h in range(2):
                ra[f * 4 + r * 2 + h] = old_slice(old, f, slot_a, 8 * r, h)
                rb[f * 4 + r * 2 + h] = old_slice(old, f, slot_b, 8 * r, h)
    high = gi % 2 == 0
    bit = jnp.where(even, 1, 0)
    for q in range(4):
        for h in range(2):
            slot = jnp.clip(bit + 2 * q + off, 0, 9)
            row0 = jnp.where(high, 8, 0)
            groups = slab_groups(lambda f: old_slice(old, f, slot, row0, h), high, sub)
            for g in range(4):
                ra[24 + (g * 4 + q) * 2 + h] = groups[g]
            slot = jnp.clip(1 - bit + 2 * q + off, 0, 9)
            groups = slab_groups(
                lambda f: old_slice(old, f, slot, 8 - row0, h), jnp.logical_not(high), sub
            )
            for g in range(4):
                ib[(g * 4 + q) * 2 + h] = groups[g]
    other = jnp.where(even, d - 1, d + 1)
    gi_other = where_is(other)[1]
    high = gi_other % 2 == 1
    row0 = jnp.where(high, 8, 0)
    for h in range(2):
        groups = slab_groups(lambda f: old_slice(old, f, slot_b, row0, h), high, sub)
        for g in range(4):
            ic[g * 2 + h] = groups[g]
    top = jnp.zeros((8, 128), F32)
    for s in range(10):
        level = levels[jnp.minimum(start + s, 1023)]
        inv = jnp.where(s < count, jnp.left_shift(1, level), 0).astype(F32)
        part = jnp.zeros((8, 128), F32)
        for r in range(2):
            for h in range(2):
                u = [jnp.abs(old[1 + a, s, pl.ds(8 * r, 8), halves(h)]) for a in range(3)]
                part = jnp.maximum(part, u[0] + u[1] + u[2])
        top = jnp.maximum(top, part * inv)
    ra[56] = top
    peak[0] = top


FLAG_COUNT = 6


def own_kernel(old, bounds, ext, mine, flags):
    d, tree, gi, gj, gk = where_am_i()
    sub, lane = iotas()
    off = 8 * d - bounds[d]
    even = d % 2 == 0
    for t in range(8):
        slot = jnp.clip(t + off, 0, 9)
        bj, bk = (t >> 1) & 1, (t >> 2) & 1
        row0 = 16 * ((t & 1) ^ tree)
        for f in range(6):
            for r in range(2):
                for h in range(2):
                    rows = pl.ds(pl.multiple_of(row0 + 8 * r, 8), 8)
                    ext[f, 2 * bj + h, bk, rows, :] = old_slice(old, f, slot, 8 * r, h)
    high = gi % 2 == 1
    row0 = jnp.where(high, 8, 0)
    slot_a = jnp.where(even, 8 + off, 0)
    for h in range(2):
        groups = slab_groups(lambda f: old_slice(old, f, slot_a, row0, h), high, sub)
        for g in range(4):
            mine[g * 2 + h] = groups[g]
    near_gi = (gi + jnp.where(gi % 2 == 1, 1, 7)) % 8
    upper = near_gi >= 4
    li = jnp.where(upper, 7 - near_gi, near_gi)
    e = (d & 54) | (li & 1) | ((li >> 1) << 3) | jnp.where(upper, 64, 0)
    e_even = e % 2 == 0
    odd, e_odd = jnp.logical_not(even), jnp.logical_not(e_even)
    values = (
        bounds[d] == 8 * d + 1,
        bounds[d + 1] == 8 * d + 7,
        even & (bounds[d + 1] == 8 * d + 9),
        odd & (bounds[d] == 8 * d - 1),
        e_even & (bounds[e] == 8 * e + 1),
        e_odd & (bounds[e + 1] == 8 * e + 7),
    )
    for n, value in enumerate(values):
        flags[n] = jnp.full((8, 128), jnp.where(value, 1.0, 0.0), F32)


def block_kernel(
    own, mine, flags, ra, rb, ib_in, ic, peak, x64, coef, ext, ia, ib, ja, jb, peak_out
):
    d, tree, gi, gj, gk = where_am_i()
    sub, lane = iotas()
    even = d % 2 == 0
    flag = [flags[n] > 0.5 for n in range(FLAG_COUNT)]
    ext[...] = own[...]
    for t, missing in ((0, flag[0]), (7, flag[1])):
        bj, bk = (t >> 1) & 1, (t >> 2) & 1
        row0 = 16 * ((t & 1) ^ tree)
        use_b = even if t == 0 else jnp.logical_not(even)
        for f in range(6):
            for r in range(2):
                for h in range(2):
                    n = f * 4 + r * 2 + h
                    rows = pl.ds(pl.multiple_of(row0 + 8 * r, 8), 8)
                    came = jnp.where(use_b, rb[n], ra[n])
                    ext[f, 2 * bj + h, bk, rows, :] = jnp.where(
                        missing, came, own[f, 2 * bj + h, bk, rows, :]
                    )
    for q in range(4):
        for h in range(2):
            for g in range(4):
                n = (g * 4 + q) * 2 + h
                x, y = ra[24 + n], ib_in[n]
                if q == 0:
                    x = jnp.where(flag[2], mine[g * 2 + h], x)
                    y = jnp.where(flag[4], ic[g * 2 + h], y)
                if q == 3:
                    x = jnp.where(flag[3], mine[g * 2 + h], x)
                    y = jnp.where(flag[5], ic[g * 2 + h], y)
                ia[n] = x
                ib[n] = y
    top = jnp.maximum(peak[0], x64[0])
    pack_j(ext, ia, ib, ja, jb, gi, gj, sub, lane)
    ja[42] = top
    jb[42] = top
    peak_out[0] = top


def make_block(ext, ia, ib, gi, sub):
    first_high = gi % 2 == 0

    def pair(g, jq, kt):
        n = (g * 4 + jq // 2 + 2 * kt) * 2 + jq % 2
        a, b = ia[n], ib[n]
        return jnp.where(first_high, a, b), jnp.where(first_high, b, a)

    def rows(f, jq, kt, b):
        if b < 4:
            return ext[f, jq, kt, pl.ds(8 * b, 8), :]
        if f == 0:
            return pair(0, jq, kt)[b - 4]
        hi, lo = pair((1, 1, 2, 2, 3, 3)[f], jq, kt)
        if f in (3, 4):
            return rs(jnp.where(sub < 4, lo, hi), 4)
        return jnp.where(sub < 4, hi, lo)

    return rows, pair


def pack_j(ext, ia, ib, ja, jb, gi, gj, sub, lane):
    rows, _ = make_block(ext, ia, ib, gi, sub)
    even = gj % 2 == 0

    def pack(jq, kt, g, b):
        if g == 0:
            return rows(0, jq, kt, b)
        if g == 1:
            return rows(2, jq, kt, b)
        fa, fb = ((1, 3), (5, 4))[g - 2]
        nat = lane < 64 if jq == 0 else lane >= 64
        return jnp.where(nat, rows(fa, jq, kt, b), rl(rows(fb, jq, kt, b), 64))

    for g in range(4):
        for kt in range(2):
            for b in range(6 if g == 0 else 5):
                n = kt * 6 + b if g == 0 else 12 + ((g - 1) * 2 + kt) * 5 + b
                lo, hi = pack(0, kt, g, b), pack(3, kt, g, b)
                ja[n] = jnp.where(even, hi, lo)
                jb[n] = jnp.where(even, lo, hi)


def make_wide(rows, ja, jb, gj):
    first_high = gj % 2 == 0

    def wide(f, jq, kt, b):
        if jq < 4:
            return rows(f, jq, kt, b)
        if f == 0:
            n = kt * 6 + b
        else:
            n = 12 + ((1, 1, 0, 1, 2, 2)[f] * 2 + kt) * 5 + b
        if jq == 4:
            x = jnp.where(first_high, ja[n], jb[n])
        else:
            x = jnp.where(first_high, jb[n], ja[n])
        return rl(x, 64) if f in (3, 4) else x

    return wide


def k_place(g, jt, b):
    return jt * 6 + b if g == 0 else 18 + ((g - 1) * 3 + jt) * 5 + b


def pack_k(wide, jt, ka, kb, gk, lane):
    even = gk % 2 == 0
    near = lane % 16 < 8
    small = lane % 8 < 4

    def squeeze(f, kt, b):
        first, last = wide(f, 2 * jt, kt, b), wide(f, 2 * jt + 1, kt, b)
        if kt == 0:
            return jnp.where(near, first, rl(last, 8))
        return jnp.where(near, rl(first, -8), last)

    def pack(kt, g, b):
        if g == 0:
            return squeeze(0, kt, b)
        if g == 1:
            return squeeze(3, kt, b)
        fa, fb = ((1, 2), (5, 4))[g - 2]
        one, two = squeeze(fa, kt, b), squeeze(fb, kt, b)
        if kt == 0:
            return jnp.where(small, one, rl(two, 4))
        return jnp.where(small, rl(two, -4), one)

    for g in range(4):
        for b in range(6 if g == 0 else 5):
            n = k_place(g, jt, b)
            lo, hi = pack(0, g, b), pack(1, g, b)
            ka[n] = jnp.where(even, hi, lo)
            kb[n] = jnp.where(even, lo, hi)


def early_k_kernel(ext, ia, ib, ka, kb):
    d, tree, gi, gj, gk = where_am_i()
    sub, lane = iotas()
    rows, _ = make_block(ext, ia, ib, gi, sub)
    for jt in range(2):
        pack_k(rows, jt, ka, kb, gk, lane)


def late_k_kernel(ka_in, kb_in, ja, jb, peak, x16, ka, kb, peak_out):
    d, tree, gi, gj, gk = where_am_i()
    sub, lane = iotas()
    wide = make_wide(None, ja, jb, gj)
    for jt in range(2):
        for g in range(4):
            for b in range(6 if g == 0 else 5):
                n = k_place(g, jt, b)
                ka[n] = ka_in[n]
                kb[n] = kb_in[n]
    pack_k(wide, 2, ka, kb, gk, lane)
    top = jnp.maximum(jnp.maximum(peak[0], x16[0]), jnp.maximum(ja[42], jb[42]))
    ka[63] = top
    kb[63] = top
    peak_out[0] = top


def coefficient_kernel(neighbours, levels, refine, out, table, ratio):
    d, tree, gi, gj, gk = where_am_i()
    sub, lane = iotas()
    for n in range(7):
        ratio[n] = 2.0 / (1.0 + 2.0 ** (n - 3))

    def one(pos, carry):
        ip, jp, kp = pos >> 4, (pos >> 2) & 3, pos & 3
        x = 2 * gi + jnp.where(ip == 3, -1, ip)
        y = 2 * gj + jnp.where(jp == 3, -1, jp)
        z = 2 * gk + jnp.where(kp == 3, -1, kp)
        inside = (x >= 0) & (x < 16) & (y >= 0) & (y < 8) & (z >= 0) & (z < 8)
        upper = x >= 8
        lx = jnp.where(upper, 15 - x, x)
        code = jnp.where(upper, 512, 0)
        for bit in range(3):
            for axis, v in enumerate((lx, y, z)):
                code = code | (((v >> bit) & 1) << (3 * bit + axis))
        code = jnp.where(inside, code, 0)
        level = levels[code]
        depth = level + refine[code]
        for f in range(6):
            p = neighbours[code * 6 + f]
            opened = inside & (p >= 0)
            safe = jnp.maximum(p, 0)
            other = levels[safe] + refine[safe]
            table[f * 64 + pos] = jnp.where(opened, 1.0, 0.0)
            table[(6 + f) * 64 + pos] = jnp.where(opened, ratio[depth - other + 3], 1.0)
        table[12 * 64 + pos] = jnp.left_shift(1, level).astype(F32)
        table[13 * 64 + pos] = jnp.left_shift(1, 6 - 2 * depth).astype(F32) * (2.0 / 64.0)
        return carry

    lax.fori_loop(0, 64, one, 0)

    def expand(step, carry):
        item, jp = step >> 2, step & 3
        base = item * 64 + jp * 4
        vals = {}
        for ip in range(4):
            v = [jnp.full((8, 128), table[base + ip * 16 + kp], F32) for kp in range(4)]
            vals[ip] = (v[0], v[1], jnp.where(lane % 16 < 8, v[2], v[3]))
        for kt in range(3):
            mixed = jnp.where(sub < 4, vals[2][kt], vals[3][kt])
            for b, v in enumerate((vals[0][kt], vals[0][kt], vals[1][kt], vals[1][kt], mixed)):
                out[item, jp, kt, pl.ds(8 * b, 8), :] = v
        return carry

    lax.fori_loop(0, 56, expand, 0)


def minmod(a, b):
    return jnp.maximum(jnp.minimum(a, b), 0.0) + jnp.minimum(jnp.maximum(a, b), 0.0)


def face_change(c, up1, up2, dn1, dn2, u, u_up, u_dn):
    upper, lower = up1 - c, c - dn1
    half = 0.5 * minmod(upper, lower)
    half_up = 0.5 * minmod(up2 - up1, upper)
    half_dn = 0.5 * minmod(lower, dn1 - dn2)
    w_up, w_dn = 0.5 * (u + u_up), 0.5 * (u_dn + u)
    flux_up = jnp.maximum(w_up, 0.0) * (c + half) + jnp.minimum(w_up, 0.0) * (up1 - half_up)
    flux_dn = jnp.maximum(w_dn, 0.0) * (dn1 + half_dn) + jnp.minimum(w_dn, 0.0) * (c - half)
    return flux_up - flux_dn


def wrap48(x, sub):
    return jnp.concatenate([x[:32], jnp.where(sub < 4, x[32:40], x[40:48])], axis=0)


class Shifts:
    def __init__(self):
        self.sub, self.lane = iotas()
        self.row = lax.broadcasted_iota(jnp.int32, (40, 128), 0)
        self.lane5 = lax.broadcasted_iota(jnp.int32, (40, 128), 1)
        self.k16 = self.lane5 % 16
        row = self.row
        self.i_top1 = (row == 15) | (row == 31) | (row == 39)
        self.i_top2 = self.i_top1 | (row == 14) | (row == 30) | (row == 38)
        self.i_bot1 = (row == 0) | (row == 16) | (row == 32)
        self.i_bot2 = self.i_bot1 | (row == 1) | (row == 17) | (row == 33)

    def wrap(self, x):
        return wrap48(x, self.sub)

    def k_up(self, x, nxt, n, m=None):
        nxt = rl(nxt, 16 - n)
        return jnp.where(self.k16 < 16 - n, rl(x, -n), nxt if m is None else m * nxt)

    def k_dn(self, x, prv, n, m=None):
        prv = rl(prv, n - 16)
        return jnp.where(self.k16 >= n, rl(x, n), prv if m is None else m * prv)

    def j_up(self, x, nxt, n):
        return rl(jnp.where(self.lane5 < 16 * n, nxt, x), -16 * n)

    def j_dn(self, x, prv, n):
        return rl(jnp.where(self.lane5 >= 128 - 16 * n, prv, x), 16 * n)

    def change_ij(self, jq, kt, coef, c40, u1, c48, v48):
        jt = tile_j(jq)
        jn, jp = lax.rem(jq + 1, 6), lax.rem(jq + 5, 6)
        odd = jq % 2 == 1
        lane5 = self.lane5
        c = c40(jq)
        m_dn = jnp.where(odd, 1.0, coef[2, jt, kt])
        m_up = jnp.where(odd, coef[3, jt, kt], 1.0)
        up_m1 = jnp.where(lane5 >= 112, m_up, 1.0)
        up_m2 = jnp.where(lane5 >= 96, m_up, 1.0)
        dn_m1 = jnp.where(lane5 < 16, m_dn, 1.0)
        dn_m2 = jnp.where(lane5 < 32, m_dn, 1.0)
        cn, cp = c40(jn), c40(jp)
        u = u1(jq)
        change = face_change(
            c, self.j_up(c, cn, 1) * up_m1, self.j_up(c, cn, 2) * up_m2,
            self.j_dn(c, cp, 1) * dn_m1, self.j_dn(c, cp, 2) * dn_m2,
            u, self.j_up(u, u1(jn), 1) * up_m1, self.j_dn(u, u1(jp), 1) * dn_m1,
        )
        m_dn, m_up = coef[0, jt, kt], coef[1, jt, kt]
        up_m1, up_m2 = jnp.where(self.i_top1, m_up, 1.0), jnp.where(self.i_top2, m_up, 1.0)
        dn_m1, dn_m2 = jnp.where(self.i_bot1, m_dn, 1.0), jnp.where(self.i_bot2, m_dn, 1.0)
        wrap = self.wrap
        return change + face_change(
            c, wrap(rs(c48, -1)) * up_m1, wrap(rs(c48, -2)) * up_m2,
            wrap(rs(c48, 1)) * dn_m1, wrap(rs(c48, 2)) * dn_m2,
            wrap(v48), wrap(rs(v48, -1)) * up_m1, wrap(rs(v48, 1)) * dn_m1,
        )


def tile_j(jq):
    return jnp.where(jq < 4, jq >> 1, jq - 2)


def early_kernel(ext, ia, ib, ja, jb, coef, c40, u2, src, prs, chg, c48, v48, u1):
    d, tree, gi, gj, gk = where_am_i()
    sh = Shifts()
    sub = sh.sub
    rows, pair = make_block(ext, ia, ib, gi, sub)
    wide = make_wide(rows, ja, jb, gj)
    dest = (c48, v48, u1, u2, src, prs)
    for f in range(6):
        for jq in range(6):
            for kt in range(2):
                for b in range(6 if f == 0 else 5):
                    x = wide(f, jq, kt, b)
                    if f == 1 and b == 4:
                        hi, lo = pair(1, jq, kt) if jq < 4 else (x, x)
                        v48[jq, kt, pl.ds(32, 8), :] = hi
                        v48[jq, kt, pl.ds(40, 8), :] = lo
                    else:
                        dest[f][jq, kt, pl.ds(8 * b, 8), :] = x
                    if f == 0 and b < 4:
                        c40[jq, kt, pl.ds(8 * b, 8), :] = x
                if f == 0:
                    c40[jq, kt, pl.ds(32, 8), :] = jnp.where(
                        sub < 4, c48[jq, kt, pl.ds(32, 8), :], c48[jq, kt, pl.ds(40, 8), :]
                    )

    def step(jq, carry):
        for kt in range(2):
            chg[jq, kt] = sh.change_ij(
                jq, kt, coef, lambda n: c40[n, kt], lambda n: u1[n, kt], c48[jq, kt], v48[jq, kt]
            )
        return carry

    lax.fori_loop(0, 6, step, 0)


def main_kernel(
    c_in, u_in, s_in, p_in, chg, ka, kb, peak, x32, coef,
    out_adv, out_p, send_a, send_b,
    c48, v48, c_k, u1, u2, src, p_k, p0, p1, adv, mob, hgt, rhs, wts,
):
    d, tree, gi, gj, gk = where_am_i()
    sh = Shifts()
    sub, lane, lane5, k16 = sh.sub, sh.lane, sh.lane5, sh.k16
    near = lane % 16 < 8
    k_even = gk % 2 == 0
    dest = (c48, v48, u1, u2, src, p_k)
    for f in range(6):
        for b in range(6 if f == 0 else 5):
            for jt in range(3):
                n = k_place((0, 2, 2, 1, 3, 3)[f], jt, b)
                a, e = ka[n], kb[n]
                low_pack = jnp.where(k_even, a, e)
                high_pack = jnp.where(k_even, e, a)
                if f in (2, 4):
                    low_pack, high_pack = rl(low_pack, -4), rl(high_pack, 4)
                first = jnp.where(near, low_pack, rl(high_pack, 8))
                last = jnp.where(near, rl(low_pack, -8), high_pack)
                for jq, x in ((2 * jt, first), (2 * jt + 1, last)):
                    dest[f][jq, pl.ds(8 * b, 8), :] = x
                    if f == 0 and b < 4:
                        c_k[jq, pl.ds(8 * b, 8), :] = x
                    if f == 1 and b == 4:
                        v48[jq, pl.ds(40, 8), :] = x
    for jq in range(6):
        c_k[jq, pl.ds(32, 8), :] = jnp.where(
            sub < 4, c48[jq, pl.ds(32, 8), :], c48[jq, pl.ds(40, 8), :]
        )

    def c40(jq, kt):
        return c_k[jq] if kt == 2 else c_in[jq, kt]

    def uk(jq, kt):
        return u2[jq] if kt == 2 else u_in[jq, kt]

    top = jnp.maximum(jnp.maximum(peak[0], x32[0]), jnp.maximum(ka[63], kb[63]))
    top = jnp.max(top, keepdims=True)
    step = jnp.broadcast_to(CFL / top, (8, 128))
    step = jnp.concatenate([step] * 5, axis=0)

    def advance(jq, carry):
        jt = tile_j(jq)
        for kt in range(3):
            kn, kp = (kt + 1) % 3, (kt + 2) % 3
            if kt == 2:
                change = sh.change_ij(
                    jq, 2, coef, lambda n: c_k[n], lambda n: u1[n], c48[jq], v48[jq]
                )
            else:
                change = chg[jq, kt]
            c = c40(jq, kt)
            m_dn, m_up = coef[4, jt, kt], coef[5, jt, kt]
            cn, cp = c40(jq, kn), c40(jq, kp)
            up1, up2 = sh.k_up(c, cn, 1, m_up), sh.k_up(c, cn, 2, m_up)
            dn1, dn2 = sh.k_dn(c, cp, 1, m_dn), sh.k_dn(c, cp, 2, m_dn)
            hgt[jq, kt] = dn2 + dn1 + c + up1 + up2
            u = uk(jq, kt)
            u_up, u_dn = sh.k_up(u, uk(jq, kn), 1, m_up), sh.k_dn(u, uk(jq, kp), 1, m_dn)
            change = change + face_change(c, up1, up2, dn1, dn2, u, u_up, u_dn)
            a = jnp.clip(c - step * coef[12, jt, kt] * change, 0.0, 1.0)
            adv[jq, kt] = a
            mob[jq, kt] = 1.0 / (RHO_GAS + (RHO_LIQ - RHO_GAS) * a)
        return carry

    lax.fori_loop(0, 6, advance, 0)

    def weigh(jq, carry):
        jt = tile_j(jq)
        jn, jp = lax.rem(jq + 1, 6), lax.rem(jq + 5, 6)
        odd = jq % 2 == 1
        for kt in range(3):
            kn, kp = (kt + 1) % 3, (kt + 2) % 3
            mi_dn = jnp.where(sh.i_bot1, coef[0, jt, kt], 1.0)
            mi_up = jnp.where(sh.i_top1, coef[1, jt, kt], 1.0)
            at_dn = (lane5 < 16) & jnp.logical_not(odd)
            at_up = (lane5 >= 112) & odd
            mj_dn = jnp.where(at_dn, coef[2, jt, kt], 1.0)
            mj_up = jnp.where(at_up, coef[3, jt, kt], 1.0)
            h = hgt[jq, kt]
            h_up, h_dn = rs(h, -1) * mi_up, rs(h, 1) * mi_dn
            gx, sx = 0.5 * (h_up - h_dn), h_up - 2.0 * h + h_dn
            h_up = sh.j_up(h, hgt[jn, kt], 1) * mj_up
            h_dn = sh.j_dn(h, hgt[jp, kt], 1) * mj_dn
            gy, sy = 0.5 * (h_up - h_dn), h_up - 2.0 * h + h_dn
            gx2, gy2 = gx * gx, gy * gy
            root = lax.rsqrt(1.0 + gx2 + gy2)
            bend = (sx * (1.0 + gy2) + sy * (1.0 + gx2)) * coef[12, jt, kt] * (root * root * root)
            right = (src[jq] if kt == 2 else s_in[jq, kt]) - SIGMA * bend * adv[jq, kt]
            m = mob[jq, kt]
            mk_dn = jnp.where(k16 < 1, coef[4, jt, kt], 1.0)
            mk_up = jnp.where(k16 >= 15, coef[5, jt, kt], 1.0)
            across = (
                rs(m, 1), rs(m, -1),
                sh.j_dn(m, mob[jp, kt], 1), sh.j_up(m, mob[jn, kt], 1),
                sh.k_dn(m, mob[jq, kp], 1), sh.k_up(m, mob[jq, kn], 1),
            )
            masks = (mi_dn, mi_up, mj_dn, mj_up, mk_dn, mk_up)
            edges = (sh.i_bot1, sh.i_top1, at_dn, at_up, k16 < 1, k16 >= 15)
            diag = jnp.zeros_like(m)
            parts = []
            for f in range(6):
                w = (m + masks[f] * across[f]) * jnp.where(edges[f], coef[6 + f, jt, kt], 1.0)
                diag = diag + w
                parts.append(w * masks[f])
            inv = 1.0 / diag
            for f in range(6):
                wts[f, jq, kt] = parts[f] * inv
            rhs[jq, kt] = right * coef[13, jt, kt] * inv
        return carry

    lax.fori_loop(0, 6, weigh, 0)

    for sweep in range(SWEEPS):
        new = p0 if sweep % 2 == 0 else p1
        older = p1 if sweep % 2 == 0 else p0
        last = sweep == SWEEPS - 1

        def old(jq, kt, sweep=sweep, older=older):
            if sweep:
                return older[jq, kt]
            return p_k[jq] if kt == 2 else p_in[jq, kt]

        def relax(jq, carry, old=old, new=new, last=last):
            jn, jp = lax.rem(jq + 1, 6), lax.rem(jq + 5, 6)
            for kt in range(2 if last else 3):
                kn, kp = (kt + 1) % 3, (kt + 2) % 3
                p = old(jq, kt)
                total = wts[0, jq, kt] * rs(p, 1) + wts[1, jq, kt] * rs(p, -1)
                total = total + wts[2, jq, kt] * sh.j_dn(p, old(jp, kt), 1)
                total = total + wts[3, jq, kt] * sh.j_up(p, old(jn, kt), 1)
                total = total + wts[4, jq, kt] * sh.k_dn(p, old(jq, kp), 1)
                total = total + wts[5, jq, kt] * sh.k_up(p, old(jq, kn), 1)
                total = total - rhs[jq, kt]
                if last:
                    out_p[jq, kt] = total[:32]
                    out_adv[jq, kt] = adv[jq, kt][:32]
                else:
                    new[jq, kt] = total
            return carry

        lax.fori_loop(0, 4 if last else 6, relax, 0)

    even = d % 2 == 0
    for h in range(2):
        for n, ref in enumerate((out_adv, out_p)):
            low, high = tile_half(ref, 0, h, tree), tile_half(ref, 7, h, tree)
            send_a[n, :, halves(h)] = jnp.where(even, high, low)
            send_b[n, :, halves(h)] = jnp.where(even, low, high)


def tile_half(ref, t, h, tree):
    row0 = pl.multiple_of(16 * ((t & 1) ^ tree), 16)
    return ref[2 * ((t >> 1) & 1) + h, (t >> 2) & 1, pl.ds(row0, 16), :]


def slots_kernel(adv, prs, bounds, vof, pres):
    d, tree, gi, gj, gk = where_am_i()
    start = bounds[d]
    count = bounds[d + 1] - start
    off = 8 * d - start
    vof[...] = jnp.zeros_like(vof)
    pres[...] = jnp.zeros_like(pres)
    for t in range(8):
        slot = t + off

        @pl.when((slot >= 0) & (slot < count))
        def _(t=t, slot=slot):
            for h in range(2):
                vof[slot, :, halves(h)] = tile_half(adv, t, h, tree)
                pres[slot, :, halves(h)] = tile_half(prs, t, h, tree)


VM = pl.BlockSpec(memory_space=pltpu.VMEM)
SM = pl.BlockSpec(memory_space=pltpu.SMEM)
HB = pl.BlockSpec(memory_space=pltpu.HBM)


def shape(*dims):
    return jax.ShapeDtypeStruct(dims, F32)


def blocks(n):
    return shape(n, 8, 128)


def call(kernel, specs, outs, args, scratch=(), micros=1):
    return pl.pallas_call(
        kernel,
        out_shape=outs,
        in_specs=specs,
        out_specs=jax.tree.map(lambda _: VM, outs),
        scratch_shapes=list(scratch),
        compiler_params=pltpu.CompilerParams(vmem_limit_bytes=40 * 1024 * 1024),
        cost_estimate=pl.CostEstimate(
            flops=micros * 1000000, bytes_accessed=micros * 3000000, transcendentals=0
        ),
    )(*args)


def local(volume, velocity, source, pressure_prev, neighbours, levels, refine, bounds_old, bounds_new):
    d = lax.axis_index("row") * 16 + lax.axis_index("col")
    one = blocks(1)
    ra, rb, ib, ic, peak, old = call(
        first_kernel,
        [HB] * 6,
        (blocks(57), blocks(24), blocks(32), blocks(8), one, shape(6, 10, 16, 256)),
        (volume, velocity, source, pressure_prev, levels, bounds_old),
        [
            pltpu.SMEM((1024,), jnp.int32),
            pltpu.SMEM((129,), jnp.int32),
            pltpu.SemaphoreType.DMA((6,)),
        ],
    )
    x8, x9 = send(peak, flip_pairs(8)), send(peak, flip_pairs(9))
    rb, ic = send(rb, ODD_PAIRS), send(ic, FAR_PAIRS)
    ib, ra = send(ib, axis_pairs(0, 1)), send(ra, EVEN_PAIRS)
    peak = jnp.maximum(jnp.maximum(peak, ra[56:57]), jnp.maximum(x8, x9))
    x64 = send(peak, flip_pairs(64))
    coef = call(
        coefficient_kernel,
        [SM] * 3,
        shape(14, 4, 3, 40, 128),
        (neighbours.reshape(-1), levels, refine),
        [pltpu.SMEM((14 * 64,), F32), pltpu.SMEM((7,), F32)],
        5,
    )
    own, mine, flags = call(
        own_kernel, [VM, SM], (shape(6, 4, 2, 32, 128), blocks(8), blocks(FLAG_COUNT)), (old, bounds_old)
    )
    ext, ia, ib, ja, jb, peak = call(
        block_kernel,
        [VM] * 9 + [HB],
        (shape(6, 4, 2, 32, 128), blocks(32), blocks(32), blocks(43), blocks(43), one),
        (own, mine, flags, ra, rb, ib, ic, peak, x64, coef),
    )
    x16 = send(peak, flip_pairs(16))
    ja, jb = send(ja, axis_pairs(1, 0)), send(jb, axis_pairs(1, 1))
    ka, kb = call(early_k_kernel, [VM] * 3, (blocks(64), blocks(64)), (ext, ia, ib), (), 2)
    ka, kb, peak = call(
        late_k_kernel, [VM] * 6, (blocks(64), blocks(64), one), (ka, kb, ja, jb, peak, x16)
    )
    x32 = send(peak, flip_pairs(32))
    ka, kb = send(ka, axis_pairs(2, 0)), send(kb, axis_pairs(2, 1))
    part, part_tall = (6, 2, 40, 128), (6, 2, 48, 128)
    early = call(
        early_kernel,
        [VM] * 6,
        (shape(*part),) * 5,
        (ext, ia, ib, ja, jb, coef),
        [pltpu.VMEM(part_tall, F32)] * 2 + [pltpu.VMEM(part, F32)],
        4,
    )
    halo, grid = (6, 40, 128), (6, 3, 40, 128)
    adv, prs, sa, sb = call(
        main_kernel,
        [VM] * 10,
        (shape(4, 2, 32, 128),) * 2 + (shape(2, 16, 256),) * 2,
        (*early, ka, kb, peak, x32, coef),
        [pltpu.VMEM((6, 48, 128), F32)] * 2
        + [pltpu.VMEM(halo, F32)] * 5
        + [pltpu.VMEM(grid, F32)] * 6
        + [pltpu.VMEM((6, *grid), F32)],
        8,
    )
    sb, sa = send(sb, ODD_PAIRS), send(sa, EVEN_PAIRS)
    vof, pres = call(slots_kernel, [VM] * 2 + [SM], (shape(10, 16, 256),) * 2, (adv, prs, bounds_new))
    even = d % 2 == 0
    low, high = jnp.where(even, sb, sa), jnp.where(even, sa, sb)
    start, stop = bounds_new[d], bounds_new[d + 1]
    slots = jnp.arange(10, dtype=jnp.int32)
    at_low = ((slots == 0) & (start == 8 * d - 1))[:, None, None]
    at_high = ((slots == 8 * d + 8 - start) & (stop == 8 * d + 9))[:, None, None]
    outs = [
        jnp.where(at_low, low[n][None], jnp.where(at_high, high[n][None], x))
        for n, x in enumerate((vof, pres))
    ]
    return tuple(outs)


def solution(mesh):
    in_specs = (
        P(AXES, None, None),
        P(None, AXES, None, None),
        P(AXES, None, None),
        P(AXES, None, None),
        P(),
        P(),
        P(),
        P(),
        P(),
    )
    out_specs = (P(AXES, None, None), P(AXES, None, None))
    return jax.shard_map(local, mesh=mesh, in_specs=in_specs, out_specs=out_specs, check_vma=False)
```

```python
import jax
import jax.numpy as jnp
from jax import lax
from jax.experimental import pallas as pl
from jax.experimental.pallas import tpu as pltpu
from jax.sharding import PartitionSpec as P

SWEEPS = 4
CFL = 0.4
SIGMA = 0.05
RHO_GAS = 0.05
RHO_LIQ = 1.0
AXES = ("row", "col")
DEVS = 128
F32 = jnp.float32


def block_coords(d):
    tree, low = d >> 6, d & 63
    i = (low & 1) | (((low >> 3) & 1) << 1)
    j = ((low >> 1) & 1) | (((low >> 4) & 1) << 1)
    k = ((low >> 2) & 1) | (((low >> 5) & 1) << 1)
    return (7 - i if tree else i), j, k


PLACE = {block_coords(d): d for d in range(DEVS)}


def axis_pairs(axis, odd):
    count = (8, 4, 4)[axis]
    pairs = []
    for d in range(DEVS):
        c = list(block_coords(d))
        step = 1 if (c[axis] % 2 == 0) != bool(odd) else -1
        c[axis] = (c[axis] + step) % count
        pairs.append((d, PLACE[tuple(c)]))
    return pairs


def flip_pairs(bits):
    return [(d, d ^ bits) for d in range(DEVS)]


EVEN_PAIRS = flip_pairs(1)
ODD_PAIRS = [(d, d + 1 if d % 2 else d - 1) for d in range(1, DEVS - 1)]


def send(x, pairs):
    return lax.ppermute(x, AXES, pairs)


def where_is(d):
    tree = d >> 6
    i = (d & 1) | (((d >> 3) & 1) << 1)
    gi = jnp.where(tree == 1, 7 - i, i)
    gj = ((d >> 1) & 1) | (((d >> 4) & 1) << 1)
    gk = ((d >> 2) & 1) | (((d >> 5) & 1) << 1)
    return tree, gi, gj, gk


def where_am_i():
    d = lax.axis_index("row") * 16 + lax.axis_index("col")
    return d, *where_is(d)


def iotas():
    sub = lax.broadcasted_iota(jnp.int32, (8, 128), 0)
    lane = lax.broadcasted_iota(jnp.int32, (8, 128), 1)
    return sub, lane


def rl(x, shift):
    return pltpu.roll(x, shift % 128, 1)


def rs(x, shift):
    n = x.shape[0]
    return pltpu.roll(x, shift % n, 0)


def halves(h):
    return pl.ds(128 * h, 128)


def old_slice(old, f, slot, start, h):
    return old[f, slot, pl.ds(pl.multiple_of(start, 8), 8), halves(h)]


def slab_groups(get, high, sub):
    nat = (sub >= 4) == high
    return (
        get(0),
        get(1),
        jnp.where(nat, get(2), rs(get(3), 4)),
        jnp.where(nat, get(5), rs(get(4), 4)),
    )


def first_kernel(old, facts, ra, rb, peak):
    d, tree, gi, gj, gk = where_am_i()
    sub, lane = iotas()
    off, count = facts[0], facts[1]
    even = d % 2 == 0
    slot_a = jnp.where(even, 8 + off, 0)
    slot_b = jnp.where(even, 0, 8 + off)
    for f in range(6):
        for r in range(2):
            for h in range(2):
                ra[f * 4 + r * 2 + h] = old_slice(old, f, slot_a, 8 * r, h)
                rb[f * 4 + r * 2 + h] = old_slice(old, f, slot_b, 8 * r, h)
    high = gi % 2 == 0
    row0 = jnp.where(high, 8, 0)
    bit = jnp.where(even, 1, 0)
    for q in range(4):
        for h in range(2):
            slot = jnp.clip(bit + 2 * q + off, 0, 9)
            groups = slab_groups(lambda f: old_slice(old, f, slot, row0, h), high, sub)
            for g in range(4):
                ra[24 + (g * 4 + q) * 2 + h] = groups[g]
    top = jnp.zeros((8, 128), F32)
    for s in range(10):
        inv = jnp.where(s < count, jnp.left_shift(1, facts[2 + s]), 0).astype(F32)
        part = jnp.zeros((8, 128), F32)
        for r in range(2):
            for h in range(2):
                u = [jnp.abs(old[1 + a, s, pl.ds(8 * r, 8), halves(h)]) for a in range(3)]
                part = jnp.maximum(part, u[0] + u[1] + u[2])
        top = jnp.maximum(top, part * inv)
    ra[56] = top
    peak[0] = top


FLAG_COUNT = 6


def own_kernel(old, bounds, ext, mine, flags, ib):
    d, tree, gi, gj, gk = where_am_i()
    sub, lane = iotas()
    off = 8 * d - bounds[d]
    even = d % 2 == 0
    for t in range(8):
        slot = jnp.clip(t + off, 0, 9)
        bj, bk = (t >> 1) & 1, (t >> 2) & 1
        row0 = 16 * ((t & 1) ^ tree)
        for f in range(6):
            for r in range(2):
                for h in range(2):
                    rows = pl.ds(pl.multiple_of(row0 + 8 * r, 8), 8)
                    ext[f, 2 * bj + h, bk, rows, :] = old_slice(old, f, slot, 8 * r, h)
    high = gi % 2 == 1
    row0 = jnp.where(high, 8, 0)
    slot_a = jnp.where(even, 8 + off, 0)
    bit = jnp.where(even, 0, 1)
    for h in range(2):
        groups = slab_groups(lambda f: old_slice(old, f, slot_a, row0, h), high, sub)
        for g in range(4):
            mine[g * 2 + h] = groups[g]
        for q in range(4):
            slot = jnp.clip(bit + 2 * q + off, 0, 9)
            groups = slab_groups(lambda f: old_slice(old, f, slot, row0, h), high, sub)
            for g in range(4):
                ib[(g * 4 + q) * 2 + h] = groups[g]
    odd = jnp.logical_not(even)
    first, last = bounds[d] == 8 * d + 1, bounds[d + 1] == 8 * d + 7
    values = (
        first,
        last,
        even & (bounds[d + 1] == 8 * d + 9),
        odd & (bounds[d] == 8 * d - 1),
        even & first,
        odd & last,
    )
    for n, value in enumerate(values):
        flags[n] = jnp.full((8, 128), jnp.where(value, 1.0, 0.0), F32)


def second_kernel(ib_in, flags, rb, ra, peak, x8, x9, ib, peak_out):
    d, tree, gi, gj, gk = where_am_i()
    sub, lane = iotas()
    high = gi % 2 == 1
    block = jnp.where(high, 2, 0)
    for q in range(4):
        for h in range(2):
            if q in (0, 3):
                groups = slab_groups(lambda f: rb[f * 4 + block + h], high, sub)
                flag = flags[4 if q == 0 else 5] > 0.5
            for g in range(4):
                n = (g * 4 + q) * 2 + h
                ib[n] = jnp.where(flag, groups[g], ib_in[n]) if q in (0, 3) else ib_in[n]
    peak_out[0] = jnp.maximum(jnp.maximum(peak[0], ra[56]), jnp.maximum(x8[0], x9[0]))


def block_kernel(own, mine, flags, ra, rb, ext, ia):
    d, tree, gi, gj, gk = where_am_i()
    even = d % 2 == 0
    flag = [flags[n] > 0.5 for n in range(4)]
    ext[...] = own[...]
    for t, missing in ((0, flag[0]), (7, flag[1])):
        bj, bk = (t >> 1) & 1, (t >> 2) & 1
        row0 = 16 * ((t & 1) ^ tree)
        use_b = even if t == 0 else jnp.logical_not(even)
        for f in range(6):
            for r in range(2):
                for h in range(2):
                    n = f * 4 + r * 2 + h
                    rows = pl.ds(pl.multiple_of(row0 + 8 * r, 8), 8)
                    came = jnp.where(use_b, rb[n], ra[n])
                    ext[f, 2 * bj + h, bk, rows, :] = jnp.where(
                        missing, came, own[f, 2 * bj + h, bk, rows, :]
                    )
    for q in range(4):
        for h in range(2):
            for g in range(4):
                n = (g * 4 + q) * 2 + h
                x = ra[24 + n]
                if q == 0:
                    x = jnp.where(flag[2], mine[g * 2 + h], x)
                if q == 3:
                    x = jnp.where(flag[3], mine[g * 2 + h], x)
                ia[n] = x


def make_block(ext, ia, ib, gi, sub):
    first_high = gi % 2 == 0

    def pair(g, jq, kt):
        n = (g * 4 + jq // 2 + 2 * kt) * 2 + jq % 2
        a, b = ia[n], ib[n]
        return jnp.where(first_high, a, b), jnp.where(first_high, b, a)

    def rows(f, jq, kt, b):
        if b < 4:
            return ext[f, jq, kt, pl.ds(8 * b, 8), :]
        if f == 0:
            return pair(0, jq, kt)[b - 4]
        hi, lo = pair((1, 1, 2, 2, 3, 3)[f], jq, kt)
        if f in (3, 4):
            return rs(jnp.where(sub < 4, lo, hi), 4)
        return jnp.where(sub < 4, hi, lo)

    return rows, pair


J_BLOCKS = 37


def j_place(f, kt, b):
    if f == 0:
        return kt * 6 + b
    if f == 5:
        return 32 + b
    return (12 if f in (2, 4) else 22) + kt * 5 + b


def third_kernel(ext, ia, ib, peak, x64, ja, jb, peak_out):
    d, tree, gi, gj, gk = where_am_i()
    sub, lane = iotas()
    rows, _ = make_block(ext, ia, ib, gi, sub)
    even = gj % 2 == 0

    def put(f, kt, b, get):
        lo, hi = get(0), get(3)
        ja[j_place(f, kt, b)] = jnp.where(even, hi, lo)
        jb[j_place(f, kt, b)] = jnp.where(even, lo, hi)

    for b in range(6):
        for kt in range(2):
            put(0, kt, b, lambda jq: rows(0, jq, kt, b))
    for b in range(5):
        for kt in range(2):
            def five(jq):
                nat = lane < 80 if jq == 0 else lane >= 48
                turn = 80 if jq == 0 else -80
                return jnp.where(nat, rows(2, jq, kt, b), rl(rows(4, jq, kt, b), turn))

            def four(jq):
                nat = lane < 64 if jq == 0 else lane >= 64
                return jnp.where(nat, rows(1, jq, kt, b), rl(rows(3, jq, kt, b), 64))

            put(2, kt, b, five)
            put(1, kt, b, four)

        def both(jq):
            nat = lane < 64 if jq == 0 else lane >= 64
            return jnp.where(nat, rows(5, jq, 0, b), rl(rows(5, jq, 1, b), 64))

        put(5, 0, b, both)
    top = jnp.maximum(peak[0], x64[0])
    ja[J_BLOCKS] = top
    jb[J_BLOCKS] = top
    peak_out[0] = top


def make_wide(rows, ja, jb, gj):
    first_high = gj % 2 == 0

    def wide(f, jq, kt, b):
        if jq < 4:
            return rows(f, jq, kt, b)
        n = j_place(f, kt, b)
        if jq == 4:
            x = jnp.where(first_high, ja[n], jb[n])
        else:
            x = jnp.where(first_high, jb[n], ja[n])
        if f == 4:
            return rl(x, -80 if jq == 4 else 80)
        return rl(x, 64) if f == 3 or (f == 5 and kt == 1) else x

    return wide


K_BLOCKS = 43


def k_place(kind, jt, b):
    if kind == 0:
        return jt * 6 + b
    if jt == 2:
        return 38 + b
    return (18 if kind < 3 else 28) + jt * 5 + b


def pack_k(get, ka, kb, gk, lane):
    even = gk % 2 == 0
    near = lane % 16 < 8
    k8 = lane % 8

    def put(n, lo, hi):
        ka[n] = jnp.where(even, hi, lo)
        kb[n] = jnp.where(even, lo, hi)

    def squeeze(first, last, kt):
        if kt == 0:
            return jnp.where(near, first, rl(last, 8))
        return jnp.where(near, rl(first, -8), last)

    def join(kind, value, kt):
        if kind == 1:
            nat, turn = (k8 < 5, 5) if kt == 0 else (k8 >= 3, -5)
        else:
            nat, turn = (k8 < 4, 4) if kt == 0 else (k8 >= 4, -4)
        return jnp.where(nat, value(kind), rl(value(kind + 1), turn))

    for jt in range(3):
        for b in range(6):
            sides = [squeeze(get(0, 2 * jt, kt, b), get(0, 2 * jt + 1, kt, b), kt) for kt in range(2)]
            put(k_place(0, jt, b), *sides)
    for jt in range(2):
        for kind in (1, 3):
            for b in range(5):
                sides = [
                    join(
                        kind,
                        lambda n: squeeze(get(n, 2 * jt, kt, b), get(n, 2 * jt + 1, kt, b), kt),
                        kt,
                    )
                    for kt in range(2)
                ]
                put(k_place(kind, jt, b), *sides)
    for b in range(5):
        sides = []
        for kt in range(2):
            both = [
                join(kind, lambda n: jnp.where(lane < 64, get(n, 4, kt, b), get(n, 5, kt, b)), kt)
                for kind in (1, 3)
            ]
            sides.append(squeeze(*both, kt))
        put(k_place(1, 2, b), *sides)


def coefficient_kernel(neighbours, levels, refine, out, table, ratio):
    d, tree, gi, gj, gk = where_am_i()
    sub, lane = iotas()
    for n in range(7):
        ratio[n] = 2.0 / (1.0 + 2.0 ** (n - 3))

    def one(pos, carry):
        ip, jp, kp = pos >> 4, (pos >> 2) & 3, pos & 3
        x = 2 * gi + jnp.where(ip == 3, -1, ip)
        y = 2 * gj + jnp.where(jp == 3, -1, jp)
        z = 2 * gk + jnp.where(kp == 3, -1, kp)
        inside = (x >= 0) & (x < 16) & (y >= 0) & (y < 8) & (z >= 0) & (z < 8)
        upper = x >= 8
        lx = jnp.where(upper, 15 - x, x)
        code = jnp.where(upper, 512, 0)
        for bit in range(3):
            for axis, v in enumerate((lx, y, z)):
                code = code | (((v >> bit) & 1) << (3 * bit + axis))
        code = jnp.where(inside, code, 0)
        level = levels[code]
        depth = level + refine[code]
        for f in range(6):
            p = neighbours[code * 6 + f]
            opened = inside & (p >= 0)
            safe = jnp.maximum(p, 0)
            other = levels[safe] + refine[safe]
            table[f * 64 + pos] = jnp.where(opened, 1.0, 0.0)
            table[(6 + f) * 64 + pos] = jnp.where(opened, ratio[depth - other + 3], 1.0)
        table[12 * 64 + pos] = jnp.left_shift(1, level).astype(F32)
        table[13 * 64 + pos] = jnp.left_shift(1, 6 - 2 * depth).astype(F32) * (2.0 / 64.0)
        return carry

    lax.fori_loop(0, 64, one, 0)

    def expand(step, carry):
        item, jp = step >> 2, step & 3
        base = item * 64 + jp * 4
        vals = {}
        for ip in range(4):
            v = [jnp.full((8, 128), table[base + ip * 16 + kp], F32) for kp in range(4)]
            vals[ip] = (v[0], v[1], jnp.where(lane % 16 < 8, v[2], v[3]))
        for kt in range(3):
            out[item, jp, kt, 0] = vals[0][kt]
            out[item, jp, kt, 1] = vals[1][kt]
            out[item, jp, kt, 2] = jnp.where(sub < 4, vals[2][kt], vals[3][kt])
        return carry

    lax.fori_loop(0, 56, expand, 0)


def coefficient(coef, item, jt, kt):
    a, b, c = (coef[item, jt, kt, n] for n in range(3))
    return jnp.concatenate([a, a, b, b, c], axis=0)


def minmod(a, b):
    return jnp.maximum(jnp.minimum(a, b), 0.0) + jnp.minimum(jnp.maximum(a, b), 0.0)


def face_change(c, up1, up2, dn1, dn2, u, u_up, u_dn):
    upper, lower = up1 - c, c - dn1
    half = 0.5 * minmod(upper, lower)
    half_up = 0.5 * minmod(up2 - up1, upper)
    half_dn = 0.5 * minmod(lower, dn1 - dn2)
    w_up, w_dn = 0.5 * (u + u_up), 0.5 * (u_dn + u)
    flux_up = jnp.maximum(w_up, 0.0) * (c + half) + jnp.minimum(w_up, 0.0) * (up1 - half_up)
    flux_dn = jnp.maximum(w_dn, 0.0) * (dn1 + half_dn) + jnp.minimum(w_dn, 0.0) * (c - half)
    return flux_up - flux_dn


def wrap48(x, sub):
    return jnp.concatenate([x[:32], jnp.where(sub < 4, x[32:40], x[40:48])], axis=0)


class Shifts:
    def __init__(self):
        self.sub, self.lane = iotas()
        self.row = lax.broadcasted_iota(jnp.int32, (40, 128), 0)
        self.lane5 = lax.broadcasted_iota(jnp.int32, (40, 128), 1)
        self.k16 = self.lane5 % 16
        row = self.row
        self.i_top1 = (row == 15) | (row == 31) | (row == 39)
        self.i_top2 = self.i_top1 | (row == 14) | (row == 30) | (row == 38)
        self.i_bot1 = (row == 0) | (row == 16) | (row == 32)
        self.i_bot2 = self.i_bot1 | (row == 1) | (row == 17) | (row == 33)

    def wrap(self, x):
        return wrap48(x, self.sub)

    def k_up(self, x, nxt, n, m=None):
        nxt = rl(nxt, 16 - n)
        return jnp.where(self.k16 < 16 - n, rl(x, -n), nxt if m is None else m * nxt)

    def k_dn(self, x, prv, n, m=None):
        prv = rl(prv, n - 16)
        return jnp.where(self.k16 >= n, rl(x, n), prv if m is None else m * prv)

    def j_up(self, x, nxt, n):
        return rl(jnp.where(self.lane5 < 16 * n, nxt, x), -16 * n)

    def j_dn(self, x, prv, n):
        return rl(jnp.where(self.lane5 >= 128 - 16 * n, prv, x), 16 * n)

    def change_ij(self, jq, kt, coef, c40, u1, c48, v48):
        jt = tile_j(jq)
        jn, jp = lax.rem(jq + 1, 6), lax.rem(jq + 5, 6)
        odd = jq % 2 == 1
        lane5 = self.lane5
        c = c40(jq)
        m_dn = jnp.where(odd, 1.0, coefficient(coef, 2, jt, kt))
        m_up = jnp.where(odd, coefficient(coef, 3, jt, kt), 1.0)
        up_m1 = jnp.where(lane5 >= 112, m_up, 1.0)
        up_m2 = jnp.where(lane5 >= 96, m_up, 1.0)
        dn_m1 = jnp.where(lane5 < 16, m_dn, 1.0)
        dn_m2 = jnp.where(lane5 < 32, m_dn, 1.0)
        cn, cp = c40(jn), c40(jp)
        u = u1(jq)
        change = face_change(
            c, self.j_up(c, cn, 1) * up_m1, self.j_up(c, cn, 2) * up_m2,
            self.j_dn(c, cp, 1) * dn_m1, self.j_dn(c, cp, 2) * dn_m2,
            u, self.j_up(u, u1(jn), 1) * up_m1, self.j_dn(u, u1(jp), 1) * dn_m1,
        )
        m_dn, m_up = coefficient(coef, 0, jt, kt), coefficient(coef, 1, jt, kt)
        up_m1, up_m2 = jnp.where(self.i_top1, m_up, 1.0), jnp.where(self.i_top2, m_up, 1.0)
        dn_m1, dn_m2 = jnp.where(self.i_bot1, m_dn, 1.0), jnp.where(self.i_bot2, m_dn, 1.0)
        wrap = self.wrap
        return change + face_change(
            c, wrap(rs(c48, -1)) * up_m1, wrap(rs(c48, -2)) * up_m2,
            wrap(rs(c48, 1)) * dn_m1, wrap(rs(c48, 2)) * dn_m2,
            wrap(v48), wrap(rs(v48, -1)) * up_m1, wrap(rs(v48, 1)) * dn_m1,
        )


def tile_j(jq):
    return jnp.where(jq < 4, jq >> 1, jq - 2)


def early_kernel(
    ext, ia, ib, ja, jb, peak, x16, coef,
    c40, u2, src, prs, chg, ka, kb, peak_out,
    c48, v48, u1,
):
    d, tree, gi, gj, gk = where_am_i()
    sh = Shifts()
    sub = sh.sub
    rows, pair = make_block(ext, ia, ib, gi, sub)
    wide = make_wide(rows, ja, jb, gj)
    dest = (c48, v48, u1, u2, src, prs)
    for f in range(6):
        for jq in range(6):
            for kt in range(2):
                for b in range(6 if f == 0 else 5):
                    x = wide(f, jq, kt, b)
                    if f == 1 and b == 4:
                        hi, lo = pair(1, jq, kt) if jq < 4 else (x, x)
                        v48[jq, kt, pl.ds(32, 8), :] = hi
                        v48[jq, kt, pl.ds(40, 8), :] = lo
                    else:
                        dest[f][jq, kt, pl.ds(8 * b, 8), :] = x
                    if f == 0 and b < 4:
                        c40[jq, kt, pl.ds(8 * b, 8), :] = x
                if f == 0:
                    c40[jq, kt, pl.ds(32, 8), :] = jnp.where(
                        sub < 4, c48[jq, kt, pl.ds(32, 8), :], c48[jq, kt, pl.ds(40, 8), :]
                    )

    def step(jq, carry):
        for kt in range(2):
            chg[jq, kt] = sh.change_ij(
                jq, kt, coef, lambda n: c40[n, kt], lambda n: u1[n, kt], c48[jq, kt], v48[jq, kt]
            )
        return carry

    lax.fori_loop(0, 6, step, 0)
    kinds = (c48, u2, src, chg, prs)
    pack_k(
        lambda kind, jq, kt, b: kinds[kind][jq, kt, pl.ds(8 * b, 8), :], ka, kb, gk, sh.lane
    )
    top = jnp.maximum(
        jnp.maximum(peak[0], x16[0]), jnp.maximum(ja[J_BLOCKS], jb[J_BLOCKS])
    )
    ka[K_BLOCKS] = top
    kb[K_BLOCKS] = top
    peak_out[0] = top


def main_kernel(
    c_in, u_in, s_in, p_in, chg_in, ka, kb, peak, x32, coef,
    out_adv, out_p, send_a, send_b,
    c_k, u2, src, p_k, chg_k, p0, p1, adv, mob, hgt, rhs, wts,
):
    d, tree, gi, gj, gk = where_am_i()
    sh = Shifts()
    sub, lane, lane5, k16 = sh.sub, sh.lane, sh.lane5, sh.k16
    near = lane % 16 < 8
    k_even = gk % 2 == 0

    def sides(kind, jt, b):
        a, e = ka[k_place(kind, jt, b)], kb[k_place(kind, jt, b)]
        low, high = jnp.where(k_even, a, e), jnp.where(k_even, e, a)
        if jt == 2 and kind == 3:
            low, high = rl(low, -8), rl(high, 0)
        elif jt == 2 and kind == 1:
            low, high = low, rl(high, 8)
        return low, high

    for b in range(6):
        for jt in range(3):
            low, high = sides(0, jt, b)
            halves_of = (
                jnp.where(near, low, rl(high, 8)), jnp.where(near, rl(low, -8), high)
            )
            for jq, x in zip((2 * jt, 2 * jt + 1), halves_of):
                if b < 4:
                    c_k[jq, pl.ds(8 * b, 8), :] = x
                elif b == 4:
                    c_k[jq, pl.ds(32, 8), :] = x
                else:
                    c_k[jq, pl.ds(32, 8), :] = jnp.where(sub < 4, c_k[jq, pl.ds(32, 8), :], x)
    dest = {1: u2, 2: src, 3: chg_k, 4: p_k}
    for b in range(5):
        for kind in (1, 3):
            turn = 5 if kind == 1 else 4
            for jt in range(3):
                low, high = sides(kind, jt, b)
                for n in range(2):
                    if n == 1:
                        low, high = rl(low, -turn), rl(high, turn)
                    if jt == 2:
                        first = last = jnp.where(near, low, high)
                    else:
                        first = jnp.where(near, low, rl(high, 8))
                        last = jnp.where(near, rl(low, -8), high)
                    dest[kind + n][2 * jt, pl.ds(8 * b, 8), :] = first
                    dest[kind + n][2 * jt + 1, pl.ds(8 * b, 8), :] = last

    def c40(jq, kt):
        return c_k[jq] if kt == 2 else c_in[jq, kt]

    def uk(jq, kt):
        return u2[jq] if kt == 2 else u_in[jq, kt]

    top = jnp.maximum(
        jnp.maximum(peak[0], x32[0]), jnp.maximum(ka[K_BLOCKS], kb[K_BLOCKS])
    )
    top = jnp.max(top, keepdims=True)
    step = jnp.broadcast_to(CFL / top, (8, 128))
    step = jnp.concatenate([step] * 5, axis=0)

    def advance(jq, carry):
        jt = tile_j(jq)
        for kt in range(3):
            kn, kp = (kt + 1) % 3, (kt + 2) % 3
            change = chg_k[jq] if kt == 2 else chg_in[jq, kt]
            c = c40(jq, kt)
            m_dn, m_up = coefficient(coef, 4, jt, kt), coefficient(coef, 5, jt, kt)
            cn, cp = c40(jq, kn), c40(jq, kp)
            up1, up2 = sh.k_up(c, cn, 1, m_up), sh.k_up(c, cn, 2, m_up)
            dn1, dn2 = sh.k_dn(c, cp, 1, m_dn), sh.k_dn(c, cp, 2, m_dn)
            hgt[jq, kt] = dn2 + dn1 + c + up1 + up2
            u = uk(jq, kt)
            u_up, u_dn = sh.k_up(u, uk(jq, kn), 1, m_up), sh.k_dn(u, uk(jq, kp), 1, m_dn)
            change = change + face_change(c, up1, up2, dn1, dn2, u, u_up, u_dn)
            a = jnp.clip(c - step * coefficient(coef, 12, jt, kt) * change, 0.0, 1.0)
            adv[jq, kt] = a
            mob[jq, kt] = 1.0 / (RHO_GAS + (RHO_LIQ - RHO_GAS) * a)
        return carry

    lax.fori_loop(0, 6, advance, 0)

    def weigh(jq, carry):
        jt = tile_j(jq)
        jn, jp = lax.rem(jq + 1, 6), lax.rem(jq + 5, 6)
        odd = jq % 2 == 1
        for kt in range(3):
            kn, kp = (kt + 1) % 3, (kt + 2) % 3
            mi_dn = jnp.where(sh.i_bot1, coefficient(coef, 0, jt, kt), 1.0)
            mi_up = jnp.where(sh.i_top1, coefficient(coef, 1, jt, kt), 1.0)
            at_dn = (lane5 < 16) & jnp.logical_not(odd)
            at_up = (lane5 >= 112) & odd
            mj_dn = jnp.where(at_dn, coefficient(coef, 2, jt, kt), 1.0)
            mj_up = jnp.where(at_up, coefficient(coef, 3, jt, kt), 1.0)
            h = hgt[jq, kt]
            h_up, h_dn = rs(h, -1) * mi_up, rs(h, 1) * mi_dn
            gx, sx = 0.5 * (h_up - h_dn), h_up - 2.0 * h + h_dn
            h_up = sh.j_up(h, hgt[jn, kt], 1) * mj_up
            h_dn = sh.j_dn(h, hgt[jp, kt], 1) * mj_dn
            gy, sy = 0.5 * (h_up - h_dn), h_up - 2.0 * h + h_dn
            gx2, gy2 = gx * gx, gy * gy
            root = lax.rsqrt(1.0 + gx2 + gy2)
            bend = (sx * (1.0 + gy2) + sy * (1.0 + gx2)) * coefficient(coef, 12, jt, kt) * (root * root * root)
            right = (src[jq] if kt == 2 else s_in[jq, kt]) - SIGMA * bend * adv[jq, kt]
            m = mob[jq, kt]
            mk_dn = jnp.where(k16 < 1, coefficient(coef, 4, jt, kt), 1.0)
            mk_up = jnp.where(k16 >= 15, coefficient(coef, 5, jt, kt), 1.0)
            across = (
                rs(m, 1), rs(m, -1),
                sh.j_dn(m, mob[jp, kt], 1), sh.j_up(m, mob[jn, kt], 1),
                sh.k_dn(m, mob[jq, kp], 1), sh.k_up(m, mob[jq, kn], 1),
            )
            masks = (mi_dn, mi_up, mj_dn, mj_up, mk_dn, mk_up)
            edges = (sh.i_bot1, sh.i_top1, at_dn, at_up, k16 < 1, k16 >= 15)
            diag = jnp.zeros_like(m)
            parts = []
            for f in range(6):
                w = (m + masks[f] * across[f]) * jnp.where(edges[f], coefficient(coef, 6 + f, jt, kt), 1.0)
                diag = diag + w
                parts.append(w * masks[f])
            inv = 1.0 / diag
            for f in range(6):
                wts[f, jq, kt] = parts[f] * inv
            rhs[jq, kt] = right * coefficient(coef, 13, jt, kt) * inv
        return carry

    lax.fori_loop(0, 6, weigh, 0)

    for sweep in range(SWEEPS):
        new = p0 if sweep % 2 == 0 else p1
        older = p1 if sweep % 2 == 0 else p0
        last = sweep == SWEEPS - 1

        def old(jq, kt, sweep=sweep, older=older):
            if sweep:
                return older[jq, kt]
            return p_k[jq] if kt == 2 else p_in[jq, kt]

        def relax(jq, carry, old=old, new=new, last=last):
            jn, jp = lax.rem(jq + 1, 6), lax.rem(jq + 5, 6)
            for kt in range(2 if last else 3):
                kn, kp = (kt + 1) % 3, (kt + 2) % 3
                p = old(jq, kt)
                total = wts[0, jq, kt] * rs(p, 1) + wts[1, jq, kt] * rs(p, -1)
                total = total + wts[2, jq, kt] * sh.j_dn(p, old(jp, kt), 1)
                total = total + wts[3, jq, kt] * sh.j_up(p, old(jn, kt), 1)
                total = total + wts[4, jq, kt] * sh.k_dn(p, old(jq, kp), 1)
                total = total + wts[5, jq, kt] * sh.k_up(p, old(jq, kn), 1)
                total = total - rhs[jq, kt]
                if last:
                    out_p[jq, kt] = total[:32]
                    out_adv[jq, kt] = adv[jq, kt][:32]
                else:
                    new[jq, kt] = total
            return carry

        lax.fori_loop(0, 4 if last else 6, relax, 0)

    even = d % 2 == 0
    for h in range(2):
        for n, ref in enumerate((out_adv, out_p)):
            low, high = tile_half(ref, 0, h, tree), tile_half(ref, 7, h, tree)
            send_a[n, :, halves(h)] = jnp.where(even, high, low)
            send_b[n, :, halves(h)] = jnp.where(even, low, high)


def tile_half(ref, t, h, tree):
    row0 = pl.multiple_of(16 * ((t & 1) ^ tree), 16)
    return ref[2 * ((t >> 1) & 1) + h, (t >> 2) & 1, pl.ds(row0, 16), :]


def slots_kernel(adv, prs, bounds, vof, pres):
    d, tree, gi, gj, gk = where_am_i()
    start = bounds[d]
    count = bounds[d + 1] - start
    off = 8 * d - start
    vof[...] = jnp.zeros_like(vof)
    pres[...] = jnp.zeros_like(pres)
    for t in range(8):
        slot = t + off

        @pl.when((slot >= 0) & (slot < count))
        def _(t=t, slot=slot):
            for h in range(2):
                vof[slot, :, halves(h)] = tile_half(adv, t, h, tree)
                pres[slot, :, halves(h)] = tile_half(prs, t, h, tree)


VM = pl.BlockSpec(memory_space=pltpu.VMEM)
SM = pl.BlockSpec(memory_space=pltpu.SMEM)


def shape(*dims):
    return jax.ShapeDtypeStruct(dims, F32)


def blocks(n):
    return shape(n, 8, 128)


def call(kernel, specs, outs, args, scratch=(), micros=1, mib=8):
    return pl.pallas_call(
        kernel,
        out_shape=outs,
        in_specs=specs,
        out_specs=jax.tree.map(lambda _: VM, outs),
        scratch_shapes=list(scratch),
        compiler_params=pltpu.CompilerParams(vmem_limit_bytes=mib * 1024 * 1024),
        cost_estimate=pl.CostEstimate(
            flops=micros * 1000000, bytes_accessed=micros * 3000000, transcendentals=0
        ),
    )(*args)


def local(volume, velocity, source, pressure_prev, neighbours, levels, refine, bounds_old, bounds_new):
    d = lax.axis_index("row") * 16 + lax.axis_index("col")
    one = blocks(1)
    old = jnp.concatenate([volume[None], velocity, source[None], pressure_prev[None]], axis=0)
    start = bounds_old[d]
    own_levels = lax.dynamic_slice_in_dim(jnp.pad(levels, (0, 16)), start, 14, 0)
    facts = jnp.concatenate([jnp.stack([8 * d - start, bounds_old[d + 1] - start]), own_levels])
    ra, rb, peak = call(first_kernel, [VM, SM], (blocks(57), blocks(24), one), (old, facts))
    x8, x9 = send(peak, flip_pairs(8)), send(peak, flip_pairs(9))
    rb, ra = send(rb, ODD_PAIRS), send(ra, EVEN_PAIRS)
    own, mine, flags, ib = call(
        own_kernel,
        [VM, SM],
        (shape(6, 4, 2, 32, 128), blocks(8), blocks(FLAG_COUNT), blocks(32)),
        (old, bounds_old),
    )
    ib, peak = call(
        second_kernel, [VM] * 7, (blocks(32), one), (ib, flags, rb, ra, peak, x8, x9)
    )
    x64 = send(peak, flip_pairs(64))
    ib = send(ib, axis_pairs(0, 1))
    ext, ia = call(
        block_kernel,
        [VM] * 5,
        (shape(6, 4, 2, 32, 128), blocks(32)),
        (own, mine, flags, ra, rb),
    )
    ja, jb, peak = call(
        third_kernel,
        [VM] * 5,
        (blocks(J_BLOCKS + 1), blocks(J_BLOCKS + 1), one),
        (ext, ia, ib, peak, x64),
    )
    x16 = send(peak, flip_pairs(16))
    ja, jb = send(ja, axis_pairs(1, 0)), send(jb, axis_pairs(1, 1))
    coef = call(
        coefficient_kernel,
        [SM] * 3,
        shape(14, 4, 3, 3, 8, 128),
        (neighbours.reshape(-1), levels, refine),
        [pltpu.SMEM((14 * 64,), F32), pltpu.SMEM((7,), F32)],
        5,
    )
    part, part_tall = (6, 2, 40, 128), (6, 2, 48, 128)
    *early, ka, kb, peak = call(
        early_kernel,
        [VM] * 8,
        (shape(*part),) * 5 + (blocks(K_BLOCKS + 1),) * 2 + (one,),
        (ext, ia, ib, ja, jb, peak, x16, coef),
        [pltpu.VMEM(part_tall, F32)] * 2 + [pltpu.VMEM(part, F32)],
        2,
        12,
    )
    x32 = send(peak, flip_pairs(32))
    ka, kb = send(ka, axis_pairs(2, 0)), send(kb, axis_pairs(2, 1))
    halo, grid = (6, 40, 128), (6, 3, 40, 128)
    adv, prs, sa, sb = call(
        main_kernel,
        [VM] * 10,
        (shape(4, 2, 32, 128),) * 2 + (shape(2, 16, 256),) * 2,
        (*early, ka, kb, peak, x32, coef),
        [pltpu.VMEM(halo, F32)] * 5
        + [pltpu.VMEM(grid, F32)] * 6
        + [pltpu.VMEM((6, *grid), F32)],
        8,
        16,
    )
    sb, sa = send(sb, ODD_PAIRS), send(sa, EVEN_PAIRS)
    vof, pres = call(slots_kernel, [VM] * 2 + [SM], (shape(10, 16, 256),) * 2, (adv, prs, bounds_new))
    even = d % 2 == 0
    low, high = jnp.where(even, sb, sa), jnp.where(even, sa, sb)
    start, stop = bounds_new[d], bounds_new[d + 1]
    slots = jnp.arange(10, dtype=jnp.int32)
    at_low = ((slots == 0) & (start == 8 * d - 1))[:, None, None]
    at_high = ((slots == 8 * d + 8 - start) & (stop == 8 * d + 9))[:, None, None]
    outs = [
        jnp.where(at_low, low[n][None], jnp.where(at_high, high[n][None], x))
        for n, x in enumerate((vof, pres))
    ]
    return tuple(outs)


def solution(mesh):
    in_specs = (
        P(AXES, None, None),
        P(None, AXES, None, None),
        P(AXES, None, None),
        P(AXES, None, None),
        P(),
        P(),
        P(),
        P(),
        P(),
    )
    out_specs = (P(AXES, None, None), P(AXES, None, None))
    return jax.shard_map(local, mesh=mesh, in_specs=in_specs, out_specs=out_specs, check_vma=False)
```

```python
import jax
import jax.numpy as jnp
from jax import lax
from jax.experimental import pallas as pl
from jax.experimental.pallas import tpu as pltpu
from jax.sharding import PartitionSpec as P

SWEEPS = 4
CFL = 0.4
SIGMA = 0.05
RHO_GAS = 0.05
RHO_LIQ = 1.0
AXES = ("row", "col")
DEVS = 128
F32 = jnp.float32


def block_coords(d):
    tree, low = d >> 6, d & 63
    i = (low & 1) | (((low >> 3) & 1) << 1)
    j = ((low >> 1) & 1) | (((low >> 4) & 1) << 1)
    k = ((low >> 2) & 1) | (((low >> 5) & 1) << 1)
    return (7 - i if tree else i), j, k


PLACE = {block_coords(d): d for d in range(DEVS)}


def axis_pairs(axis, odd):
    count = (8, 4, 4)[axis]
    pairs = []
    for d in range(DEVS):
        c = list(block_coords(d))
        step = 1 if (c[axis] % 2 == 0) != bool(odd) else -1
        c[axis] = (c[axis] + step) % count
        pairs.append((d, PLACE[tuple(c)]))
    return pairs


def flip_pairs(bits):
    return [(d, d ^ bits) for d in range(DEVS)]


EVEN_PAIRS = flip_pairs(1)
ODD_PAIRS = [(d, d + 1 if d % 2 else d - 1) for d in range(1, DEVS - 1)]


def send(x, pairs):
    return lax.ppermute(x, AXES, pairs)


def where_is(d):
    tree = d >> 6
    i = (d & 1) | (((d >> 3) & 1) << 1)
    gi = jnp.where(tree == 1, 7 - i, i)
    gj = ((d >> 1) & 1) | (((d >> 4) & 1) << 1)
    gk = ((d >> 2) & 1) | (((d >> 5) & 1) << 1)
    return tree, gi, gj, gk


def where_am_i():
    d = lax.axis_index("row") * 16 + lax.axis_index("col")
    return d, *where_is(d)


def iotas():
    sub = lax.broadcasted_iota(jnp.int32, (8, 128), 0)
    lane = lax.broadcasted_iota(jnp.int32, (8, 128), 1)
    return sub, lane


def rl(x, shift):
    return pltpu.roll(x, shift % 128, 1)


def rs(x, shift):
    n = x.shape[0]
    return pltpu.roll(x, shift % n, 0)


def halves(h):
    return pl.ds(128 * h, 128)


def old_slice(old, f, slot, start, h):
    return old[f, slot, pl.ds(pl.multiple_of(start, 8), 8), halves(h)]


def slab_groups(get, high, sub):
    nat = (sub >= 4) == high
    return (
        get(0),
        get(1),
        jnp.where(nat, get(2), rs(get(3), 4)),
        jnp.where(nat, get(5), rs(get(4), 4)),
    )


def first_kernel(old, levels, bounds, ra, rb, peak):
    d, tree, gi, gj, gk = where_am_i()
    sub, lane = iotas()
    start = bounds[d]
    count = bounds[d + 1] - start
    off = 8 * d - start
    even = d % 2 == 0
    slot_a = jnp.where(even, 8 + off, 0)
    slot_b = jnp.where(even, 0, 8 + off)
    for f in range(6):
        for r in range(2):
            for h in range(2):
                ra[f * 4 + r * 2 + h] = old_slice(old, f, slot_a, 8 * r, h)
                rb[f * 4 + r * 2 + h] = old_slice(old, f, slot_b, 8 * r, h)
    high = gi % 2 == 0
    row0 = jnp.where(high, 8, 0)
    bit = jnp.where(even, 1, 0)
    for q in range(4):
        for h in range(2):
            slot = jnp.clip(bit + 2 * q + off, 0, 9)
            groups = slab_groups(lambda f: old_slice(old, f, slot, row0, h), high, sub)
            for g in range(4):
                ra[24 + (g * 4 + q) * 2 + h] = groups[g]
    top = jnp.zeros((8, 128), F32)
    for s in range(10):
        level = levels[jnp.minimum(start + s, 1023)]
        inv = jnp.where(s < count, jnp.left_shift(1, level), 0).astype(F32)
        part = jnp.zeros((8, 128), F32)
        for r in range(2):
            for h in range(2):
                u = [jnp.abs(old[1 + a, s, pl.ds(8 * r, 8), halves(h)]) for a in range(3)]
                part = jnp.maximum(part, u[0] + u[1] + u[2])
        top = jnp.maximum(top, part * inv)
    ra[56] = top
    peak[0] = top


FLAG_COUNT = 6


def own_kernel(old, bounds, ext, mine, flags, ib):
    d, tree, gi, gj, gk = where_am_i()
    sub, lane = iotas()
    off = 8 * d - bounds[d]
    even = d % 2 == 0
    for t in range(8):
        slot = jnp.clip(t + off, 0, 9)
        bj, bk = (t >> 1) & 1, (t >> 2) & 1
        row0 = 16 * ((t & 1) ^ tree)
        for f in range(6):
            for r in range(2):
                for h in range(2):
                    rows = pl.ds(pl.multiple_of(row0 + 8 * r, 8), 8)
                    ext[f, 2 * bj + h, bk, rows, :] = old_slice(old, f, slot, 8 * r, h)
    high = gi % 2 == 1
    row0 = jnp.where(high, 8, 0)
    slot_a = jnp.where(even, 8 + off, 0)
    bit = jnp.where(even, 0, 1)
    for h in range(2):
        groups = slab_groups(lambda f: old_slice(old, f, slot_a, row0, h), high, sub)
        for g in range(4):
            mine[g * 2 + h] = groups[g]
        for q in range(4):
            slot = jnp.clip(bit + 2 * q + off, 0, 9)
            groups = slab_groups(lambda f: old_slice(old, f, slot, row0, h), high, sub)
            for g in range(4):
                ib[(g * 4 + q) * 2 + h] = groups[g]
    odd = jnp.logical_not(even)
    first, last = bounds[d] == 8 * d + 1, bounds[d + 1] == 8 * d + 7
    values = (
        first,
        last,
        even & (bounds[d + 1] == 8 * d + 9),
        odd & (bounds[d] == 8 * d - 1),
        even & first,
        odd & last,
    )
    for n, value in enumerate(values):
        flags[n] = jnp.full((8, 128), jnp.where(value, 1.0, 0.0), F32)


def second_kernel(ib_in, flags, rb, ra, peak, x8, x9, ib, peak_out):
    d, tree, gi, gj, gk = where_am_i()
    sub, lane = iotas()
    high = gi % 2 == 1
    block = jnp.where(high, 2, 0)
    for q in range(4):
        for h in range(2):
            if q in (0, 3):
                groups = slab_groups(lambda f: rb[f * 4 + block + h], high, sub)
                flag = flags[4 if q == 0 else 5] > 0.5
            for g in range(4):
                n = (g * 4 + q) * 2 + h
                ib[n] = jnp.where(flag, groups[g], ib_in[n]) if q in (0, 3) else ib_in[n]
    peak_out[0] = jnp.maximum(jnp.maximum(peak[0], ra[56]), jnp.maximum(x8[0], x9[0]))


def block_kernel(own, mine, flags, ra, rb, ext, ia):
    d, tree, gi, gj, gk = where_am_i()
    even = d % 2 == 0
    flag = [flags[n] > 0.5 for n in range(4)]
    ext[...] = own[...]
    for t, missing in ((0, flag[0]), (7, flag[1])):
        bj, bk = (t >> 1) & 1, (t >> 2) & 1
        row0 = 16 * ((t & 1) ^ tree)
        use_b = even if t == 0 else jnp.logical_not(even)
        for f in range(6):
            for r in range(2):
                for h in range(2):
                    n = f * 4 + r * 2 + h
                    rows = pl.ds(pl.multiple_of(row0 + 8 * r, 8), 8)
                    came = jnp.where(use_b, rb[n], ra[n])
                    ext[f, 2 * bj + h, bk, rows, :] = jnp.where(
                        missing, came, own[f, 2 * bj + h, bk, rows, :]
                    )
    for q in range(4):
        for h in range(2):
            for g in range(4):
                n = (g * 4 + q) * 2 + h
                x = ra[24 + n]
                if q == 0:
                    x = jnp.where(flag[2], mine[g * 2 + h], x)
                if q == 3:
                    x = jnp.where(flag[3], mine[g * 2 + h], x)
                ia[n] = x


def make_block(ext, ia, ib, gi, sub):
    first_high = gi % 2 == 0

    def pair(g, jq, kt):
        n = (g * 4 + jq // 2 + 2 * kt) * 2 + jq % 2
        a, b = ia[n], ib[n]
        return jnp.where(first_high, a, b), jnp.where(first_high, b, a)

    def rows(f, jq, kt, b):
        if b < 4:
            return ext[f, jq, kt, pl.ds(8 * b, 8), :]
        if f == 0:
            return pair(0, jq, kt)[b - 4]
        hi, lo = pair((1, 1, 2, 2, 3, 3)[f], jq, kt)
        if f in (3, 4):
            return rs(jnp.where(sub < 4, lo, hi), 4)
        return jnp.where(sub < 4, hi, lo)

    return rows, pair


J_BLOCKS = 37


def j_place(f, kt, b):
    if f == 0:
        return kt * 6 + b
    if f == 5:
        return 32 + b
    return (12 if f in (2, 4) else 22) + kt * 5 + b


def third_kernel(ext, ia, ib, peak, x64, ja, jb, peak_out):
    d, tree, gi, gj, gk = where_am_i()
    sub, lane = iotas()
    rows, _ = make_block(ext, ia, ib, gi, sub)
    even = gj % 2 == 0

    def put(f, kt, b, get):
        lo, hi = get(0), get(3)
        ja[j_place(f, kt, b)] = jnp.where(even, hi, lo)
        jb[j_place(f, kt, b)] = jnp.where(even, lo, hi)

    for b in range(6):
        for kt in range(2):
            put(0, kt, b, lambda jq: rows(0, jq, kt, b))
    for b in range(5):
        for kt in range(2):
            def five(jq):
                nat = lane < 80 if jq == 0 else lane >= 48
                turn = 80 if jq == 0 else -80
                return jnp.where(nat, rows(2, jq, kt, b), rl(rows(4, jq, kt, b), turn))

            def four(jq):
                nat = lane < 64 if jq == 0 else lane >= 64
                return jnp.where(nat, rows(1, jq, kt, b), rl(rows(3, jq, kt, b), 64))

            put(2, kt, b, five)
            put(1, kt, b, four)

        def both(jq):
            nat = lane < 64 if jq == 0 else lane >= 64
            return jnp.where(nat, rows(5, jq, 0, b), rl(rows(5, jq, 1, b), 64))

        put(5, 0, b, both)
    top = jnp.maximum(peak[0], x64[0])
    ja[J_BLOCKS] = top
    jb[J_BLOCKS] = top
    peak_out[0] = top


def make_wide(rows, ja, jb, gj):
    first_high = gj % 2 == 0

    def wide(f, jq, kt, b):
        if jq < 4:
            return rows(f, jq, kt, b)
        n = j_place(f, kt, b)
        if jq == 4:
            x = jnp.where(first_high, ja[n], jb[n])
        else:
            x = jnp.where(first_high, jb[n], ja[n])
        if f == 4:
            return rl(x, -80 if jq == 4 else 80)
        return rl(x, 64) if f == 3 or (f == 5 and kt == 1) else x

    return wide


K_BLOCKS = 38


def k_place(kind, jt, b):
    if jt == 2:
        return 30 + b
    return (0, 10, 10, 20, 20)[kind] + jt * 5 + b


class KPack:
    def __init__(self, gk, lane):
        self.even = gk % 2 == 0
        self.near = lane % 16 < 8
        self.k8 = lane % 8

    def put(self, ka, kb, n, lo, hi):
        ka[n] = jnp.where(self.even, hi, lo)
        kb[n] = jnp.where(self.even, lo, hi)

    def squeeze(self, first, last, kt):
        if kt == 0:
            return jnp.where(self.near, first, rl(last, 8))
        return jnp.where(self.near, rl(first, -8), last)

    def join(self, kind, value, kt):
        if kind == 0:
            return value(0)
        if kind == 1:
            nat, turn = (self.k8 < 5, 5) if kt == 0 else (self.k8 >= 3, -5)
        else:
            nat, turn = (self.k8 < 4, 4) if kt == 0 else (self.k8 >= 4, -4)
        return jnp.where(nat, value(kind), rl(value(kind + 1), turn))

    def block(self, kinds, get, ka, kb):
        for jt in range(2):
            for kind in kinds:
                for b in range(5):
                    sides = []
                    for kt in range(2):

                        def value(n):
                            one, two = get(n, 2 * jt, kt, b), get(n, 2 * jt + 1, kt, b)
                            return self.squeeze(one, two, kt)

                        sides.append(self.join(kind, value, kt))
                    self.put(ka, kb, k_place(kind, jt, b), *sides)

    def halo(self, get, ka, kb):
        for n in range(8):
            sides = []
            for kt in range(2):
                packs = []
                for m in (n, min(n + 8, 14)):
                    kind, b = (0, 1, 3)[m // 5], m % 5
                    packs.append(self.join(kind, lambda f: get(f, kt, b), kt))
                sides.append(self.squeeze(*packs, kt))
            self.put(ka, kb, 30 + n, *sides)


def coefficient_kernel(neighbours, levels, refine, out, table, ratio):
    d, tree, gi, gj, gk = where_am_i()
    sub, lane = iotas()
    for n in range(7):
        ratio[n] = 2.0 / (1.0 + 2.0 ** (n - 3))

    def one(pos, carry):
        ip, jp, kp = pos >> 4, (pos >> 2) & 3, pos & 3
        x = 2 * gi + jnp.where(ip == 3, -1, ip)
        y = 2 * gj + jnp.where(jp == 3, -1, jp)
        z = 2 * gk + jnp.where(kp == 3, -1, kp)
        inside = (x >= 0) & (x < 16) & (y >= 0) & (y < 8) & (z >= 0) & (z < 8)
        upper = x >= 8
        lx = jnp.where(upper, 15 - x, x)
        code = jnp.where(upper, 512, 0)
        for bit in range(3):
            for axis, v in enumerate((lx, y, z)):
                code = code | (((v >> bit) & 1) << (3 * bit + axis))
        code = jnp.where(inside, code, 0)
        level = levels[code]
        depth = level + refine[code]
        for f in range(6):
            p = neighbours[code * 6 + f]
            opened = inside & (p >= 0)
            safe = jnp.maximum(p, 0)
            other = levels[safe] + refine[safe]
            table[f * 64 + pos] = jnp.where(opened, 1.0, 0.0)
            table[(6 + f) * 64 + pos] = jnp.where(opened, ratio[depth - other + 3], 1.0)
        table[12 * 64 + pos] = jnp.left_shift(1, level).astype(F32)
        table[13 * 64 + pos] = jnp.left_shift(1, 6 - 2 * depth).astype(F32) * (2.0 / 64.0)
        return carry

    lax.fori_loop(0, 64, one, 0, unroll=4)

    def expand(step, carry):
        base = step * 64

        def tiles(jp):
            vals = []
            for ip in range(4):
                n = base + ip * 16 + jp * 4
                v = [jnp.full((8, 128), table[n + kp], F32) for kp in range(4)]
                vals.append((v[0], v[1], jnp.where(lane % 16 < 8, v[2], v[3])))
            return [
                [vals[0][kt], vals[1][kt], jnp.where(sub < 4, vals[2][kt], vals[3][kt])]
                for kt in range(3)
            ]

        high, low = tiles(2), tiles(3)
        sets = (
            tiles(0),
            tiles(1),
            [[jnp.where(lane < 64, high[k][n], low[k][n]) for n in range(3)] for k in range(3)],
        )
        for jt in range(3):
            for kt in range(3):
                for n in range(3):
                    out[step, jt, kt, n] = sets[jt][kt][n]
        return carry

    lax.fori_loop(0, 14, expand, 0)


def coefficient(coef, item, jt, kt):
    a, b, c = (coef[item, jt, kt, n] for n in range(3))
    return jnp.concatenate([a, a, b, b, c], axis=0)


def minmod(a, b):
    return jnp.maximum(jnp.minimum(a, b), 0.0) + jnp.minimum(jnp.maximum(a, b), 0.0)


def face_change(c, up1, up2, dn1, dn2, u, u_up, u_dn):
    upper, lower = up1 - c, c - dn1
    half = 0.5 * minmod(upper, lower)
    half_up = 0.5 * minmod(up2 - up1, upper)
    half_dn = 0.5 * minmod(lower, dn1 - dn2)
    w_up, w_dn = 0.5 * (u + u_up), 0.5 * (u_dn + u)
    flux_up = jnp.maximum(w_up, 0.0) * (c + half) + jnp.minimum(w_up, 0.0) * (up1 - half_up)
    flux_dn = jnp.maximum(w_dn, 0.0) * (dn1 + half_dn) + jnp.minimum(w_dn, 0.0) * (c - half)
    return flux_up - flux_dn


def wrap48(x, sub):
    return jnp.concatenate([x[:32], jnp.where(sub < 4, x[32:40], x[40:48])], axis=0)


class Shifts:
    def __init__(self):
        self.sub, self.lane = iotas()
        self.row = lax.broadcasted_iota(jnp.int32, (40, 128), 0)
        self.lane5 = lax.broadcasted_iota(jnp.int32, (40, 128), 1)
        self.k16 = self.lane5 % 16
        row = self.row
        self.i_top1 = (row == 15) | (row == 31) | (row == 39)
        self.i_top2 = self.i_top1 | (row == 14) | (row == 30) | (row == 38)
        self.i_bot1 = (row == 0) | (row == 16) | (row == 32)
        self.i_bot2 = self.i_bot1 | (row == 1) | (row == 17) | (row == 33)

    def wrap(self, x):
        return wrap48(x, self.sub)

    def k_up(self, x, nxt, n, m=None):
        nxt = rl(nxt, 16 - n)
        return jnp.where(self.k16 < 16 - n, rl(x, -n), nxt if m is None else m * nxt)

    def k_dn(self, x, prv, n, m=None):
        prv = rl(prv, n - 16)
        return jnp.where(self.k16 >= n, rl(x, n), prv if m is None else m * prv)

    def j_up(self, x, nxt, n):
        return rl(jnp.where(self.lane5 < 16 * n, nxt, x), -16 * n)

    def j_dn(self, x, prv, n):
        return rl(jnp.where(self.lane5 >= 128 - 16 * n, prv, x), 16 * n)

    def change_j(self, c, cn, cp, u, un, up, m_dn, m_up):
        lane5 = self.lane5

        def masked(x, m, at):
            return x if m is None else x * jnp.where(at, m, 1.0)

        return face_change(
            c,
            masked(self.j_up(c, cn, 1), m_up, lane5 >= 112),
            masked(self.j_up(c, cn, 2), m_up, lane5 >= 96),
            masked(self.j_dn(c, cp, 1), m_dn, lane5 < 16),
            masked(self.j_dn(c, cp, 2), m_dn, lane5 < 32),
            u,
            masked(self.j_up(u, un, 1), m_up, lane5 >= 112),
            masked(self.j_dn(u, up, 1), m_dn, lane5 < 16),
        )

    def change_i(self, c48, v48, m_dn, m_up):
        up_m1, up_m2 = jnp.where(self.i_top1, m_up, 1.0), jnp.where(self.i_top2, m_up, 1.0)
        dn_m1, dn_m2 = jnp.where(self.i_bot1, m_dn, 1.0), jnp.where(self.i_bot2, m_dn, 1.0)
        wrap = self.wrap
        return face_change(
            wrap(c48), wrap(rs(c48, -1)) * up_m1, wrap(rs(c48, -2)) * up_m2,
            wrap(rs(c48, 1)) * dn_m1, wrap(rs(c48, 2)) * dn_m2,
            wrap(v48), wrap(rs(v48, -1)) * up_m1, wrap(rs(v48, 1)) * dn_m1,
        )


def inner_kernel(ext, ia, ib, coef, c40, u2, src, prs, u1, chg, ka, kb):
    d, tree, gi, gj, gk = where_am_i()
    sh = Shifts()
    rows, pair = make_block(ext, ia, ib, gi, sh.sub)
    dest = {0: c40, 2: u1, 3: u2, 4: src, 5: prs}
    for jq in range(4):
        for kt in range(2):
            jt = jq // 2
            c48 = jnp.concatenate([rows(0, jq, kt, b) for b in range(6)], axis=0)
            v48 = jnp.concatenate(
                [rows(1, jq, kt, b) for b in range(4)] + list(pair(1, jq, kt)), axis=0
            )
            for f, ref in dest.items():
                if f == 0:
                    ref[jq, kt] = sh.wrap(c48)
                else:
                    ref[jq, kt] = jnp.concatenate([rows(f, jq, kt, b) for b in range(5)], axis=0)
            m_dn, m_up = coefficient(coef, 0, jt, kt), coefficient(coef, 1, jt, kt)
            chg[jq, kt] = sh.change_i(c48, v48, m_dn, m_up)
    for jq in (1, 2):
        for kt in range(2):
            m_dn = coefficient(coef, 2, jq // 2, kt) if jq == 2 else None
            m_up = coefficient(coef, 3, jq // 2, kt) if jq == 1 else None
            chg[jq, kt] = chg[jq, kt] + sh.change_j(
                c40[jq, kt], c40[jq + 1, kt], c40[jq - 1, kt],
                u1[jq, kt], u1[jq + 1, kt], u1[jq - 1, kt], m_dn, m_up,
            )
    kinds = (c40, u2, src)
    KPack(gk, sh.lane).block(
        (0, 1), lambda kind, jq, kt, b: kinds[kind][jq, kt, pl.ds(8 * b, 8), :], ka, kb
    )


def outer_kernel(
    ja, jb, peak, x16, coef, c_in, u2_in, src_in, prs_in, u1_in, chg_in, ka_in, kb_in,
    c40, u2, src, prs, chg, ka, kb, peak_out,
):
    d, tree, gi, gj, gk = where_am_i()
    sh = Shifts()
    wide = make_wide(None, ja, jb, gj)
    low5 = sh.lane5 < 64
    for jq in range(4):
        for kt in range(2):
            c40[jq, kt], u2[jq, kt] = c_in[jq, kt], u2_in[jq, kt]
            src[jq, kt], prs[jq, kt] = src_in[jq, kt], prs_in[jq, kt]
            if jq in (1, 2):
                chg[jq, kt] = chg_in[jq, kt]
    for n in range(20):
        ka[n], kb[n] = ka_in[n], kb_in[n]

    def whole(f, jq, kt, count=5):
        return jnp.concatenate([wide(f, jq, kt, b) for b in range(count)], axis=0)

    for kt in range(2):
        for f, ref in ((3, u2), (4, src), (5, prs)):
            ref[4, kt] = jnp.where(low5, whole(f, 4, kt), whole(f, 5, kt))
        c48 = [whole(0, jq, kt, 6) for jq in (4, 5)]
        c_high, c_low = sh.wrap(c48[0]), sh.wrap(c48[1])
        c40[4, kt] = jnp.where(low5, c_high, c_low)
        u_high, u_low = whole(2, 4, kt), whole(2, 5, kt)
        m_dn, m_up = coefficient(coef, 0, 2, kt), coefficient(coef, 1, 2, kt)
        side = []
        for n in range(2):
            v40 = whole(1, 4 + n, kt)
            v48 = jnp.concatenate([v40, v40[32:]], axis=0)
            side.append(sh.change_i(c48[n], v48, m_dn, m_up))
        m_dn, m_up = coefficient(coef, 2, 2, kt), coefficient(coef, 3, 2, kt)
        side[0] = side[0] + sh.change_j(
            c_high, c_low, c_in[3, kt], u_high, u_low, u1_in[3, kt], m_dn, None
        )
        side[1] = side[1] + sh.change_j(
            c_low, c_in[0, kt], c_high, u_low, u1_in[0, kt], u_high, None, m_up
        )
        chg[4, kt] = jnp.where(low5, side[0], side[1])
        chg[0, kt] = chg_in[0, kt] + sh.change_j(
            c_in[0, kt], c_in[1, kt], c_low, u1_in[0, kt], u1_in[1, kt], u_low,
            coefficient(coef, 2, 0, kt), None,
        )
        chg[3, kt] = chg_in[3, kt] + sh.change_j(
            c_in[3, kt], c_high, c_in[2, kt], u1_in[3, kt], u_high, u1_in[2, kt],
            None, coefficient(coef, 3, 1, kt),
        )
    kinds = (c40, u2, src, chg, prs)
    pack = KPack(gk, sh.lane)
    pack.block((3,), lambda kind, jq, kt, b: kinds[kind][jq, kt, pl.ds(8 * b, 8), :], ka, kb)
    pack.halo(lambda kind, kt, b: kinds[kind][4, kt, pl.ds(8 * b, 8), :], ka, kb)
    top = jnp.maximum(
        jnp.maximum(peak[0], x16[0]), jnp.maximum(ja[J_BLOCKS], jb[J_BLOCKS])
    )
    ka[K_BLOCKS] = top
    kb[K_BLOCKS] = top
    peak_out[0] = top


def main_kernel(
    c_in, u_in, s_in, p_in, chg_in, ka, kb, peak, x32, coef,
    out_adv, out_p, send_a, send_b,
    c_k, u2, src, p_k, chg_k, p0, p1, adv, mob, hgt, rhs, wts,
):
    d, tree, gi, gj, gk = where_am_i()
    sh = Shifts()
    sub, lane, lane5, k16 = sh.sub, sh.lane, sh.lane5, sh.k16
    near = lane % 16 < 8
    k_even = gk % 2 == 0
    dest = (c_k, u2, src, chg_k, p_k)

    def both_sides(n):
        a, e = ka[n], kb[n]
        return jnp.where(k_even, a, e), jnp.where(k_even, e, a)

    for kind in (0, 1, 3):
        turn = (0, 5, 0, 4)[kind]
        for b in range(5):
            rows = pl.ds(8 * b, 8)
            for n in range(1 if kind == 0 else 2):
                ref = dest[kind + n]
                for jt in range(2):
                    low, high = both_sides(k_place(kind, jt, b))
                    if n == 1:
                        low, high = rl(low, -turn), rl(high, turn)
                    ref[2 * jt, rows, :] = jnp.where(near, low, rl(high, 8))
                    ref[2 * jt + 1, rows, :] = jnp.where(near, rl(low, -8), high)
                m = (0, 1, 0, 2)[kind] * 5 + b
                low, high = both_sides(30 + m % 8)
                if m < 8:
                    high = rl(high, 8)
                else:
                    low = rl(low, -8)
                if n == 1:
                    low, high = rl(low, -turn), rl(high, turn)
                ref[4, rows, :] = jnp.where(near, low, high)

    def c40(jq, kt):
        return c_k[jq] if kt == 2 else c_in[jq, kt]

    def uk(jq, kt):
        return u2[jq] if kt == 2 else u_in[jq, kt]

    top = jnp.maximum(
        jnp.maximum(peak[0], x32[0]), jnp.maximum(ka[K_BLOCKS], kb[K_BLOCKS])
    )
    top = jnp.max(top, keepdims=True)
    step = jnp.broadcast_to(CFL / top, (8, 128))
    step = jnp.concatenate([step] * 5, axis=0)

    def advance(jq, carry):
        jt = jq >> 1
        for kt in range(3):
            kn, kp = (kt + 1) % 3, (kt + 2) % 3
            change = chg_k[jq] if kt == 2 else chg_in[jq, kt]
            c = c40(jq, kt)
            m_dn, m_up = coefficient(coef, 4, jt, kt), coefficient(coef, 5, jt, kt)
            cn, cp = c40(jq, kn), c40(jq, kp)
            up1, up2 = sh.k_up(c, cn, 1, m_up), sh.k_up(c, cn, 2, m_up)
            dn1, dn2 = sh.k_dn(c, cp, 1, m_dn), sh.k_dn(c, cp, 2, m_dn)
            hgt[jq, kt] = dn2 + dn1 + c + up1 + up2
            u = uk(jq, kt)
            u_up, u_dn = sh.k_up(u, uk(jq, kn), 1, m_up), sh.k_dn(u, uk(jq, kp), 1, m_dn)
            change = change + face_change(c, up1, up2, dn1, dn2, u, u_up, u_dn)
            a = jnp.clip(c - step * coefficient(coef, 12, jt, kt) * change, 0.0, 1.0)
            adv[jq, kt] = a
            mob[jq, kt] = 1.0 / (RHO_GAS + (RHO_LIQ - RHO_GAS) * a)
        return carry

    lax.fori_loop(0, 5, advance, 0)

    def weigh(jq, carry):
        jt = jq >> 1
        jn, jp = lax.rem(jq + 1, 5), lax.rem(jq + 4, 5)
        begins, ends = jq % 2 == 0, (jq % 2 == 1) | (jq == 4)
        for kt in range(3):
            kn, kp = (kt + 1) % 3, (kt + 2) % 3
            mi_dn = jnp.where(sh.i_bot1, coefficient(coef, 0, jt, kt), 1.0)
            mi_up = jnp.where(sh.i_top1, coefficient(coef, 1, jt, kt), 1.0)
            at_dn = (lane5 < 16) & begins
            at_up = (lane5 >= 112) & ends
            mj_dn = jnp.where(at_dn, coefficient(coef, 2, jt, kt), 1.0)
            mj_up = jnp.where(at_up, coefficient(coef, 3, jt, kt), 1.0)
            h = hgt[jq, kt]
            h_up, h_dn = rs(h, -1) * mi_up, rs(h, 1) * mi_dn
            gx, sx = 0.5 * (h_up - h_dn), h_up - 2.0 * h + h_dn
            h_up = sh.j_up(h, hgt[jn, kt], 1) * mj_up
            h_dn = sh.j_dn(h, hgt[jp, kt], 1) * mj_dn
            gy, sy = 0.5 * (h_up - h_dn), h_up - 2.0 * h + h_dn
            gx2, gy2 = gx * gx, gy * gy
            root = lax.rsqrt(1.0 + gx2 + gy2)
            bend = (sx * (1.0 + gy2) + sy * (1.0 + gx2)) * coefficient(coef, 12, jt, kt) * (root * root * root)
            right = (src[jq] if kt == 2 else s_in[jq, kt]) - SIGMA * bend * adv[jq, kt]
            m = mob[jq, kt]
            mk_dn = jnp.where(k16 < 1, coefficient(coef, 4, jt, kt), 1.0)
            mk_up = jnp.where(k16 >= 15, coefficient(coef, 5, jt, kt), 1.0)
            across = (
                rs(m, 1), rs(m, -1),
                sh.j_dn(m, mob[jp, kt], 1), sh.j_up(m, mob[jn, kt], 1),
                sh.k_dn(m, mob[jq, kp], 1), sh.k_up(m, mob[jq, kn], 1),
            )
            masks = (mi_dn, mi_up, mj_dn, mj_up, mk_dn, mk_up)
            edges = (sh.i_bot1, sh.i_top1, at_dn, at_up, k16 < 1, k16 >= 15)
            diag = jnp.zeros_like(m)
            parts = []
            for f in range(6):
                w = (m + masks[f] * across[f]) * jnp.where(edges[f], coefficient(coef, 6 + f, jt, kt), 1.0)
                diag = diag + w
                parts.append(w * masks[f])
            inv = 1.0 / diag
            for f in range(6):
                wts[f, jq, kt] = parts[f] * inv
            rhs[jq, kt] = right * coefficient(coef, 13, jt, kt) * inv
        return carry

    lax.fori_loop(0, 5, weigh, 0)

    for sweep in range(SWEEPS):
        new = p0 if sweep % 2 == 0 else p1
        older = p1 if sweep % 2 == 0 else p0
        last = sweep == SWEEPS - 1

        def old(jq, kt, sweep=sweep, older=older):
            if sweep:
                return older[jq, kt]
            return p_k[jq] if kt == 2 else p_in[jq, kt]

        def relax(jq, carry, old=old, new=new, last=last):
            jn, jp = lax.rem(jq + 1, 5), lax.rem(jq + 4, 5)
            for kt in range(2 if last else 3):
                kn, kp = (kt + 1) % 3, (kt + 2) % 3
                p = old(jq, kt)
                total = wts[0, jq, kt] * rs(p, 1) + wts[1, jq, kt] * rs(p, -1)
                total = total + wts[2, jq, kt] * sh.j_dn(p, old(jp, kt), 1)
                total = total + wts[3, jq, kt] * sh.j_up(p, old(jn, kt), 1)
                total = total + wts[4, jq, kt] * sh.k_dn(p, old(jq, kp), 1)
                total = total + wts[5, jq, kt] * sh.k_up(p, old(jq, kn), 1)
                total = total - rhs[jq, kt]
                if last:
                    out_p[jq, kt] = total[:32]
                    out_adv[jq, kt] = adv[jq, kt][:32]
                else:
                    new[jq, kt] = total
            return carry

        lax.fori_loop(0, 4 if last else 5, relax, 0)

    even = d % 2 == 0
    for h in range(2):
        for n, ref in enumerate((out_adv, out_p)):
            low, high = tile_half(ref, 0, h, tree), tile_half(ref, 7, h, tree)
            send_a[n, :, halves(h)] = jnp.where(even, high, low)
            send_b[n, :, halves(h)] = jnp.where(even, low, high)


def tile_half(ref, t, h, tree):
    row0 = pl.multiple_of(16 * ((t & 1) ^ tree), 16)
    return ref[2 * ((t >> 1) & 1) + h, (t >> 2) & 1, pl.ds(row0, 16), :]


def slots_kernel(adv, prs, bounds, vof, pres):
    d, tree, gi, gj, gk = where_am_i()
    start = bounds[d]
    count = bounds[d + 1] - start
    off = 8 * d - start
    vof[...] = jnp.zeros_like(vof)
    pres[...] = jnp.zeros_like(pres)
    for t in range(8):
        slot = t + off

        @pl.when((slot >= 0) & (slot < count))
        def _(t=t, slot=slot):
            for h in range(2):
                vof[slot, :, halves(h)] = tile_half(adv, t, h, tree)
                pres[slot, :, halves(h)] = tile_half(prs, t, h, tree)


VM = pl.BlockSpec(memory_space=pltpu.VMEM)
SM = pl.BlockSpec(memory_space=pltpu.SMEM)


def shape(*dims):
    return jax.ShapeDtypeStruct(dims, F32)


def blocks(n):
    return shape(n, 8, 128)


def call(kernel, specs, outs, args, scratch=(), micros=1, mib=8):
    return pl.pallas_call(
        kernel,
        out_shape=outs,
        in_specs=specs,
        out_specs=jax.tree.map(lambda _: VM, outs),
        scratch_shapes=list(scratch),
        compiler_params=pltpu.CompilerParams(vmem_limit_bytes=mib * 1024 * 1024),
        cost_estimate=pl.CostEstimate(
            flops=micros * 100000, bytes_accessed=micros * 100000, transcendentals=0
        ),
    )(*args)


def local(volume, velocity, source, pressure_prev, neighbours, levels, refine, bounds_old, bounds_new):
    d = lax.axis_index("row") * 16 + lax.axis_index("col")
    one = blocks(1)
    old = jnp.concatenate([volume[None], velocity, source[None], pressure_prev[None]], axis=0)
    ra, rb, peak = call(
        first_kernel, [VM, SM, SM], (blocks(57), blocks(24), one), (old, levels, bounds_old)
    )
    x8, x9 = send(peak, flip_pairs(8)), send(peak, flip_pairs(9))
    rb, ra = send(rb, ODD_PAIRS), send(ra, EVEN_PAIRS)
    own, mine, flags, ib = call(
        own_kernel,
        [VM, SM],
        (shape(6, 4, 2, 32, 128), blocks(8), blocks(FLAG_COUNT), blocks(32)),
        (old, bounds_old),
    )
    ib, peak = call(
        second_kernel, [VM] * 7, (blocks(32), one), (ib, flags, rb, ra, peak, x8, x9)
    )
    x64 = send(peak, flip_pairs(64))
    ib = send(ib, axis_pairs(0, 1))
    ext, ia = call(
        block_kernel,
        [VM] * 5,
        (shape(6, 4, 2, 32, 128), blocks(32)),
        (own, mine, flags, ra, rb),
    )
    ja, jb, peak = call(
        third_kernel,
        [VM] * 5,
        (blocks(J_BLOCKS + 1), blocks(J_BLOCKS + 1), one),
        (ext, ia, ib, peak, x64),
    )
    x16 = send(peak, flip_pairs(16))
    ja, jb = send(ja, axis_pairs(1, 0)), send(jb, axis_pairs(1, 1))
    coef = call(
        coefficient_kernel,
        [SM] * 3,
        shape(14, 3, 3, 3, 8, 128),
        (neighbours.reshape(-1), levels, refine),
        [pltpu.SMEM((14 * 64,), F32), pltpu.SMEM((7,), F32)],
        5,
    )
    inner = call(
        inner_kernel,
        [VM] * 4,
        (shape(4, 2, 40, 128),) * 6 + (blocks(20),) * 2,
        (ext, ia, ib, coef),
        (),
        2,
    )
    *early, ka, kb, peak = call(
        outer_kernel,
        [VM] * 13,
        (shape(5, 2, 40, 128),) * 5 + (blocks(K_BLOCKS + 1),) * 2 + (one,),
        (ja, jb, peak, x16, coef, *inner),
        (),
        1,
    )
    x32 = send(peak, flip_pairs(32))
    ka, kb = send(ka, axis_pairs(2, 0)), send(kb, axis_pairs(2, 1))
    halo, grid = (5, 40, 128), (5, 3, 40, 128)
    adv, prs, sa, sb = call(
        main_kernel,
        [VM] * 10,
        (shape(4, 2, 32, 128),) * 2 + (shape(2, 16, 256),) * 2,
        (*early, ka, kb, peak, x32, coef),
        [pltpu.VMEM(halo, F32)] * 5
        + [pltpu.VMEM(grid, F32)] * 6
        + [pltpu.VMEM((6, *grid), F32)],
        8,
        16,
    )
    sb, sa = send(sb, ODD_PAIRS), send(sa, EVEN_PAIRS)
    vof, pres = call(slots_kernel, [VM] * 2 + [SM], (shape(10, 16, 256),) * 2, (adv, prs, bounds_new))
    even = d % 2 == 0
    low, high = jnp.where(even, sb, sa), jnp.where(even, sa, sb)
    start, stop = bounds_new[d], bounds_new[d + 1]
    slots = jnp.arange(10, dtype=jnp.int32)
    at_low = ((slots == 0) & (start == 8 * d - 1))[:, None, None]
    at_high = ((slots == 8 * d + 8 - start) & (stop == 8 * d + 9))[:, None, None]
    outs = [
        jnp.where(at_low, low[n][None], jnp.where(at_high, high[n][None], x))
        for n, x in enumerate((vof, pres))
    ]
    return tuple(outs)


def solution(mesh):
    in_specs = (
        P(AXES, None, None),
        P(None, AXES, None, None),
        P(AXES, None, None),
        P(AXES, None, None),
        P(),
        P(),
        P(),
        P(),
        P(),
    )
    out_specs = (P(AXES, None, None), P(AXES, None, None))
    return jax.shard_map(local, mesh=mesh, in_specs=in_specs, out_specs=out_specs, check_vma=False)
```

```python
import jax
import jax.numpy as jnp
from jax import lax
from jax.experimental import pallas as pl
from jax.experimental.pallas import tpu as pltpu
from jax.sharding import PartitionSpec as P

SWEEPS = 4
CFL = 0.4
SIGMA = 0.05
RHO_GAS = 0.05
RHO_LIQ = 1.0
AXES = ("row", "col")
DEVS = 128
F32 = jnp.float32


def block_coords(d):
    tree, low = d >> 6, d & 63
    i = (low & 1) | (((low >> 3) & 1) << 1)
    j = ((low >> 1) & 1) | (((low >> 4) & 1) << 1)
    k = ((low >> 2) & 1) | (((low >> 5) & 1) << 1)
    return (7 - i if tree else i), j, k


PLACE = {block_coords(d): d for d in range(DEVS)}


def axis_pairs(axis, odd):
    count = (8, 4, 4)[axis]
    pairs = []
    for d in range(DEVS):
        c = list(block_coords(d))
        step = 1 if (c[axis] % 2 == 0) != bool(odd) else -1
        c[axis] = (c[axis] + step) % count
        pairs.append((d, PLACE[tuple(c)]))
    return pairs


def flip_pairs(bits):
    return [(d, d ^ bits) for d in range(DEVS)]


EVEN_PAIRS = flip_pairs(1)
ODD_PAIRS = [(d, d + 1 if d % 2 else d - 1) for d in range(1, DEVS - 1)]


def send(x, pairs):
    return lax.ppermute(x, AXES, pairs)


def where_is(d):
    tree = d >> 6
    i = (d & 1) | (((d >> 3) & 1) << 1)
    gi = jnp.where(tree == 1, 7 - i, i)
    gj = ((d >> 1) & 1) | (((d >> 4) & 1) << 1)
    gk = ((d >> 2) & 1) | (((d >> 5) & 1) << 1)
    return tree, gi, gj, gk


def where_am_i():
    d = lax.axis_index("row") * 16 + lax.axis_index("col")
    return d, *where_is(d)


def iotas():
    sub = lax.broadcasted_iota(jnp.int32, (8, 128), 0)
    lane = lax.broadcasted_iota(jnp.int32, (8, 128), 1)
    return sub, lane


def rl(x, shift):
    return pltpu.roll(x, shift % 128, 1)


def rs(x, shift):
    n = x.shape[0]
    return pltpu.roll(x, shift % n, 0)


def halves(h):
    return pl.ds(128 * h, 128)


def old_slice(old, f, slot, start, h):
    return old[f, slot, pl.ds(pl.multiple_of(start, 8), 8), halves(h)]


def slab_groups(get, high, sub):
    nat = (sub >= 4) == high
    return (
        get(0),
        get(1),
        jnp.where(nat, get(2), rs(get(3), 4)),
        jnp.where(nat, get(5), rs(get(4), 4)),
    )


def first_kernel(old, levels, bounds, ra, rb, peak):
    d, tree, gi, gj, gk = where_am_i()
    sub, lane = iotas()
    start = bounds[d]
    count = bounds[d + 1] - start
    off = 8 * d - start
    even = d % 2 == 0
    slot_a = jnp.where(even, 8 + off, 0)
    slot_b = jnp.where(even, 0, 8 + off)
    for f in range(6):
        for r in range(2):
            for h in range(2):
                ra[f * 4 + r * 2 + h] = old_slice(old, f, slot_a, 8 * r, h)
                rb[f * 4 + r * 2 + h] = old_slice(old, f, slot_b, 8 * r, h)
    high = gi % 2 == 0
    row0 = jnp.where(high, 8, 0)
    bit = jnp.where(even, 1, 0)
    for q in range(4):
        for h in range(2):
            slot = jnp.clip(bit + 2 * q + off, 0, 9)
            groups = slab_groups(lambda f: old_slice(old, f, slot, row0, h), high, sub)
            for g in range(4):
                ra[24 + (g * 4 + q) * 2 + h] = groups[g]
    top = jnp.zeros((8, 128), F32)
    for s in range(10):
        level = levels[jnp.minimum(start + s, 1023)]
        inv = jnp.where(s < count, jnp.left_shift(1, level), 0).astype(F32)
        part = jnp.zeros((8, 128), F32)
        for r in range(2):
            for h in range(2):
                u = [jnp.abs(old[1 + a, s, pl.ds(8 * r, 8), halves(h)]) for a in range(3)]
                part = jnp.maximum(part, u[0] + u[1] + u[2])
        top = jnp.maximum(top, part * inv)
    ra[56] = top
    peak[0] = top


FLAG_COUNT = 6


def own_kernel(old, bounds, ext, mine, flags, ib):
    d, tree, gi, gj, gk = where_am_i()
    sub, lane = iotas()
    off = 8 * d - bounds[d]
    even = d % 2 == 0
    for t in range(8):
        slot = jnp.clip(t + off, 0, 9)
        bj, bk = (t >> 1) & 1, (t >> 2) & 1
        row0 = 16 * ((t & 1) ^ tree)
        for f in range(6):
            for r in range(2):
                for h in range(2):
                    rows = pl.ds(pl.multiple_of(row0 + 8 * r, 8), 8)
                    ext[f, 2 * bj + h, bk, rows, :] = old_slice(old, f, slot, 8 * r, h)
    high = gi % 2 == 1
    row0 = jnp.where(high, 8, 0)
    slot_a = jnp.where(even, 8 + off, 0)
    bit = jnp.where(even, 0, 1)
    for h in range(2):
        groups = slab_groups(lambda f: old_slice(old, f, slot_a, row0, h), high, sub)
        for g in range(4):
            mine[g * 2 + h] = groups[g]
        for q in range(4):
            slot = jnp.clip(bit + 2 * q + off, 0, 9)
            groups = slab_groups(lambda f: old_slice(old, f, slot, row0, h), high, sub)
            for g in range(4):
                ib[(g * 4 + q) * 2 + h] = groups[g]
    odd = jnp.logical_not(even)
    first, last = bounds[d] == 8 * d + 1, bounds[d + 1] == 8 * d + 7
    values = (
        first,
        last,
        even & (bounds[d + 1] == 8 * d + 9),
        odd & (bounds[d] == 8 * d - 1),
        even & first,
        odd & last,
    )
    for n, value in enumerate(values):
        flags[n] = jnp.full((8, 128), jnp.where(value, 1.0, 0.0), F32)


def second_kernel(ib_in, flags, rb, ra, peak, x8, x9, coef, ib, peak_out):
    d, tree, gi, gj, gk = where_am_i()
    sub, lane = iotas()
    high = gi % 2 == 1
    block = jnp.where(high, 2, 0)
    for q in range(4):
        for h in range(2):
            if q in (0, 3):
                groups = slab_groups(lambda f: rb[f * 4 + block + h], high, sub)
                flag = flags[4 if q == 0 else 5] > 0.5
            for g in range(4):
                n = (g * 4 + q) * 2 + h
                ib[n] = jnp.where(flag, groups[g], ib_in[n]) if q in (0, 3) else ib_in[n]
    peak_out[0] = jnp.maximum(jnp.maximum(peak[0], ra[56]), jnp.maximum(x8[0], x9[0]))


def block_kernel(own, mine, flags, ra, rb, ext, ia):
    d, tree, gi, gj, gk = where_am_i()
    even = d % 2 == 0
    flag = [flags[n] > 0.5 for n in range(4)]
    ext[...] = own[...]
    for t, missing in ((0, flag[0]), (7, flag[1])):
        bj, bk = (t >> 1) & 1, (t >> 2) & 1
        row0 = 16 * ((t & 1) ^ tree)
        use_b = even if t == 0 else jnp.logical_not(even)
        for f in range(6):
            for r in range(2):
                for h in range(2):
                    n = f * 4 + r * 2 + h
                    rows = pl.ds(pl.multiple_of(row0 + 8 * r, 8), 8)
                    came = jnp.where(use_b, rb[n], ra[n])
                    ext[f, 2 * bj + h, bk, rows, :] = jnp.where(
                        missing, came, own[f, 2 * bj + h, bk, rows, :]
                    )
    for q in range(4):
        for h in range(2):
            for g in range(4):
                n = (g * 4 + q) * 2 + h
                x = ra[24 + n]
                if q == 0:
                    x = jnp.where(flag[2], mine[g * 2 + h], x)
                if q == 3:
                    x = jnp.where(flag[3], mine[g * 2 + h], x)
                ia[n] = x


def make_block(ext, ia, ib, gi, sub):
    first_high = gi % 2 == 0

    def pair(g, jq, kt):
        n = (g * 4 + jq // 2 + 2 * kt) * 2 + jq % 2
        a, b = ia[n], ib[n]
        return jnp.where(first_high, a, b), jnp.where(first_high, b, a)

    def rows(f, jq, kt, b):
        if b < 4:
            return ext[f, jq, kt, pl.ds(8 * b, 8), :]
        if f == 0:
            return pair(0, jq, kt)[b - 4]
        hi, lo = pair((1, 1, 2, 2, 3, 3)[f], jq, kt)
        if f in (3, 4):
            return rs(jnp.where(sub < 4, lo, hi), 4)
        return jnp.where(sub < 4, hi, lo)

    return rows, pair


J_BLOCKS = 37


def j_place(f, kt, b):
    if f == 0:
        return kt * 6 + b
    if f == 5:
        return 32 + b
    return (12 if f in (2, 4) else 22) + kt * 5 + b


def third_kernel(ext, ia, ib, peak, x64, ja, jb, peak_out):
    d, tree, gi, gj, gk = where_am_i()
    sub, lane = iotas()
    rows, _ = make_block(ext, ia, ib, gi, sub)
    even = gj % 2 == 0

    def put(f, kt, b, get):
        lo, hi = get(0), get(3)
        ja[j_place(f, kt, b)] = jnp.where(even, hi, lo)
        jb[j_place(f, kt, b)] = jnp.where(even, lo, hi)

    for b in range(6):
        for kt in range(2):
            put(0, kt, b, lambda jq: rows(0, jq, kt, b))
    for b in range(5):
        for kt in range(2):
            def five(jq):
                nat = lane < 80 if jq == 0 else lane >= 48
                turn = 80 if jq == 0 else -80
                return jnp.where(nat, rows(2, jq, kt, b), rl(rows(4, jq, kt, b), turn))

            def four(jq):
                nat = lane < 64 if jq == 0 else lane >= 64
                return jnp.where(nat, rows(1, jq, kt, b), rl(rows(3, jq, kt, b), 64))

            put(2, kt, b, five)
            put(1, kt, b, four)

        def both(jq):
            nat = lane < 64 if jq == 0 else lane >= 64
            return jnp.where(nat, rows(5, jq, 0, b), rl(rows(5, jq, 1, b), 64))

        put(5, 0, b, both)
    top = jnp.maximum(peak[0], x64[0])
    ja[J_BLOCKS] = top
    jb[J_BLOCKS] = top
    peak_out[0] = top


def make_wide(rows, ja, jb, gj):
    first_high = gj % 2 == 0

    def wide(f, jq, kt, b):
        if jq < 4:
            return rows(f, jq, kt, b)
        n = j_place(f, kt, b)
        if jq == 4:
            x = jnp.where(first_high, ja[n], jb[n])
        else:
            x = jnp.where(first_high, jb[n], ja[n])
        if f == 4:
            return rl(x, -80 if jq == 4 else 80)
        return rl(x, 64) if f == 3 or (f == 5 and kt == 1) else x

    return wide


K_BLOCKS = 38


def k_place(kind, jt, b):
    if jt == 2:
        return 30 + b
    return (0, 10, 10, 20, 20)[kind] + jt * 5 + b


class KPack:
    def __init__(self, gk, lane):
        self.even = gk % 2 == 0
        self.near = lane % 16 < 8
        self.k8 = lane % 8

    def put(self, ka, kb, n, lo, hi):
        ka[n] = jnp.where(self.even, hi, lo)
        kb[n] = jnp.where(self.even, lo, hi)

    def squeeze(self, first, last, kt):
        if kt == 0:
            return jnp.where(self.near, first, rl(last, 8))
        return jnp.where(self.near, rl(first, -8), last)

    def join(self, kind, value, kt):
        if kind == 0:
            return value(0)
        if kind == 1:
            nat, turn = (self.k8 < 5, 5) if kt == 0 else (self.k8 >= 3, -5)
        else:
            nat, turn = (self.k8 < 4, 4) if kt == 0 else (self.k8 >= 4, -4)
        return jnp.where(nat, value(kind), rl(value(kind + 1), turn))

    def block(self, kinds, get, ka, kb):
        for jt in range(2):
            for kind in kinds:
                for b in range(5):
                    sides = []
                    for kt in range(2):

                        def value(n):
                            one, two = get(n, 2 * jt, kt, b), get(n, 2 * jt + 1, kt, b)
                            return self.squeeze(one, two, kt)

                        sides.append(self.join(kind, value, kt))
                    self.put(ka, kb, k_place(kind, jt, b), *sides)

    def halo(self, get, ka, kb):
        for n in range(8):
            sides = []
            for kt in range(2):
                packs = []
                for m in (n, min(n + 8, 14)):
                    kind, b = (0, 1, 3)[m // 5], m % 5
                    packs.append(self.join(kind, lambda f: get(f, kt, b), kt))
                sides.append(self.squeeze(*packs, kt))
            self.put(ka, kb, 30 + n, *sides)


def coefficient_kernel(neighbours, levels, refine, out, table):
    d, tree, gi, gj, gk = where_am_i()
    sub, lane = iotas()

    def one(pos, carry):
        ip, jp, kp = pos >> 4, (pos >> 2) & 3, pos & 3
        x = 2 * gi + jnp.where(ip == 3, -1, ip)
        y = 2 * gj + jnp.where(jp == 3, -1, jp)
        z = 2 * gk + jnp.where(kp == 3, -1, kp)
        inside = (x >= 0) & (x < 16) & (y >= 0) & (y < 8) & (z >= 0) & (z < 8)
        upper = x >= 8
        lx = jnp.where(upper, 15 - x, x)
        code = jnp.where(upper, 512, 0)
        for bit in range(3):
            for axis, v in enumerate((lx, y, z)):
                code = code | (((v >> bit) & 1) << (3 * bit + axis))
        code = jnp.where(inside, code, 0)
        level = levels[code]
        depth = level + refine[code]
        for axis in range(3):
            opened = inside & (neighbours[code * 6 + 2 * axis + 1] >= 0)
            table[axis * 64 + pos] = jnp.where(opened, 1.0, 0.0)
        table[3 * 64 + pos] = jnp.left_shift(1, level).astype(F32)
        table[4 * 64 + pos] = jnp.left_shift(1, 3 - depth).astype(F32)
        return carry

    lax.fori_loop(0, 64, one, 0, unroll=4)
    turns = {0: (0, 1, 2, 3), -1: (3, 0, 1, 3), 1: (1, 2, 2, 0)}

    def spread(item, axis=0, step=0):
        maps = [turns[step if a == axis else 0] for a in range(3)]
        made = []
        for jp in range(4):
            vals = []
            for ip in range(4):
                n = item * 64 + maps[0][ip] * 16 + maps[1][jp] * 4
                v = [jnp.full((8, 128), table[n + maps[2][kp]], F32) for kp in range(4)]
                vals.append((v[0], v[1], jnp.where(lane % 16 < 8, v[2], v[3])))
            made.append(
                [
                    (vals[0][kt], vals[1][kt], jnp.where(sub < 4, vals[2][kt], vals[3][kt]))
                    for kt in range(3)
                ]
            )
        last = [
            [jnp.where(lane < 64, made[2][kt][n], made[3][kt][n]) for n in range(3)]
            for kt in range(3)
        ]
        return made[0], made[1], last

    places = [(jt, kt, n) for jt in range(3) for kt in range(3) for n in range(3)]
    size, inverse = spread(4), spread(3)
    for jt, kt, n in places:
        e = size[jt][kt][n]
        out[12, jt, kt, n] = inverse[jt][kt][n]
        out[13, jt, kt, n] = e * e * (1.0 / 32.0)
    for axis in range(3):
        for side, step in ((0, -1), (1, 1)):
            opened = spread(axis, axis, -1) if side == 0 else spread(axis)
            other = spread(4, axis, step)
            for jt, kt, n in places:
                e, m = size[jt][kt][n], opened[jt][kt][n]
                ratio = (2.0 * e) / (e + other[jt][kt][n])
                out[2 * axis + side, jt, kt, n] = m
                out[6 + 2 * axis + side, jt, kt, n] = jnp.where(m > 0.5, ratio, 1.0)


def coefficient(coef, item, jt, kt):
    a, b, c = (coef[item, jt, kt, n] for n in range(3))
    return jnp.concatenate([a, a, b, b, c], axis=0)


def minmod(a, b):
    return jnp.maximum(jnp.minimum(a, b), 0.0) + jnp.minimum(jnp.maximum(a, b), 0.0)


def face_change(c, up1, up2, dn1, dn2, u, u_up, u_dn):
    upper, lower = up1 - c, c - dn1
    half = 0.5 * minmod(upper, lower)
    half_up = 0.5 * minmod(up2 - up1, upper)
    half_dn = 0.5 * minmod(lower, dn1 - dn2)
    w_up, w_dn = 0.5 * (u + u_up), 0.5 * (u_dn + u)
    flux_up = jnp.maximum(w_up, 0.0) * (c + half) + jnp.minimum(w_up, 0.0) * (up1 - half_up)
    flux_dn = jnp.maximum(w_dn, 0.0) * (dn1 + half_dn) + jnp.minimum(w_dn, 0.0) * (c - half)
    return flux_up - flux_dn


def wrap48(x, sub):
    return jnp.concatenate([x[:32], jnp.where(sub < 4, x[32:40], x[40:48])], axis=0)


class Shifts:
    def __init__(self):
        self.sub, self.lane = iotas()
        self.row = lax.broadcasted_iota(jnp.int32, (40, 128), 0)
        self.lane5 = lax.broadcasted_iota(jnp.int32, (40, 128), 1)
        self.k16 = self.lane5 % 16
        row = self.row
        self.i_top1 = (row == 15) | (row == 31) | (row == 39)
        self.i_top2 = self.i_top1 | (row == 14) | (row == 30) | (row == 38)
        self.i_bot1 = (row == 0) | (row == 16) | (row == 32)
        self.i_bot2 = self.i_bot1 | (row == 1) | (row == 17) | (row == 33)

    def wrap(self, x):
        return wrap48(x, self.sub)

    def k_up(self, x, nxt, n, m=None):
        nxt = rl(nxt, 16 - n)
        return jnp.where(self.k16 < 16 - n, rl(x, -n), nxt if m is None else m * nxt)

    def k_dn(self, x, prv, n, m=None):
        prv = rl(prv, n - 16)
        return jnp.where(self.k16 >= n, rl(x, n), prv if m is None else m * prv)

    def j_up(self, x, nxt, n):
        return rl(jnp.where(self.lane5 < 16 * n, nxt, x), -16 * n)

    def j_dn(self, x, prv, n):
        return rl(jnp.where(self.lane5 >= 128 - 16 * n, prv, x), 16 * n)

    def change_j(self, c, cn, cp, u, un, up, m_dn, m_up):
        lane5 = self.lane5

        def masked(x, m, at):
            return x if m is None else x * jnp.where(at, m, 1.0)

        return face_change(
            c,
            masked(self.j_up(c, cn, 1), m_up, lane5 >= 112),
            masked(self.j_up(c, cn, 2), m_up, lane5 >= 96),
            masked(self.j_dn(c, cp, 1), m_dn, lane5 < 16),
            masked(self.j_dn(c, cp, 2), m_dn, lane5 < 32),
            u,
            masked(self.j_up(u, un, 1), m_up, lane5 >= 112),
            masked(self.j_dn(u, up, 1), m_dn, lane5 < 16),
        )

    def change_i(self, c48, v48, m_dn, m_up):
        up_m1, up_m2 = jnp.where(self.i_top1, m_up, 1.0), jnp.where(self.i_top2, m_up, 1.0)
        dn_m1, dn_m2 = jnp.where(self.i_bot1, m_dn, 1.0), jnp.where(self.i_bot2, m_dn, 1.0)
        wrap = self.wrap
        return face_change(
            wrap(c48), wrap(rs(c48, -1)) * up_m1, wrap(rs(c48, -2)) * up_m2,
            wrap(rs(c48, 1)) * dn_m1, wrap(rs(c48, 2)) * dn_m2,
            wrap(v48), wrap(rs(v48, -1)) * up_m1, wrap(rs(v48, 1)) * dn_m1,
        )


def inner_kernel(ext, ia, ib, coef, c40, u2, src, prs, u1, chg, ka, kb):
    d, tree, gi, gj, gk = where_am_i()
    sh = Shifts()
    rows, pair = make_block(ext, ia, ib, gi, sh.sub)
    dest = {0: c40, 2: u1, 3: u2, 4: src, 5: prs}
    for jq in range(4):
        for kt in range(2):
            jt = jq // 2
            c48 = jnp.concatenate([rows(0, jq, kt, b) for b in range(6)], axis=0)
            v48 = jnp.concatenate(
                [rows(1, jq, kt, b) for b in range(4)] + list(pair(1, jq, kt)), axis=0
            )
            for f, ref in dest.items():
                if f == 0:
                    ref[jq, kt] = sh.wrap(c48)
                else:
                    ref[jq, kt] = jnp.concatenate([rows(f, jq, kt, b) for b in range(5)], axis=0)
            m_dn, m_up = coefficient(coef, 0, jt, kt), coefficient(coef, 1, jt, kt)
            chg[jq, kt] = sh.change_i(c48, v48, m_dn, m_up)
    for jq in (1, 2):
        for kt in range(2):
            m_dn = coefficient(coef, 2, jq // 2, kt) if jq == 2 else None
            m_up = coefficient(coef, 3, jq // 2, kt) if jq == 1 else None
            chg[jq, kt] = chg[jq, kt] + sh.change_j(
                c40[jq, kt], c40[jq + 1, kt], c40[jq - 1, kt],
                u1[jq, kt], u1[jq + 1, kt], u1[jq - 1, kt], m_dn, m_up,
            )
    kinds = (c40, u2, src)
    KPack(gk, sh.lane).block(
        (0, 1), lambda kind, jq, kt, b: kinds[kind][jq, kt, pl.ds(8 * b, 8), :], ka, kb
    )


def outer_kernel(
    ja, jb, peak, x16, coef, c_in, u2_in, src_in, prs_in, u1_in, chg_in, ka_in, kb_in,
    c40, u2, src, prs, chg, ka, kb, peak_out,
):
    d, tree, gi, gj, gk = where_am_i()
    sh = Shifts()
    wide = make_wide(None, ja, jb, gj)
    low5 = sh.lane5 < 64
    for jq in range(4):
        for kt in range(2):
            c40[jq, kt], u2[jq, kt] = c_in[jq, kt], u2_in[jq, kt]
            src[jq, kt], prs[jq, kt] = src_in[jq, kt], prs_in[jq, kt]
            if jq in (1, 2):
                chg[jq, kt] = chg_in[jq, kt]
    for n in range(20):
        ka[n], kb[n] = ka_in[n], kb_in[n]

    def whole(f, jq, kt, count=5):
        return jnp.concatenate([wide(f, jq, kt, b) for b in range(count)], axis=0)

    for kt in range(2):
        for f, ref in ((3, u2), (4, src), (5, prs)):
            ref[4, kt] = jnp.where(low5, whole(f, 4, kt), whole(f, 5, kt))
        c48 = [whole(0, jq, kt, 6) for jq in (4, 5)]
        c_high, c_low = sh.wrap(c48[0]), sh.wrap(c48[1])
        c40[4, kt] = jnp.where(low5, c_high, c_low)
        u_high, u_low = whole(2, 4, kt), whole(2, 5, kt)
        m_dn, m_up = coefficient(coef, 0, 2, kt), coefficient(coef, 1, 2, kt)
        side = []
        for n in range(2):
            v40 = whole(1, 4 + n, kt)
            v48 = jnp.concatenate([v40, v40[32:]], axis=0)
            side.append(sh.change_i(c48[n], v48, m_dn, m_up))
        m_dn, m_up = coefficient(coef, 2, 2, kt), coefficient(coef, 3, 2, kt)
        side[0] = side[0] + sh.change_j(
            c_high, c_low, c_in[3, kt], u_high, u_low, u1_in[3, kt], m_dn, None
        )
        side[1] = side[1] + sh.change_j(
            c_low, c_in[0, kt], c_high, u_low, u1_in[0, kt], u_high, None, m_up
        )
        chg[4, kt] = jnp.where(low5, side[0], side[1])
        chg[0, kt] = chg_in[0, kt] + sh.change_j(
            c_in[0, kt], c_in[1, kt], c_low, u1_in[0, kt], u1_in[1, kt], u_low,
            coefficient(coef, 2, 0, kt), None,
        )
        chg[3, kt] = chg_in[3, kt] + sh.change_j(
            c_in[3, kt], c_high, c_in[2, kt], u1_in[3, kt], u_high, u1_in[2, kt],
            None, coefficient(coef, 3, 1, kt),
        )
    kinds = (c40, u2, src, chg, prs)
    pack = KPack(gk, sh.lane)
    pack.block((3,), lambda kind, jq, kt, b: kinds[kind][jq, kt, pl.ds(8 * b, 8), :], ka, kb)
    pack.halo(lambda kind, kt, b: kinds[kind][4, kt, pl.ds(8 * b, 8), :], ka, kb)
    top = jnp.maximum(
        jnp.maximum(peak[0], x16[0]), jnp.maximum(ja[J_BLOCKS], jb[J_BLOCKS])
    )
    ka[K_BLOCKS] = top
    kb[K_BLOCKS] = top
    peak_out[0] = top


def main_kernel(
    c_in, u_in, s_in, p_in, chg_in, ka, kb, peak, x32, coef,
    out_adv, out_p, send_a, send_b,
    c_k, u2, src, p_k, chg_k, p0, p1, adv, mob, hgt, rhs, wts,
):
    d, tree, gi, gj, gk = where_am_i()
    sh = Shifts()
    sub, lane, lane5, k16 = sh.sub, sh.lane, sh.lane5, sh.k16
    near = lane % 16 < 8
    k_even = gk % 2 == 0
    dest = (c_k, u2, src, chg_k, p_k)

    def both_sides(n):
        a, e = ka[n], kb[n]
        return jnp.where(k_even, a, e), jnp.where(k_even, e, a)

    for kind in (0, 1, 3):
        turn = (0, 5, 0, 4)[kind]
        for b in range(5):
            rows = pl.ds(8 * b, 8)
            for n in range(1 if kind == 0 else 2):
                ref = dest[kind + n]
                for jt in range(2):
                    low, high = both_sides(k_place(kind, jt, b))
                    if n == 1:
                        low, high = rl(low, -turn), rl(high, turn)
                    ref[2 * jt, rows, :] = jnp.where(near, low, rl(high, 8))
                    ref[2 * jt + 1, rows, :] = jnp.where(near, rl(low, -8), high)
                m = (0, 1, 0, 2)[kind] * 5 + b
                low, high = both_sides(30 + m % 8)
                if m < 8:
                    high = rl(high, 8)
                else:
                    low = rl(low, -8)
                if n == 1:
                    low, high = rl(low, -turn), rl(high, turn)
                ref[4, rows, :] = jnp.where(near, low, high)

    def c40(jq, kt):
        return c_k[jq] if kt == 2 else c_in[jq, kt]

    def uk(jq, kt):
        return u2[jq] if kt == 2 else u_in[jq, kt]

    top = jnp.maximum(
        jnp.maximum(peak[0], x32[0]), jnp.maximum(ka[K_BLOCKS], kb[K_BLOCKS])
    )
    top = jnp.max(top, keepdims=True)
    step = jnp.broadcast_to(CFL / top, (8, 128))
    step = jnp.concatenate([step] * 5, axis=0)

    for jq in range(5):
        jt = jq // 2
        for kt in range(3):
            kn, kp = (kt + 1) % 3, (kt + 2) % 3
            change = chg_k[jq] if kt == 2 else chg_in[jq, kt]
            c = c40(jq, kt)
            m_dn, m_up = coefficient(coef, 4, jt, kt), coefficient(coef, 5, jt, kt)
            cn, cp = c40(jq, kn), c40(jq, kp)
            up1, up2 = sh.k_up(c, cn, 1, m_up), sh.k_up(c, cn, 2, m_up)
            dn1, dn2 = sh.k_dn(c, cp, 1, m_dn), sh.k_dn(c, cp, 2, m_dn)
            hgt[jq, kt] = dn2 + dn1 + c + up1 + up2
            u = uk(jq, kt)
            u_up, u_dn = sh.k_up(u, uk(jq, kn), 1, m_up), sh.k_dn(u, uk(jq, kp), 1, m_dn)
            change = change + face_change(c, up1, up2, dn1, dn2, u, u_up, u_dn)
            a = jnp.clip(c - step * coefficient(coef, 12, jt, kt) * change, 0.0, 1.0)
            adv[jq, kt] = a
            mob[jq, kt] = 1.0 / (RHO_GAS + (RHO_LIQ - RHO_GAS) * a)

    k_bot, k_top, j_bot, j_top = k16 < 1, k16 >= 15, lane5 < 16, lane5 >= 112
    for jq in range(5):
        jt, jn, jp = jq // 2, (jq + 1) % 5, (jq + 4) % 5
        edges = (
            sh.i_bot1, sh.i_top1,
            j_bot if jq % 2 == 0 else None, j_top if jq in (1, 3, 4) else None,
            k_bot, k_top,
        )
        for kt in range(3):
            kn, kp = (kt + 1) % 3, (kt + 2) % 3
            opened = [None if e is None else coefficient(coef, f, jt, kt) for f, e in enumerate(edges)]

            def masked(x, f):
                return x if edges[f] is None else x * jnp.where(edges[f], opened[f], 1.0)

            h = hgt[jq, kt]
            h_up, h_dn = masked(rs(h, -1), 1), masked(rs(h, 1), 0)
            gx, sx = 0.5 * (h_up - h_dn), h_up - 2.0 * h + h_dn
            h_up = masked(sh.j_up(h, hgt[jn, kt], 1), 3)
            h_dn = masked(sh.j_dn(h, hgt[jp, kt], 1), 2)
            gy, sy = 0.5 * (h_up - h_dn), h_up - 2.0 * h + h_dn
            gx2, gy2 = gx * gx, gy * gy
            root = lax.rsqrt(1.0 + gx2 + gy2)
            bend = (sx * (1.0 + gy2) + sy * (1.0 + gx2)) * coefficient(coef, 12, jt, kt)
            bend = bend * (root * root * root)
            right = (src[jq] if kt == 2 else s_in[jq, kt]) - SIGMA * bend * adv[jq, kt]
            m = mob[jq, kt]
            across = (
                rs(m, 1), rs(m, -1),
                sh.j_dn(m, mob[jp, kt], 1), sh.j_up(m, mob[jn, kt], 1),
                sh.k_dn(m, mob[jq, kp], 1), sh.k_up(m, mob[jq, kn], 1),
            )
            closed = jnp.zeros_like(m)
            diag = jnp.zeros_like(m)
            parts = []
            for f in range(6):
                part = m + across[f]
                if edges[f] is not None:
                    ratio = coefficient(coef, 6 + f, jt, kt)
                    part = part * jnp.where(edges[f], ratio * opened[f], 1.0)
                    closed = closed + jnp.where(edges[f], 1.0 - opened[f], 0.0)
                diag = diag + part
                parts.append(part)
            inv = 1.0 / (diag + closed * m)
            for f in range(6):
                wts[f, jq, kt] = parts[f] * inv
            rhs[jq, kt] = right * coefficient(coef, 13, jt, kt) * inv

    for sweep in range(SWEEPS):
        new = p0 if sweep % 2 == 0 else p1
        older = p1 if sweep % 2 == 0 else p0
        last = sweep == SWEEPS - 1

        def old(jq, kt):
            if sweep:
                return older[jq, kt]
            return p_k[jq] if kt == 2 else p_in[jq, kt]

        for jq in range(4 if last else 5):
            jn, jp = (jq + 1) % 5, (jq + 4) % 5
            for kt in range(2 if last else 3):
                kn, kp = (kt + 1) % 3, (kt + 2) % 3
                p = old(jq, kt)
                total = wts[0, jq, kt] * rs(p, 1) + wts[1, jq, kt] * rs(p, -1)
                total = total + wts[2, jq, kt] * sh.j_dn(p, old(jp, kt), 1)
                total = total + wts[3, jq, kt] * sh.j_up(p, old(jn, kt), 1)
                total = total + wts[4, jq, kt] * sh.k_dn(p, old(jq, kp), 1)
                total = total + wts[5, jq, kt] * sh.k_up(p, old(jq, kn), 1)
                total = total - rhs[jq, kt]
                if last:
                    out_p[jq, kt] = total[:32]
                    out_adv[jq, kt] = adv[jq, kt][:32]
                else:
                    new[jq, kt] = total

    even = d % 2 == 0
    for h in range(2):
        for n, ref in enumerate((out_adv, out_p)):
            low, high = tile_half(ref, 0, h, tree), tile_half(ref, 7, h, tree)
            send_a[n, :, halves(h)] = jnp.where(even, high, low)
            send_b[n, :, halves(h)] = jnp.where(even, low, high)


def tile_half(ref, t, h, tree):
    row0 = pl.multiple_of(16 * ((t & 1) ^ tree), 16)
    return ref[2 * ((t >> 1) & 1) + h, (t >> 2) & 1, pl.ds(row0, 16), :]


def slots_kernel(adv, prs, bounds, vof, pres):
    d, tree, gi, gj, gk = where_am_i()
    start = bounds[d]
    count = bounds[d + 1] - start
    off = 8 * d - start
    vof[...] = jnp.zeros_like(vof)
    pres[...] = jnp.zeros_like(pres)
    for t in range(8):
        slot = t + off

        @pl.when((slot >= 0) & (slot < count))
        def _(t=t, slot=slot):
            for h in range(2):
                vof[slot, :, halves(h)] = tile_half(adv, t, h, tree)
                pres[slot, :, halves(h)] = tile_half(prs, t, h, tree)


VM = pl.BlockSpec(memory_space=pltpu.VMEM)
SM = pl.BlockSpec(memory_space=pltpu.SMEM)


def shape(*dims):
    return jax.ShapeDtypeStruct(dims, F32)


def blocks(n):
    return shape(n, 8, 128)


def call(kernel, specs, outs, args, scratch=(), micros=1, mib=8):
    return pl.pallas_call(
        kernel,
        out_shape=outs,
        in_specs=specs,
        out_specs=jax.tree.map(lambda _: VM, outs),
        scratch_shapes=list(scratch),
        compiler_params=pltpu.CompilerParams(vmem_limit_bytes=mib * 1024 * 1024),
        cost_estimate=pl.CostEstimate(
            flops=micros * 100000, bytes_accessed=micros * 100000, transcendentals=0
        ),
    )(*args)


def local(volume, velocity, source, pressure_prev, neighbours, levels, refine, bounds_old, bounds_new):
    d = lax.axis_index("row") * 16 + lax.axis_index("col")
    one = blocks(1)
    old = jnp.concatenate([volume[None], velocity, source[None], pressure_prev[None]], axis=0)
    ra, rb, peak = call(
        first_kernel, [VM, SM, SM], (blocks(57), blocks(24), one), (old, levels, bounds_old)
    )
    x8, x9 = send(peak, flip_pairs(8)), send(peak, flip_pairs(9))
    rb, ra = send(rb, ODD_PAIRS), send(ra, EVEN_PAIRS)
    own, mine, flags, ib = call(
        own_kernel,
        [VM, SM],
        (shape(6, 4, 2, 32, 128), blocks(8), blocks(FLAG_COUNT), blocks(32)),
        (old, bounds_old),
    )
    coef = call(
        coefficient_kernel,
        [SM] * 3,
        shape(14, 3, 3, 3, 8, 128),
        (neighbours.reshape(-1), levels, refine),
        [pltpu.SMEM((5 * 64,), F32)],
        5,
    )
    ib, peak = call(
        second_kernel,
        [VM] * 7 + [pl.BlockSpec(memory_space=pl.ANY)],
        (blocks(32), one),
        (ib, flags, rb, ra, peak, x8, x9, coef),
    )
    x64 = send(peak, flip_pairs(64))
    ib = send(ib, axis_pairs(0, 1))
    ext, ia = call(
        block_kernel,
        [VM] * 5,
        (shape(6, 4, 2, 32, 128), blocks(32)),
        (own, mine, flags, ra, rb),
    )
    ja, jb, peak = call(
        third_kernel,
        [VM] * 5,
        (blocks(J_BLOCKS + 1), blocks(J_BLOCKS + 1), one),
        (ext, ia, ib, peak, x64),
    )
    x16 = send(peak, flip_pairs(16))
    ja, jb = send(ja, axis_pairs(1, 0)), send(jb, axis_pairs(1, 1))
    inner = call(
        inner_kernel,
        [VM] * 4,
        (shape(4, 2, 40, 128),) * 6 + (blocks(20),) * 2,
        (ext, ia, ib, coef),
        (),
        2,
    )
    *early, ka, kb, peak = call(
        outer_kernel,
        [VM] * 13,
        (shape(5, 2, 40, 128),) * 5 + (blocks(K_BLOCKS + 1),) * 2 + (one,),
        (ja, jb, peak, x16, coef, *inner),
        (),
        1,
    )
    x32 = send(peak, flip_pairs(32))
    ka, kb = send(ka, axis_pairs(2, 0)), send(kb, axis_pairs(2, 1))
    halo, grid = (5, 40, 128), (5, 3, 40, 128)
    adv, prs, sa, sb = call(
        main_kernel,
        [VM] * 10,
        (shape(4, 2, 32, 128),) * 2 + (shape(2, 16, 256),) * 2,
        (*early, ka, kb, peak, x32, coef),
        [pltpu.VMEM(halo, F32)] * 5
        + [pltpu.VMEM(grid, F32)] * 6
        + [pltpu.VMEM((6, *grid), F32)],
        8,
        16,
    )
    sb, sa = send(sb, ODD_PAIRS), send(sa, EVEN_PAIRS)
    vof, pres = call(slots_kernel, [VM] * 2 + [SM], (shape(10, 16, 256),) * 2, (adv, prs, bounds_new))
    even = d % 2 == 0
    low, high = jnp.where(even, sb, sa), jnp.where(even, sa, sb)
    start, stop = bounds_new[d], bounds_new[d + 1]
    slots = jnp.arange(10, dtype=jnp.int32)
    at_low = ((slots == 0) & (start == 8 * d - 1))[:, None, None]
    at_high = ((slots == 8 * d + 8 - start) & (stop == 8 * d + 9))[:, None, None]
    outs = [
        jnp.where(at_low, low[n][None], jnp.where(at_high, high[n][None], x))
        for n, x in enumerate((vof, pres))
    ]
    return tuple(outs)


def solution(mesh):
    in_specs = (
        P(AXES, None, None),
        P(None, AXES, None, None),
        P(AXES, None, None),
        P(AXES, None, None),
        P(),
        P(),
        P(),
        P(),
        P(),
    )
    out_specs = (P(AXES, None, None), P(AXES, None, None))
    return jax.shard_map(local, mesh=mesh, in_specs=in_specs, out_specs=out_specs, check_vma=False)
```

```python
import jax
import jax.numpy as jnp
from jax import lax
from jax.experimental import pallas as pl
from jax.experimental.pallas import tpu as pltpu
from jax.sharding import PartitionSpec as P

SWEEPS = 4
CFL = 0.4
SIGMA = 0.05
RHO_GAS = 0.05
RHO_LIQ = 1.0
AXES = ("row", "col")
DEVS = 128
F32 = jnp.float32


def block_coords(d):
    tree, low = d >> 6, d & 63
    i = (low & 1) | (((low >> 3) & 1) << 1)
    j = ((low >> 1) & 1) | (((low >> 4) & 1) << 1)
    k = ((low >> 2) & 1) | (((low >> 5) & 1) << 1)
    return (7 - i if tree else i), j, k


PLACE = {block_coords(d): d for d in range(DEVS)}


def axis_pairs(axis, odd):
    count = (8, 4, 4)[axis]
    pairs = []
    for d in range(DEVS):
        c = list(block_coords(d))
        step = 1 if (c[axis] % 2 == 0) != bool(odd) else -1
        c[axis] += step
        if 0 <= c[axis] < count:
            pairs.append((d, PLACE[tuple(c)]))
    return pairs


def flip_pairs(bits):
    return [(d, d ^ bits) for d in range(DEVS)]


EVEN_PAIRS = flip_pairs(1)
ODD_PAIRS = [(d, d + 1 if d % 2 else d - 1) for d in range(1, DEVS - 1)]


def send(x, pairs):
    return lax.ppermute(x, AXES, pairs)


def where_is(d):
    tree = d >> 6
    i = (d & 1) | (((d >> 3) & 1) << 1)
    gi = jnp.where(tree == 1, 7 - i, i)
    gj = ((d >> 1) & 1) | (((d >> 4) & 1) << 1)
    gk = ((d >> 2) & 1) | (((d >> 5) & 1) << 1)
    return tree, gi, gj, gk


def where_am_i():
    d = lax.axis_index("row") * 16 + lax.axis_index("col")
    return d, *where_is(d)


def iotas():
    sub = lax.broadcasted_iota(jnp.int32, (8, 128), 0)
    lane = lax.broadcasted_iota(jnp.int32, (8, 128), 1)
    return sub, lane


def rl(x, shift):
    return pltpu.roll(x, shift % 128, 1)


def rs(x, shift):
    n = x.shape[0]
    return pltpu.roll(x, shift % n, 0)


def halves(h):
    return pl.ds(128 * h, 128)


def old_slice(old, f, slot, start, h):
    return old[f, slot, pl.ds(pl.multiple_of(start, 8), 8), halves(h)]


def slab_groups(get, high, sub):
    nat = (sub >= 4) == high
    return (
        get(0),
        get(1),
        jnp.where(nat, get(2), rs(get(3), 4)),
        jnp.where(nat, get(5), rs(get(4), 4)),
    )


def first_kernel(old, levels, bounds, ra, rb, peak):
    d, tree, gi, gj, gk = where_am_i()
    sub, lane = iotas()
    start = bounds[d]
    count = bounds[d + 1] - start
    off = 8 * d - start
    even = d % 2 == 0
    slot_a = jnp.where(even, 8 + off, 0)
    slot_b = jnp.where(even, 0, 8 + off)
    for f in range(6):
        for r in range(2):
            for h in range(2):
                ra[f * 4 + r * 2 + h] = old_slice(old, f, slot_a, 8 * r, h)
                rb[f * 4 + r * 2 + h] = old_slice(old, f, slot_b, 8 * r, h)
    high = gi % 2 == 0
    row0 = jnp.where(high, 8, 0)
    bit = jnp.where(even, 1, 0)
    for q in range(4):
        for h in range(2):
            slot = jnp.clip(bit + 2 * q + off, 0, 9)
            groups = slab_groups(lambda f: old_slice(old, f, slot, row0, h), high, sub)
            for g in range(4):
                ra[24 + (g * 4 + q) * 2 + h] = groups[g]
    top = jnp.zeros((8, 128), F32)
    for s in range(10):
        level = levels[jnp.minimum(start + s, 1023)]
        inv = jnp.where(s < count, jnp.left_shift(1, level), 0).astype(F32)
        part = jnp.zeros((8, 128), F32)
        for r in range(2):
            for h in range(2):
                u = [jnp.abs(old[1 + a, s, pl.ds(8 * r, 8), halves(h)]) for a in range(3)]
                part = jnp.maximum(part, u[0] + u[1] + u[2])
        top = jnp.maximum(top, part * inv)
    ra[56] = top
    peak[0] = top


FLAG_COUNT = 6


def own_kernel(old, bounds, ext, mine, flags, ib):
    d, tree, gi, gj, gk = where_am_i()
    sub, lane = iotas()
    off = 8 * d - bounds[d]
    even = d % 2 == 0
    for t in range(8):
        slot = jnp.clip(t + off, 0, 9)
        bj, bk = (t >> 1) & 1, (t >> 2) & 1
        row0 = 16 * ((t & 1) ^ tree)
        for f in range(6):
            for r in range(2):
                for h in range(2):
                    rows = pl.ds(pl.multiple_of(row0 + 8 * r, 8), 8)
                    ext[f, 2 * bj + h, bk, rows, :] = old_slice(old, f, slot, 8 * r, h)
    high = gi % 2 == 1
    row0 = jnp.where(high, 8, 0)
    slot_a = jnp.where(even, 8 + off, 0)
    bit = jnp.where(even, 0, 1)
    for h in range(2):
        groups = slab_groups(lambda f: old_slice(old, f, slot_a, row0, h), high, sub)
        for g in range(4):
            mine[g * 2 + h] = groups[g]
        for q in range(4):
            slot = jnp.clip(bit + 2 * q + off, 0, 9)
            groups = slab_groups(lambda f: old_slice(old, f, slot, row0, h), high, sub)
            for g in range(4):
                ib[(g * 4 + q) * 2 + h] = groups[g]
    odd = jnp.logical_not(even)
    first, last = bounds[d] == 8 * d + 1, bounds[d + 1] == 8 * d + 7
    values = (
        first,
        last,
        even & (bounds[d + 1] == 8 * d + 9),
        odd & (bounds[d] == 8 * d - 1),
        even & first,
        odd & last,
    )
    for n, value in enumerate(values):
        flags[n] = jnp.full((8, 128), jnp.where(value, 1.0, 0.0), F32)


def second_kernel(ib_in, flags, rb, peak, x8, coef, ib, peak_out):
    d, tree, gi, gj, gk = where_am_i()
    sub, lane = iotas()
    high = gi % 2 == 1
    block = jnp.where(high, 2, 0)
    for q in range(4):
        for h in range(2):
            if q in (0, 3):
                groups = slab_groups(lambda f: rb[f * 4 + block + h], high, sub)
                flag = flags[4 if q == 0 else 5] > 0.5
            for g in range(4):
                n = (g * 4 + q) * 2 + h
                ib[n] = jnp.where(flag, groups[g], ib_in[n]) if q in (0, 3) else ib_in[n]
    peak_out[0] = jnp.maximum(peak[0], x8[0])


def block_kernel(own, mine, flags, ra, rb, ext, ia):
    d, tree, gi, gj, gk = where_am_i()
    even = d % 2 == 0
    flag = [flags[n] > 0.5 for n in range(4)]
    ext[...] = own[...]
    for t, missing in ((0, flag[0]), (7, flag[1])):
        bj, bk = (t >> 1) & 1, (t >> 2) & 1
        row0 = 16 * ((t & 1) ^ tree)
        use_b = even if t == 0 else jnp.logical_not(even)
        for f in range(6):
            for r in range(2):
                for h in range(2):
                    n = f * 4 + r * 2 + h
                    rows = pl.ds(pl.multiple_of(row0 + 8 * r, 8), 8)
                    came = jnp.where(use_b, rb[n], ra[n])
                    ext[f, 2 * bj + h, bk, rows, :] = jnp.where(
                        missing, came, own[f, 2 * bj + h, bk, rows, :]
                    )
    for q in range(4):
        for h in range(2):
            for g in range(4):
                n = (g * 4 + q) * 2 + h
                x = ra[24 + n]
                if q == 0:
                    x = jnp.where(flag[2], mine[g * 2 + h], x)
                if q == 3:
                    x = jnp.where(flag[3], mine[g * 2 + h], x)
                ia[n] = x


def make_block(ext, ia, ib, gi, sub):
    first_high = gi % 2 == 0

    def pair(g, jq, kt):
        n = (g * 4 + jq // 2 + 2 * kt) * 2 + jq % 2
        a, b = ia[n], ib[n]
        return jnp.where(first_high, a, b), jnp.where(first_high, b, a)

    def rows(f, jq, kt, b):
        if b < 4:
            return ext[f, jq, kt, pl.ds(8 * b, 8), :]
        if f == 0:
            return pair(0, jq, kt)[b - 4]
        hi, lo = pair((1, 1, 2, 2, 3, 3)[f], jq, kt)
        if f in (3, 4):
            return rs(jnp.where(sub < 4, lo, hi), 4)
        return jnp.where(sub < 4, hi, lo)

    return rows, pair


J_BLOCKS = 37


def j_place(f, kt, b):
    if f == 0:
        return kt * 6 + b
    if f == 5:
        return 32 + b
    return (12 if f in (2, 4) else 22) + kt * 5 + b


def third_kernel(ext, ia, ib, peak, x64, ja, jb, peak_out):
    d, tree, gi, gj, gk = where_am_i()
    sub, lane = iotas()
    rows, _ = make_block(ext, ia, ib, gi, sub)
    even = gj % 2 == 0

    def put(f, kt, b, get):
        lo, hi = get(0), get(3)
        ja[j_place(f, kt, b)] = jnp.where(even, hi, lo)
        jb[j_place(f, kt, b)] = jnp.where(even, lo, hi)

    for b in range(6):
        for kt in range(2):
            put(0, kt, b, lambda jq: rows(0, jq, kt, b))
    for b in range(5):
        for kt in range(2):
            def five(jq):
                nat = lane < 80 if jq == 0 else lane >= 48
                turn = 80 if jq == 0 else -80
                return jnp.where(nat, rows(2, jq, kt, b), rl(rows(4, jq, kt, b), turn))

            def four(jq):
                nat = lane < 64 if jq == 0 else lane >= 64
                return jnp.where(nat, rows(1, jq, kt, b), rl(rows(3, jq, kt, b), 64))

            put(2, kt, b, five)
            put(1, kt, b, four)

        def both(jq):
            nat = lane < 64 if jq == 0 else lane >= 64
            return jnp.where(nat, rows(5, jq, 0, b), rl(rows(5, jq, 1, b), 64))

        put(5, 0, b, both)
    top = jnp.maximum(peak[0], x64[0])
    ja[J_BLOCKS] = top
    peak_out[0] = top


def make_wide(rows, ja, jb, gj):
    first_high = gj % 2 == 0

    def wide(f, jq, kt, b):
        if jq < 4:
            return rows(f, jq, kt, b)
        n = j_place(f, kt, b)
        if jq == 4:
            x = jnp.where(first_high, ja[n], jb[n])
        else:
            x = jnp.where(first_high, jb[n], ja[n])
        if f == 4:
            return rl(x, -80 if jq == 4 else 80)
        return rl(x, 64) if f == 3 or (f == 5 and kt == 1) else x

    return wide


K_BLOCKS = 38


def k_place(kind, jt, b):
    if jt == 2:
        return 30 + b
    return (0, 10, 10, 20, 20)[kind] + jt * 5 + b


class KPack:
    def __init__(self, gk, lane):
        self.even = gk % 2 == 0
        self.near = lane % 16 < 8
        self.k8 = lane % 8

    def put(self, ka, kb, n, lo, hi):
        ka[n] = jnp.where(self.even, hi, lo)
        kb[n] = jnp.where(self.even, lo, hi)

    def squeeze(self, first, last, kt):
        if kt == 0:
            return jnp.where(self.near, first, rl(last, 8))
        return jnp.where(self.near, rl(first, -8), last)

    def join(self, kind, value, kt):
        if kind == 0:
            return value(0)
        if kind == 1:
            nat, turn = (self.k8 < 5, 5) if kt == 0 else (self.k8 >= 3, -5)
        else:
            nat, turn = (self.k8 < 4, 4) if kt == 0 else (self.k8 >= 4, -4)
        return jnp.where(nat, value(kind), rl(value(kind + 1), turn))

    def block(self, kinds, get, ka, kb):
        for jt in range(2):
            for kind in kinds:
                for b in range(5):
                    sides = []
                    for kt in range(2):

                        def value(n):
                            one, two = get(n, 2 * jt, kt, b), get(n, 2 * jt + 1, kt, b)
                            return self.squeeze(one, two, kt)

                        sides.append(self.join(kind, value, kt))
                    self.put(ka, kb, k_place(kind, jt, b), *sides)

    def halo(self, get, ka, kb):
        for n in range(8):
            sides = []
            for kt in range(2):
                packs = []
                for m in (n, min(n + 8, 14)):
                    kind, b = (0, 1, 3)[m // 5], m % 5
                    packs.append(self.join(kind, lambda f: get(f, kt, b), kt))
                sides.append(self.squeeze(*packs, kt))
            self.put(ka, kb, 30 + n, *sides)


def coefficient_kernel(neighbours, levels, refine, out, table):
    d, tree, gi, gj, gk = where_am_i()
    sub, lane = iotas()

    def one(pos, carry):
        ip, jp, kp = pos >> 4, (pos >> 2) & 3, pos & 3
        x = 2 * gi + jnp.where(ip == 3, -1, ip)
        y = 2 * gj + jnp.where(jp == 3, -1, jp)
        z = 2 * gk + jnp.where(kp == 3, -1, kp)
        inside = (x >= 0) & (x < 16) & (y >= 0) & (y < 8) & (z >= 0) & (z < 8)
        upper = x >= 8
        lx = jnp.where(upper, 15 - x, x)
        code = jnp.where(upper, 512, 0)
        for bit in range(3):
            for axis, v in enumerate((lx, y, z)):
                code = code | (((v >> bit) & 1) << (3 * bit + axis))
        code = jnp.where(inside, code, 0)
        level = levels[code]
        depth = level + refine[code]
        for axis in range(3):
            opened = inside & (neighbours[code * 6 + 2 * axis + 1] >= 0)
            table[axis * 64 + pos] = jnp.where(opened, 1.0, 0.0)
        table[3 * 64 + pos] = jnp.left_shift(1, level).astype(F32)
        table[4 * 64 + pos] = jnp.left_shift(1, 3 - depth).astype(F32)
        return carry

    lax.fori_loop(0, 64, one, 0, unroll=4)
    turns = {0: (0, 1, 2, 3), -1: (3, 0, 1, 3), 1: (1, 2, 2, 0)}

    def spread(item, axis=0, step=0):
        maps = [turns[step if a == axis else 0] for a in range(3)]
        made = []
        for jp in range(4):
            vals = []
            for ip in range(4):
                n = item * 64 + maps[0][ip] * 16 + maps[1][jp] * 4
                v = [jnp.full((8, 128), table[n + maps[2][kp]], F32) for kp in range(4)]
                vals.append((v[0], v[1], jnp.where(lane % 16 < 8, v[2], v[3])))
            made.append(
                [
                    (vals[0][kt], vals[1][kt], jnp.where(sub < 4, vals[2][kt], vals[3][kt]))
                    for kt in range(3)
                ]
            )
        last = [
            [jnp.where(lane < 64, made[2][kt][n], made[3][kt][n]) for n in range(3)]
            for kt in range(3)
        ]
        return made[0], made[1], last

    places = [(jt, kt, n) for jt in range(3) for kt in range(3) for n in range(3)]
    size, inverse = spread(4), spread(3)
    for jt, kt, n in places:
        e = size[jt][kt][n]
        out[12, jt, kt, n] = inverse[jt][kt][n]
        out[13, jt, kt, n] = e * e * (1.0 / 32.0)
    for axis in range(3):
        for side, step in ((0, -1), (1, 1)):
            opened = spread(axis, axis, -1) if side == 0 else spread(axis)
            other = spread(4, axis, step)
            for jt, kt, n in places:
                e, m = size[jt][kt][n], opened[jt][kt][n]
                ratio = (2.0 * e) / (e + other[jt][kt][n])
                out[2 * axis + side, jt, kt, n] = m
                out[6 + 2 * axis + side, jt, kt, n] = jnp.where(m > 0.5, ratio, 1.0)


def coefficient(coef, item, jt, kt):
    a, b, c = (coef[item, jt, kt, n] for n in range(3))
    return jnp.concatenate([a, a, b, b, c], axis=0)


def minmod(a, b):
    return jnp.maximum(jnp.minimum(a, b), 0.0) + jnp.minimum(jnp.maximum(a, b), 0.0)


def face_change(c, up1, up2, dn1, dn2, u, u_up, u_dn):
    upper, lower = up1 - c, c - dn1
    half = 0.5 * minmod(upper, lower)
    half_up = 0.5 * minmod(up2 - up1, upper)
    half_dn = 0.5 * minmod(lower, dn1 - dn2)
    w_up, w_dn = 0.5 * (u + u_up), 0.5 * (u_dn + u)
    flux_up = jnp.maximum(w_up, 0.0) * (c + half) + jnp.minimum(w_up, 0.0) * (up1 - half_up)
    flux_dn = jnp.maximum(w_dn, 0.0) * (dn1 + half_dn) + jnp.minimum(w_dn, 0.0) * (c - half)
    return flux_up - flux_dn


def wrap48(x, sub):
    return jnp.concatenate([x[:32], jnp.where(sub < 4, x[32:40], x[40:48])], axis=0)


class Shifts:
    def __init__(self):
        self.sub, self.lane = iotas()
        self.row = lax.broadcasted_iota(jnp.int32, (40, 128), 0)
        self.lane5 = lax.broadcasted_iota(jnp.int32, (40, 128), 1)
        self.k16 = self.lane5 % 16
        row = self.row
        self.i_top1 = (row == 15) | (row == 31) | (row == 39)
        self.i_top2 = self.i_top1 | (row == 14) | (row == 30) | (row == 38)
        self.i_bot1 = (row == 0) | (row == 16) | (row == 32)
        self.i_bot2 = self.i_bot1 | (row == 1) | (row == 17) | (row == 33)

    def wrap(self, x):
        return wrap48(x, self.sub)

    def k_up(self, x, nxt, n, m=None):
        nxt = rl(nxt, 16 - n)
        return jnp.where(self.k16 < 16 - n, rl(x, -n), nxt if m is None else m * nxt)

    def k_dn(self, x, prv, n, m=None):
        prv = rl(prv, n - 16)
        return jnp.where(self.k16 >= n, rl(x, n), prv if m is None else m * prv)

    def j_up(self, x, nxt, n):
        return rl(jnp.where(self.lane5 < 16 * n, nxt, x), -16 * n)

    def j_dn(self, x, prv, n):
        return rl(jnp.where(self.lane5 >= 128 - 16 * n, prv, x), 16 * n)

    def change_j(self, c, cn, cp, u, un, up, m_dn, m_up):
        lane5 = self.lane5

        def masked(x, m, at):
            return x if m is None else x * jnp.where(at, m, 1.0)

        return face_change(
            c,
            masked(self.j_up(c, cn, 1), m_up, lane5 >= 112),
            masked(self.j_up(c, cn, 2), m_up, lane5 >= 96),
            masked(self.j_dn(c, cp, 1), m_dn, lane5 < 16),
            masked(self.j_dn(c, cp, 2), m_dn, lane5 < 32),
            u,
            masked(self.j_up(u, un, 1), m_up, lane5 >= 112),
            masked(self.j_dn(u, up, 1), m_dn, lane5 < 16),
        )

    def change_i(self, c48, v48, m_dn, m_up):
        up_m1, up_m2 = jnp.where(self.i_top1, m_up, 1.0), jnp.where(self.i_top2, m_up, 1.0)
        dn_m1, dn_m2 = jnp.where(self.i_bot1, m_dn, 1.0), jnp.where(self.i_bot2, m_dn, 1.0)
        wrap = self.wrap
        return face_change(
            wrap(c48), wrap(rs(c48, -1)) * up_m1, wrap(rs(c48, -2)) * up_m2,
            wrap(rs(c48, 1)) * dn_m1, wrap(rs(c48, 2)) * dn_m2,
            wrap(v48), wrap(rs(v48, -1)) * up_m1, wrap(rs(v48, 1)) * dn_m1,
        )


def inner_kernel(ext, ia, ib, coef, c40, u2, src, prs, u1, chg, ka, kb):
    d, tree, gi, gj, gk = where_am_i()
    sh = Shifts()
    rows, pair = make_block(ext, ia, ib, gi, sh.sub)
    dest = {0: c40, 2: u1, 3: u2, 4: src, 5: prs}
    for jq in range(4):
        for kt in range(2):
            jt = jq // 2
            c48 = jnp.concatenate([rows(0, jq, kt, b) for b in range(6)], axis=0)
            v48 = jnp.concatenate(
                [rows(1, jq, kt, b) for b in range(4)] + list(pair(1, jq, kt)), axis=0
            )
            for f, ref in dest.items():
                if f == 0:
                    ref[jq, kt] = sh.wrap(c48)
                else:
                    ref[jq, kt] = jnp.concatenate([rows(f, jq, kt, b) for b in range(5)], axis=0)
            m_dn, m_up = coefficient(coef, 0, jt, kt), coefficient(coef, 1, jt, kt)
            chg[jq, kt] = sh.change_i(c48, v48, m_dn, m_up)
    for jq in (1, 2):
        for kt in range(2):
            m_dn = coefficient(coef, 2, jq // 2, kt) if jq == 2 else None
            m_up = coefficient(coef, 3, jq // 2, kt) if jq == 1 else None
            chg[jq, kt] = chg[jq, kt] + sh.change_j(
                c40[jq, kt], c40[jq + 1, kt], c40[jq - 1, kt],
                u1[jq, kt], u1[jq + 1, kt], u1[jq - 1, kt], m_dn, m_up,
            )
    kinds = (c40, u2, src)
    KPack(gk, sh.lane).block(
        (0, 1), lambda kind, jq, kt, b: kinds[kind][jq, kt, pl.ds(8 * b, 8), :], ka, kb
    )


def outer_kernel(
    ja, jb, peak, x16, x18, coef, c_in, u2_in, src_in, prs_in, u1_in, chg_in, ka_in, kb_in,
    c40, u2, src, prs, chg, ka, kb, peak_out,
):
    d, tree, gi, gj, gk = where_am_i()
    sh = Shifts()
    wide = make_wide(None, ja, jb, gj)
    low5 = sh.lane5 < 64
    for jq in range(4):
        for kt in range(2):
            c40[jq, kt], u2[jq, kt] = c_in[jq, kt], u2_in[jq, kt]
            src[jq, kt], prs[jq, kt] = src_in[jq, kt], prs_in[jq, kt]
            if jq in (1, 2):
                chg[jq, kt] = chg_in[jq, kt]
    for n in range(20):
        ka[n], kb[n] = ka_in[n], kb_in[n]

    def whole(f, jq, kt, count=5):
        return jnp.concatenate([wide(f, jq, kt, b) for b in range(count)], axis=0)

    for kt in range(2):
        for f, ref in ((3, u2), (4, src), (5, prs)):
            ref[4, kt] = jnp.where(low5, whole(f, 4, kt), whole(f, 5, kt))
        c48 = [whole(0, jq, kt, 6) for jq in (4, 5)]
        c_high, c_low = sh.wrap(c48[0]), sh.wrap(c48[1])
        c40[4, kt] = jnp.where(low5, c_high, c_low)
        u_high, u_low = whole(2, 4, kt), whole(2, 5, kt)
        m_dn, m_up = coefficient(coef, 0, 2, kt), coefficient(coef, 1, 2, kt)
        side = []
        for n in range(2):
            v40 = whole(1, 4 + n, kt)
            v48 = jnp.concatenate([v40, v40[32:]], axis=0)
            side.append(sh.change_i(c48[n], v48, m_dn, m_up))
        m_dn, m_up = coefficient(coef, 2, 2, kt), coefficient(coef, 3, 2, kt)
        side[0] = side[0] + sh.change_j(
            c_high, c_low, c_in[3, kt], u_high, u_low, u1_in[3, kt], m_dn, None
        )
        side[1] = side[1] + sh.change_j(
            c_low, c_in[0, kt], c_high, u_low, u1_in[0, kt], u_high, None, m_up
        )
        chg[4, kt] = jnp.where(low5, side[0], side[1])
        chg[0, kt] = chg_in[0, kt] + sh.change_j(
            c_in[0, kt], c_in[1, kt], c_low, u1_in[0, kt], u1_in[1, kt], u_low,
            coefficient(coef, 2, 0, kt), None,
        )
        chg[3, kt] = chg_in[3, kt] + sh.change_j(
            c_in[3, kt], c_high, c_in[2, kt], u1_in[3, kt], u_high, u1_in[2, kt],
            None, coefficient(coef, 3, 1, kt),
        )
    kinds = (c40, u2, src, chg, prs)
    pack = KPack(gk, sh.lane)
    pack.block((3,), lambda kind, jq, kt, b: kinds[kind][jq, kt, pl.ds(8 * b, 8), :], ka, kb)
    pack.halo(lambda kind, kt, b: kinds[kind][4, kt, pl.ds(8 * b, 8), :], ka, kb)
    top = jnp.maximum(
        jnp.maximum(peak[0], ja[J_BLOCKS]), jnp.maximum(x16[0], x18[0])
    )
    ka[K_BLOCKS] = top
    peak_out[0] = top


def main_kernel(
    c_in, u_in, s_in, p_in, chg_in, ka, kb, peak, x32, x36, coef,
    out_adv, out_p, send_a, send_b,
    c_k, u2, src, p_k, chg_k, p0, p1, adv, mob, hgt, rhs, wts,
):
    d, tree, gi, gj, gk = where_am_i()
    sh = Shifts()
    sub, lane, lane5, k16 = sh.sub, sh.lane, sh.lane5, sh.k16
    near = lane % 16 < 8
    k_even = gk % 2 == 0
    dest = (c_k, u2, src, chg_k, p_k)

    def both_sides(n):
        a, e = ka[n], kb[n]
        return jnp.where(k_even, a, e), jnp.where(k_even, e, a)

    for kind in (0, 1, 3):
        turn = (0, 5, 0, 4)[kind]
        for b in range(5):
            rows = pl.ds(8 * b, 8)
            for n in range(1 if kind == 0 else 2):
                ref = dest[kind + n]
                for jt in range(2):
                    low, high = both_sides(k_place(kind, jt, b))
                    if n == 1:
                        low, high = rl(low, -turn), rl(high, turn)
                    ref[2 * jt, rows, :] = jnp.where(near, low, rl(high, 8))
                    ref[2 * jt + 1, rows, :] = jnp.where(near, rl(low, -8), high)
                m = (0, 1, 0, 2)[kind] * 5 + b
                low, high = both_sides(30 + m % 8)
                if m < 8:
                    high = rl(high, 8)
                else:
                    low = rl(low, -8)
                if n == 1:
                    low, high = rl(low, -turn), rl(high, turn)
                ref[4, rows, :] = jnp.where(near, low, high)

    def c40(jq, kt):
        return c_k[jq] if kt == 2 else c_in[jq, kt]

    def uk(jq, kt):
        return u2[jq] if kt == 2 else u_in[jq, kt]

    top = jnp.maximum(
        jnp.maximum(peak[0], ka[K_BLOCKS]), jnp.maximum(x32[0], x36[0])
    )
    top = jnp.max(top, keepdims=True)
    step = jnp.broadcast_to(CFL / top, (8, 128))
    step = jnp.concatenate([step] * 5, axis=0)

    for jq in range(5):
        jt = jq // 2
        for kt in range(3):
            kn, kp = (kt + 1) % 3, (kt + 2) % 3
            change = chg_k[jq] if kt == 2 else chg_in[jq, kt]
            c = c40(jq, kt)
            m_dn, m_up = coefficient(coef, 4, jt, kt), coefficient(coef, 5, jt, kt)
            cn, cp = c40(jq, kn), c40(jq, kp)
            up1, up2 = sh.k_up(c, cn, 1, m_up), sh.k_up(c, cn, 2, m_up)
            dn1, dn2 = sh.k_dn(c, cp, 1, m_dn), sh.k_dn(c, cp, 2, m_dn)
            hgt[jq, kt] = dn2 + dn1 + c + up1 + up2
            u = uk(jq, kt)
            u_up, u_dn = sh.k_up(u, uk(jq, kn), 1, m_up), sh.k_dn(u, uk(jq, kp), 1, m_dn)
            change = change + face_change(c, up1, up2, dn1, dn2, u, u_up, u_dn)
            a = jnp.clip(c - step * coefficient(coef, 12, jt, kt) * change, 0.0, 1.0)
            adv[jq, kt] = a
            mob[jq, kt] = 1.0 / (RHO_GAS + (RHO_LIQ - RHO_GAS) * a)

    k_bot, k_top, j_bot, j_top = k16 < 1, k16 >= 15, lane5 < 16, lane5 >= 112
    for jq in range(5):
        jt, jn, jp = jq // 2, (jq + 1) % 5, (jq + 4) % 5
        edges = (
            sh.i_bot1, sh.i_top1,
            j_bot if jq % 2 == 0 else None, j_top if jq in (1, 3, 4) else None,
            k_bot, k_top,
        )
        for kt in range(3):
            kn, kp = (kt + 1) % 3, (kt + 2) % 3
            opened = [None if e is None else coefficient(coef, f, jt, kt) for f, e in enumerate(edges)]

            def masked(x, f):
                return x if edges[f] is None else x * jnp.where(edges[f], opened[f], 1.0)

            h = hgt[jq, kt]
            h_up, h_dn = masked(rs(h, -1), 1), masked(rs(h, 1), 0)
            gx, sx = 0.5 * (h_up - h_dn), h_up - 2.0 * h + h_dn
            h_up = masked(sh.j_up(h, hgt[jn, kt], 1), 3)
            h_dn = masked(sh.j_dn(h, hgt[jp, kt], 1), 2)
            gy, sy = 0.5 * (h_up - h_dn), h_up - 2.0 * h + h_dn
            gx2, gy2 = gx * gx, gy * gy
            root = lax.rsqrt(1.0 + gx2 + gy2)
            bend = (sx * (1.0 + gy2) + sy * (1.0 + gx2)) * coefficient(coef, 12, jt, kt)
            bend = bend * (root * root * root)
            right = (src[jq] if kt == 2 else s_in[jq, kt]) - SIGMA * bend * adv[jq, kt]
            m = mob[jq, kt]
            across = (
                rs(m, 1), rs(m, -1),
                sh.j_dn(m, mob[jp, kt], 1), sh.j_up(m, mob[jn, kt], 1),
                sh.k_dn(m, mob[jq, kp], 1), sh.k_up(m, mob[jq, kn], 1),
            )
            closed = jnp.zeros_like(m)
            diag = jnp.zeros_like(m)
            parts = []
            for f in range(6):
                part = m + across[f]
                if edges[f] is not None:
                    ratio = coefficient(coef, 6 + f, jt, kt)
                    part = part * jnp.where(edges[f], ratio * opened[f], 1.0)
                    closed = closed + jnp.where(edges[f], 1.0 - opened[f], 0.0)
                diag = diag + part
                parts.append(part)
            inv = 1.0 / (diag + closed * m)
            for f in range(6):
                wts[f, jq, kt] = parts[f] * inv
            rhs[jq, kt] = right * coefficient(coef, 13, jt, kt) * inv

    for sweep in range(SWEEPS):
        new = p0 if sweep % 2 == 0 else p1
        older = p1 if sweep % 2 == 0 else p0
        last = sweep == SWEEPS - 1

        def old(jq, kt):
            if sweep:
                return older[jq, kt]
            return p_k[jq] if kt == 2 else p_in[jq, kt]

        for jq in range(4 if last else 5):
            jn, jp = (jq + 1) % 5, (jq + 4) % 5
            for kt in range(2 if last else 3):
                kn, kp = (kt + 1) % 3, (kt + 2) % 3
                p = old(jq, kt)
                total = wts[0, jq, kt] * rs(p, 1) + wts[1, jq, kt] * rs(p, -1)
                total = total + wts[2, jq, kt] * sh.j_dn(p, old(jp, kt), 1)
                total = total + wts[3, jq, kt] * sh.j_up(p, old(jn, kt), 1)
                total = total + wts[4, jq, kt] * sh.k_dn(p, old(jq, kp), 1)
                total = total + wts[5, jq, kt] * sh.k_up(p, old(jq, kn), 1)
                total = total - rhs[jq, kt]
                if last:
                    out_p[jq, kt] = total[:32]
                    out_adv[jq, kt] = adv[jq, kt][:32]
                else:
                    new[jq, kt] = total

    even = d % 2 == 0
    for h in range(2):
        for n, ref in enumerate((out_adv, out_p)):
            low, high = tile_half(ref, 0, h, tree), tile_half(ref, 7, h, tree)
            send_a[n, :, halves(h)] = jnp.where(even, high, low)
            send_b[n, :, halves(h)] = jnp.where(even, low, high)


def tile_half(ref, t, h, tree):
    row0 = pl.multiple_of(16 * ((t & 1) ^ tree), 16)
    return ref[2 * ((t >> 1) & 1) + h, (t >> 2) & 1, pl.ds(row0, 16), :]


def slots_kernel(adv, prs, bounds, vof, pres):
    d, tree, gi, gj, gk = where_am_i()
    start = bounds[d]
    count = bounds[d + 1] - start
    off = 8 * d - start
    vof[...] = jnp.zeros_like(vof)
    pres[...] = jnp.zeros_like(pres)
    for t in range(8):
        slot = t + off

        @pl.when((slot >= 0) & (slot < count))
        def _(t=t, slot=slot):
            for h in range(2):
                vof[slot, :, halves(h)] = tile_half(adv, t, h, tree)
                pres[slot, :, halves(h)] = tile_half(prs, t, h, tree)


VM = pl.BlockSpec(memory_space=pltpu.VMEM)
SM = pl.BlockSpec(memory_space=pltpu.SMEM)


def shape(*dims):
    return jax.ShapeDtypeStruct(dims, F32)


def blocks(n):
    return shape(n, 8, 128)


def call(kernel, specs, outs, args, scratch=(), micros=1, mib=8):
    return pl.pallas_call(
        kernel,
        out_shape=outs,
        in_specs=specs,
        out_specs=jax.tree.map(lambda _: VM, outs),
        scratch_shapes=list(scratch),
        compiler_params=pltpu.CompilerParams(vmem_limit_bytes=mib * 1024 * 1024),
        cost_estimate=pl.CostEstimate(
            flops=micros * 100000, bytes_accessed=micros * 100000, transcendentals=0
        ),
    )(*args)


def local(volume, velocity, source, pressure_prev, neighbours, levels, refine, bounds_old, bounds_new):
    d = lax.axis_index("row") * 16 + lax.axis_index("col")
    one = blocks(1)
    old = jnp.concatenate([volume[None], velocity, source[None], pressure_prev[None]], axis=0)
    ra, rb, peak = call(
        first_kernel, [VM, SM, SM], (blocks(57), blocks(24), one), (old, levels, bounds_old)
    )
    rb, ra = send(rb, ODD_PAIRS), send(ra, EVEN_PAIRS)
    peak = jnp.maximum(peak, ra[56:57])
    x8 = send(peak, flip_pairs(8))
    own, mine, flags, ib = call(
        own_kernel,
        [VM, SM],
        (shape(6, 4, 2, 32, 128), blocks(8), blocks(FLAG_COUNT), blocks(32)),
        (old, bounds_old),
    )
    coef = call(
        coefficient_kernel,
        [SM] * 3,
        shape(14, 3, 3, 3, 8, 128),
        (neighbours.reshape(-1), levels, refine),
        [pltpu.SMEM((5 * 64,), F32)],
        5,
    )
    ib, peak = call(
        second_kernel,
        [VM] * 5 + [pl.BlockSpec(memory_space=pl.ANY)],
        (blocks(32), one),
        (ib, flags, rb, peak, x8, coef),
    )
    x64 = send(peak, flip_pairs(64))
    ib = send(ib, axis_pairs(0, 1))
    ext, ia = call(
        block_kernel,
        [VM] * 5,
        (shape(6, 4, 2, 32, 128), blocks(32)),
        (own, mine, flags, ra, rb),
    )
    ja, jb, peak = call(
        third_kernel,
        [VM] * 5,
        (blocks(J_BLOCKS + 1), blocks(J_BLOCKS), one),
        (ext, ia, ib, peak, x64),
    )
    x16, x18 = send(peak, flip_pairs(16)), send(peak, flip_pairs(18))
    ja, jb = send(ja, axis_pairs(1, 0)), send(jb, axis_pairs(1, 1))
    inner = call(
        inner_kernel,
        [VM] * 4,
        (shape(4, 2, 40, 128),) * 6 + (blocks(20),) * 2,
        (ext, ia, ib, coef),
        (),
        2,
    )
    *early, ka, kb, peak = call(
        outer_kernel,
        [VM] * 14,
        (shape(5, 2, 40, 128),) * 5 + (blocks(K_BLOCKS + 1), blocks(K_BLOCKS), one),
        (ja, jb, peak, x16, x18, coef, *inner),
        (),
        1,
    )
    x32, x36 = send(peak, flip_pairs(32)), send(peak, flip_pairs(36))
    ka, kb = send(ka, axis_pairs(2, 0)), send(kb, axis_pairs(2, 1))
    halo, grid = (5, 40, 128), (5, 3, 40, 128)
    adv, prs, sa, sb = call(
        main_kernel,
        [VM] * 11,
        (shape(4, 2, 32, 128),) * 2 + (shape(2, 16, 256),) * 2,
        (*early, ka, kb, peak, x32, x36, coef),
        [pltpu.VMEM(halo, F32)] * 5
        + [pltpu.VMEM(grid, F32)] * 6
        + [pltpu.VMEM((6, *grid), F32)],
        8,
        16,
    )
    sb, sa = send(sb, ODD_PAIRS), send(sa, EVEN_PAIRS)
    vof, pres = call(slots_kernel, [VM] * 2 + [SM], (shape(10, 16, 256),) * 2, (adv, prs, bounds_new))
    even = d % 2 == 0
    low, high = jnp.where(even, sb, sa), jnp.where(even, sa, sb)
    start, stop = bounds_new[d], bounds_new[d + 1]
    slots = jnp.arange(10, dtype=jnp.int32)
    at_low = ((slots == 0) & (start == 8 * d - 1))[:, None, None]
    at_high = ((slots == 8 * d + 8 - start) & (stop == 8 * d + 9))[:, None, None]
    outs = [
        jnp.where(at_low, low[n][None], jnp.where(at_high, high[n][None], x))
        for n, x in enumerate((vof, pres))
    ]
    return tuple(outs)


def solution(mesh):
    in_specs = (
        P(AXES, None, None),
        P(None, AXES, None, None),
        P(AXES, None, None),
        P(AXES, None, None),
        P(),
        P(),
        P(),
        P(),
        P(),
    )
    out_specs = (P(AXES, None, None), P(AXES, None, None))
    return jax.shard_map(local, mesh=mesh, in_specs=in_specs, out_specs=out_specs, check_vma=False)
```

```python
import jax
import jax.numpy as jnp
from jax import lax
from jax.experimental import pallas as pl
from jax.experimental.pallas import tpu as pltpu
from jax.sharding import PartitionSpec as P

SWEEPS = 4
CFL = 0.4
SIGMA = 0.05
RHO_GAS = 0.05
RHO_LIQ = 1.0
AXES = ("row", "col")
DEVS = 128
F32 = jnp.float32


def block_coords(d):
    tree, low = d >> 6, d & 63
    i = (low & 1) | (((low >> 3) & 1) << 1)
    j = ((low >> 1) & 1) | (((low >> 4) & 1) << 1)
    k = ((low >> 2) & 1) | (((low >> 5) & 1) << 1)
    return (7 - i if tree else i), j, k


PLACE = {block_coords(d): d for d in range(DEVS)}


def axis_pairs(axis, odd):
    count = (8, 4, 4)[axis]
    pairs = []
    for d in range(DEVS):
        c = list(block_coords(d))
        step = 1 if (c[axis] % 2 == 0) != bool(odd) else -1
        c[axis] = (c[axis] + step) % count
        pairs.append((d, PLACE[tuple(c)]))
    return pairs


def flip_pairs(bits):
    return [(d, d ^ bits) for d in range(DEVS)]


EVEN_PAIRS = flip_pairs(1)
ODD_PAIRS = [(d, d + 1 if d % 2 else d - 1) for d in range(1, DEVS - 1)]


def send(x, pairs):
    return lax.ppermute(x, AXES, pairs)


def where_is(d):
    tree = d >> 6
    i = (d & 1) | (((d >> 3) & 1) << 1)
    gi = jnp.where(tree == 1, 7 - i, i)
    gj = ((d >> 1) & 1) | (((d >> 4) & 1) << 1)
    gk = ((d >> 2) & 1) | (((d >> 5) & 1) << 1)
    return tree, gi, gj, gk


def where_am_i():
    d = lax.axis_index("row") * 16 + lax.axis_index("col")
    return d, *where_is(d)


def iotas():
    sub = lax.broadcasted_iota(jnp.int32, (8, 128), 0)
    lane = lax.broadcasted_iota(jnp.int32, (8, 128), 1)
    return sub, lane


def rl(x, shift):
    return pltpu.roll(x, shift % 128, 1)


def rs(x, shift):
    n = x.shape[0]
    return pltpu.roll(x, shift % n, 0)


def halves(h):
    return pl.ds(128 * h, 128)


def old_slice(old, f, slot, start, h):
    return old[f, slot, pl.ds(pl.multiple_of(start, 8), 8), halves(h)]


def slab_groups(get, high, sub):
    nat = (sub >= 4) == high
    return (
        get(0),
        get(1),
        jnp.where(nat, get(2), rs(get(3), 4)),
        jnp.where(nat, get(5), rs(get(4), 4)),
    )


def first_kernel(old, levels, bounds, ra, rb, peak):
    d, tree, gi, gj, gk = where_am_i()
    sub, lane = iotas()
    start = bounds[d]
    count = bounds[d + 1] - start
    off = 8 * d - start
    even = d % 2 == 0
    slot_a = jnp.where(even, 8 + off, 0)
    slot_b = jnp.where(even, 0, 8 + off)
    for f in range(6):
        for r in range(2):
            for h in range(2):
                ra[f * 4 + r * 2 + h] = old_slice(old, f, slot_a, 8 * r, h)
                rb[f * 4 + r * 2 + h] = old_slice(old, f, slot_b, 8 * r, h)
    high = gi % 2 == 0
    row0 = jnp.where(high, 8, 0)
    bit = jnp.where(even, 1, 0)
    for q in range(4):
        for h in range(2):
            slot = jnp.clip(bit + 2 * q + off, 0, 9)
            groups = slab_groups(lambda f: old_slice(old, f, slot, row0, h), high, sub)
            for g in range(4):
                ra[24 + (g * 4 + q) * 2 + h] = groups[g]
    top = jnp.zeros((8, 128), F32)
    for s in range(10):
        level = levels[jnp.minimum(start + s, 1023)]
        inv = jnp.where(s < count, jnp.left_shift(1, level), 0).astype(F32)
        part = jnp.zeros((8, 128), F32)
        for r in range(2):
            for h in range(2):
                u = [jnp.abs(old[1 + a, s, pl.ds(8 * r, 8), halves(h)]) for a in range(3)]
                part = jnp.maximum(part, u[0] + u[1] + u[2])
        top = jnp.maximum(top, part * inv)
    ra[56] = top
    peak[0] = top


FLAG_COUNT = 6


def own_kernel(old, bounds, ext, mine, flags, ib):
    d, tree, gi, gj, gk = where_am_i()
    sub, lane = iotas()
    off = 8 * d - bounds[d]
    even = d % 2 == 0
    for t in range(8):
        slot = jnp.clip(t + off, 0, 9)
        bj, bk = (t >> 1) & 1, (t >> 2) & 1
        row0 = 16 * ((t & 1) ^ tree)
        for f in range(6):
            for r in range(2):
                for h in range(2):
                    rows = pl.ds(pl.multiple_of(row0 + 8 * r, 8), 8)
                    ext[f, 2 * bj + h, bk, rows, :] = old_slice(old, f, slot, 8 * r, h)
    high = gi % 2 == 1
    row0 = jnp.where(high, 8, 0)
    slot_a = jnp.where(even, 8 + off, 0)
    bit = jnp.where(even, 0, 1)
    for h in range(2):
        groups = slab_groups(lambda f: old_slice(old, f, slot_a, row0, h), high, sub)
        for g in range(4):
            mine[g * 2 + h] = groups[g]
        for q in range(4):
            slot = jnp.clip(bit + 2 * q + off, 0, 9)
            groups = slab_groups(lambda f: old_slice(old, f, slot, row0, h), high, sub)
            for g in range(4):
                ib[(g * 4 + q) * 2 + h] = groups[g]
    odd = jnp.logical_not(even)
    first, last = bounds[d] == 8 * d + 1, bounds[d + 1] == 8 * d + 7
    values = (
        first,
        last,
        even & (bounds[d + 1] == 8 * d + 9),
        odd & (bounds[d] == 8 * d - 1),
        even & first,
        odd & last,
    )
    for n, value in enumerate(values):
        flags[n] = jnp.full((8, 128), jnp.where(value, 1.0, 0.0), F32)


def second_kernel(ib_in, flags, rb, ra, peak, x16, x17, coef, ib, peak_out):
    d, tree, gi, gj, gk = where_am_i()
    sub, lane = iotas()
    high = gi % 2 == 1
    block = jnp.where(high, 2, 0)
    for q in range(4):
        for h in range(2):
            if q in (0, 3):
                groups = slab_groups(lambda f: rb[f * 4 + block + h], high, sub)
                flag = flags[4 if q == 0 else 5] > 0.5
            for g in range(4):
                n = (g * 4 + q) * 2 + h
                ib[n] = jnp.where(flag, groups[g], ib_in[n]) if q in (0, 3) else ib_in[n]
    peak_out[0] = jnp.maximum(jnp.maximum(peak[0], ra[56]), jnp.maximum(x16[0], x17[0]))


def block_kernel(own, mine, flags, ra, rb, ext, ia):
    d, tree, gi, gj, gk = where_am_i()
    even = d % 2 == 0
    flag = [flags[n] > 0.5 for n in range(4)]
    ext[...] = own[...]
    for t, missing in ((0, flag[0]), (7, flag[1])):
        bj, bk = (t >> 1) & 1, (t >> 2) & 1
        row0 = 16 * ((t & 1) ^ tree)
        use_b = even if t == 0 else jnp.logical_not(even)
        for f in range(6):
            for r in range(2):
                for h in range(2):
                    n = f * 4 + r * 2 + h
                    rows = pl.ds(pl.multiple_of(row0 + 8 * r, 8), 8)
                    came = jnp.where(use_b, rb[n], ra[n])
                    ext[f, 2 * bj + h, bk, rows, :] = jnp.where(
                        missing, came, own[f, 2 * bj + h, bk, rows, :]
                    )
    for q in range(4):
        for h in range(2):
            for g in range(4):
                n = (g * 4 + q) * 2 + h
                x = ra[24 + n]
                if q == 0:
                    x = jnp.where(flag[2], mine[g * 2 + h], x)
                if q == 3:
                    x = jnp.where(flag[3], mine[g * 2 + h], x)
                ia[n] = x


def make_block(ext, ia, ib, gi, sub):
    first_high = gi % 2 == 0

    def pair(g, jq, kt):
        n = (g * 4 + jq // 2 + 2 * kt) * 2 + jq % 2
        a, b = ia[n], ib[n]
        return jnp.where(first_high, a, b), jnp.where(first_high, b, a)

    def rows(f, jq, kt, b):
        if b < 4:
            return ext[f, jq, kt, pl.ds(8 * b, 8), :]
        if f == 0:
            return pair(0, jq, kt)[b - 4]
        hi, lo = pair((1, 1, 2, 2, 3, 3)[f], jq, kt)
        if f in (3, 4):
            return rs(jnp.where(sub < 4, lo, hi), 4)
        return jnp.where(sub < 4, hi, lo)

    return rows, pair


J_BLOCKS = 37


def j_place(f, kt, b):
    if f == 0:
        return kt * 6 + b
    if f == 5:
        return 32 + b
    return (12 if f in (2, 4) else 22) + kt * 5 + b


def third_kernel(ext, ia, ib, peak, x64, ja, jb, peak_out):
    d, tree, gi, gj, gk = where_am_i()
    sub, lane = iotas()
    rows, _ = make_block(ext, ia, ib, gi, sub)
    even = gj % 2 == 0

    def put(f, kt, b, get):
        lo, hi = get(0), get(3)
        ja[j_place(f, kt, b)] = jnp.where(even, hi, lo)
        jb[j_place(f, kt, b)] = jnp.where(even, lo, hi)

    for b in range(6):
        for kt in range(2):
            put(0, kt, b, lambda jq: rows(0, jq, kt, b))
    for b in range(5):
        for kt in range(2):
            def five(jq):
                nat = lane < 80 if jq == 0 else lane >= 48
                turn = 80 if jq == 0 else -80
                return jnp.where(nat, rows(2, jq, kt, b), rl(rows(4, jq, kt, b), turn))

            def four(jq):
                nat = lane < 64 if jq == 0 else lane >= 64
                return jnp.where(nat, rows(1, jq, kt, b), rl(rows(3, jq, kt, b), 64))

            put(2, kt, b, five)
            put(1, kt, b, four)

        def both(jq):
            nat = lane < 64 if jq == 0 else lane >= 64
            return jnp.where(nat, rows(5, jq, 0, b), rl(rows(5, jq, 1, b), 64))

        put(5, 0, b, both)
    top = jnp.maximum(peak[0], x64[0])
    ja[J_BLOCKS] = top
    jb[J_BLOCKS] = top
    peak_out[0] = top


def make_wide(rows, ja, jb, gj):
    first_high = gj % 2 == 0

    def wide(f, jq, kt, b):
        if jq < 4:
            return rows(f, jq, kt, b)
        n = j_place(f, kt, b)
        if jq == 4:
            x = jnp.where(first_high, ja[n], jb[n])
        else:
            x = jnp.where(first_high, jb[n], ja[n])
        if f == 4:
            return rl(x, -80 if jq == 4 else 80)
        return rl(x, 64) if f == 3 or (f == 5 and kt == 1) else x

    return wide


K_BLOCKS = 38


def k_place(kind, jt, b):
    if jt == 2:
        return 30 + b
    return (0, 10, 10, 20, 20)[kind] + jt * 5 + b


class KPack:
    def __init__(self, gk, lane):
        self.even = gk % 2 == 0
        self.near = lane % 16 < 8
        self.k8 = lane % 8

    def put(self, ka, kb, n, lo, hi):
        ka[n] = jnp.where(self.even, hi, lo)
        kb[n] = jnp.where(self.even, lo, hi)

    def squeeze(self, first, last, kt):
        if kt == 0:
            return jnp.where(self.near, first, rl(last, 8))
        return jnp.where(self.near, rl(first, -8), last)

    def join(self, kind, value, kt):
        if kind == 0:
            return value(0)
        if kind == 1:
            nat, turn = (self.k8 < 5, 5) if kt == 0 else (self.k8 >= 3, -5)
        else:
            nat, turn = (self.k8 < 4, 4) if kt == 0 else (self.k8 >= 4, -4)
        return jnp.where(nat, value(kind), rl(value(kind + 1), turn))

    def block(self, kinds, get, ka, kb):
        for jt in range(2):
            for kind in kinds:
                for b in range(5):
                    sides = []
                    for kt in range(2):

                        def value(n):
                            one, two = get(n, 2 * jt, kt, b), get(n, 2 * jt + 1, kt, b)
                            return self.squeeze(one, two, kt)

                        sides.append(self.join(kind, value, kt))
                    self.put(ka, kb, k_place(kind, jt, b), *sides)

    def halo(self, get, ka, kb):
        for n in range(8):
            sides = []
            for kt in range(2):
                packs = []
                for m in (n, min(n + 8, 14)):
                    kind, b = (0, 1, 3)[m // 5], m % 5
                    packs.append(self.join(kind, lambda f: get(f, kt, b), kt))
                sides.append(self.squeeze(*packs, kt))
            self.put(ka, kb, 30 + n, *sides)


def coefficient_kernel(neighbours, levels, refine, out, table):
    d, tree, gi, gj, gk = where_am_i()
    sub, lane = iotas()

    def one(pos, carry):
        ip, jp, kp = pos >> 4, (pos >> 2) & 3, pos & 3
        x = 2 * gi + jnp.where(ip == 3, -1, ip)
        y = 2 * gj + jnp.where(jp == 3, -1, jp)
        z = 2 * gk + jnp.where(kp == 3, -1, kp)
        inside = (x >= 0) & (x < 16) & (y >= 0) & (y < 8) & (z >= 0) & (z < 8)
        upper = x >= 8
        lx = jnp.where(upper, 15 - x, x)
        code = jnp.where(upper, 512, 0)
        for bit in range(3):
            for axis, v in enumerate((lx, y, z)):
                code = code | (((v >> bit) & 1) << (3 * bit + axis))
        code = jnp.where(inside, code, 0)
        level = levels[code]
        depth = level + refine[code]
        for axis in range(3):
            opened = inside & (neighbours[code * 6 + 2 * axis + 1] >= 0)
            table[axis * 64 + pos] = jnp.where(opened, 1.0, 0.0)
        table[3 * 64 + pos] = jnp.left_shift(1, level).astype(F32)
        table[4 * 64 + pos] = jnp.left_shift(1, 3 - depth).astype(F32)
        return carry

    lax.fori_loop(0, 64, one, 0, unroll=4)
    turns = {0: (0, 1, 2, 3), -1: (3, 0, 1, 3), 1: (1, 2, 2, 0)}

    def spread(item, axis=0, step=0):
        maps = [turns[step if a == axis else 0] for a in range(3)]
        made = []
        for jp in range(4):
            vals = []
            for ip in range(4):
                n = item * 64 + maps[0][ip] * 16 + maps[1][jp] * 4
                v = [jnp.full((8, 128), table[n + maps[2][kp]], F32) for kp in range(4)]
                vals.append((v[0], v[1], jnp.where(lane % 16 < 8, v[2], v[3])))
            made.append(
                [
                    (vals[0][kt], vals[1][kt], jnp.where(sub < 4, vals[2][kt], vals[3][kt]))
                    for kt in range(3)
                ]
            )
        last = [
            [jnp.where(lane < 64, made[2][kt][n], made[3][kt][n]) for n in range(3)]
            for kt in range(3)
        ]
        return made[0], made[1], last

    places = [(jt, kt, n) for jt in range(3) for kt in range(3) for n in range(3)]
    size, inverse = spread(4), spread(3)
    for jt, kt, n in places:
        e = size[jt][kt][n]
        out[12, jt, kt, n] = inverse[jt][kt][n]
        out[13, jt, kt, n] = e * e * (1.0 / 32.0)
    for axis in range(3):
        for side, step in ((0, -1), (1, 1)):
            opened = spread(axis, axis, -1) if side == 0 else spread(axis)
            other = spread(4, axis, step)
            for jt, kt, n in places:
                e, m = size[jt][kt][n], opened[jt][kt][n]
                ratio = (2.0 * e) / (e + other[jt][kt][n])
                out[2 * axis + side, jt, kt, n] = m
                out[6 + 2 * axis + side, jt, kt, n] = jnp.where(m > 0.5, ratio, 1.0)


def coefficient(coef, item, jt, kt):
    a, b, c = (coef[item, jt, kt, n] for n in range(3))
    return jnp.concatenate([a, a, b, b, c], axis=0)


def minmod(a, b):
    return jnp.maximum(jnp.minimum(a, b), 0.0) + jnp.minimum(jnp.maximum(a, b), 0.0)


def face_change(c, up1, up2, dn1, dn2, u, u_up, u_dn):
    upper, lower = up1 - c, c - dn1
    half = 0.5 * minmod(upper, lower)
    half_up = 0.5 * minmod(up2 - up1, upper)
    half_dn = 0.5 * minmod(lower, dn1 - dn2)
    w_up, w_dn = 0.5 * (u + u_up), 0.5 * (u_dn + u)
    flux_up = jnp.maximum(w_up, 0.0) * (c + half) + jnp.minimum(w_up, 0.0) * (up1 - half_up)
    flux_dn = jnp.maximum(w_dn, 0.0) * (dn1 + half_dn) + jnp.minimum(w_dn, 0.0) * (c - half)
    return flux_up - flux_dn


def wrap48(x, sub):
    return jnp.concatenate([x[:32], jnp.where(sub < 4, x[32:40], x[40:48])], axis=0)


class Shifts:
    def __init__(self):
        self.sub, self.lane = iotas()
        self.row = lax.broadcasted_iota(jnp.int32, (40, 128), 0)
        self.lane5 = lax.broadcasted_iota(jnp.int32, (40, 128), 1)
        self.k16 = self.lane5 % 16
        row = self.row
        self.i_top1 = (row == 15) | (row == 31) | (row == 39)
        self.i_top2 = self.i_top1 | (row == 14) | (row == 30) | (row == 38)
        self.i_bot1 = (row == 0) | (row == 16) | (row == 32)
        self.i_bot2 = self.i_bot1 | (row == 1) | (row == 17) | (row == 33)

    def wrap(self, x):
        return wrap48(x, self.sub)

    def k_up(self, x, nxt, n, m=None):
        nxt = rl(nxt, 16 - n)
        return jnp.where(self.k16 < 16 - n, rl(x, -n), nxt if m is None else m * nxt)

    def k_dn(self, x, prv, n, m=None):
        prv = rl(prv, n - 16)
        return jnp.where(self.k16 >= n, rl(x, n), prv if m is None else m * prv)

    def j_up(self, x, nxt, n):
        return rl(jnp.where(self.lane5 < 16 * n, nxt, x), -16 * n)

    def j_dn(self, x, prv, n):
        return rl(jnp.where(self.lane5 >= 128 - 16 * n, prv, x), 16 * n)

    def change_j(self, c, cn, cp, u, un, up, m_dn, m_up):
        lane5 = self.lane5

        def masked(x, m, at):
            return x if m is None else x * jnp.where(at, m, 1.0)

        return face_change(
            c,
            masked(self.j_up(c, cn, 1), m_up, lane5 >= 112),
            masked(self.j_up(c, cn, 2), m_up, lane5 >= 96),
            masked(self.j_dn(c, cp, 1), m_dn, lane5 < 16),
            masked(self.j_dn(c, cp, 2), m_dn, lane5 < 32),
            u,
            masked(self.j_up(u, un, 1), m_up, lane5 >= 112),
            masked(self.j_dn(u, up, 1), m_dn, lane5 < 16),
        )

    def change_i(self, c48, v48, m_dn, m_up):
        up_m1, up_m2 = jnp.where(self.i_top1, m_up, 1.0), jnp.where(self.i_top2, m_up, 1.0)
        dn_m1, dn_m2 = jnp.where(self.i_bot1, m_dn, 1.0), jnp.where(self.i_bot2, m_dn, 1.0)
        wrap = self.wrap
        return face_change(
            wrap(c48), wrap(rs(c48, -1)) * up_m1, wrap(rs(c48, -2)) * up_m2,
            wrap(rs(c48, 1)) * dn_m1, wrap(rs(c48, 2)) * dn_m2,
            wrap(v48), wrap(rs(v48, -1)) * up_m1, wrap(rs(v48, 1)) * dn_m1,
        )


def inner_kernel(ext, ia, ib, coef, c40, u2, src, prs, u1, chg, ka, kb):
    d, tree, gi, gj, gk = where_am_i()
    sh = Shifts()
    rows, pair = make_block(ext, ia, ib, gi, sh.sub)
    dest = {0: c40, 2: u1, 3: u2, 4: src, 5: prs}
    for jq in range(4):
        for kt in range(2):
            jt = jq // 2
            c48 = jnp.concatenate([rows(0, jq, kt, b) for b in range(6)], axis=0)
            v48 = jnp.concatenate(
                [rows(1, jq, kt, b) for b in range(4)] + list(pair(1, jq, kt)), axis=0
            )
            for f, ref in dest.items():
                if f == 0:
                    ref[jq, kt] = sh.wrap(c48)
                else:
                    ref[jq, kt] = jnp.concatenate([rows(f, jq, kt, b) for b in range(5)], axis=0)
            m_dn, m_up = coefficient(coef, 0, jt, kt), coefficient(coef, 1, jt, kt)
            chg[jq, kt] = sh.change_i(c48, v48, m_dn, m_up)
    for jq in (1, 2):
        for kt in range(2):
            m_dn = coefficient(coef, 2, jq // 2, kt) if jq == 2 else None
            m_up = coefficient(coef, 3, jq // 2, kt) if jq == 1 else None
            chg[jq, kt] = chg[jq, kt] + sh.change_j(
                c40[jq, kt], c40[jq + 1, kt], c40[jq - 1, kt],
                u1[jq, kt], u1[jq + 1, kt], u1[jq - 1, kt], m_dn, m_up,
            )
    kinds = (c40, u2, src)
    KPack(gk, sh.lane).block(
        (0, 1), lambda kind, jq, kt, b: kinds[kind][jq, kt, pl.ds(8 * b, 8), :], ka, kb
    )


def outer_kernel(
    ja, jb, peak, x8, coef, c_in, u2_in, src_in, prs_in, u1_in, chg_in, ka_in, kb_in,
    c40, u2, src, prs, chg, ka, kb, peak_out,
):
    d, tree, gi, gj, gk = where_am_i()
    sh = Shifts()
    wide = make_wide(None, ja, jb, gj)
    low5 = sh.lane5 < 64
    low6 = lax.broadcasted_iota(jnp.int32, (48, 128), 1) < 64
    for jq in range(4):
        for kt in range(2):
            c40[jq, kt], u2[jq, kt] = c_in[jq, kt], u2_in[jq, kt]
            src[jq, kt], prs[jq, kt] = src_in[jq, kt], prs_in[jq, kt]
            if jq in (1, 2):
                chg[jq, kt] = chg_in[jq, kt]
    for n in range(20):
        ka[n], kb[n] = ka_in[n], kb_in[n]

    def whole(f, jq, kt, count=5):
        return jnp.concatenate([wide(f, jq, kt, b) for b in range(count)], axis=0)

    for kt in range(2):
        for f, ref in ((3, u2), (4, src), (5, prs)):
            ref[4, kt] = jnp.where(low5, whole(f, 4, kt), whole(f, 5, kt))
        c48 = [whole(0, jq, kt, 6) for jq in (4, 5)]
        c_high, c_low = sh.wrap(c48[0]), sh.wrap(c48[1])
        c40[4, kt] = jnp.where(low5, c_high, c_low)
        u_high, u_low = whole(2, 4, kt), whole(2, 5, kt)
        m_dn, m_up = coefficient(coef, 0, 2, kt), coefficient(coef, 1, 2, kt)
        v40 = jnp.where(low5, whole(1, 4, kt), whole(1, 5, kt))
        v48 = jnp.concatenate([v40, v40[32:]], axis=0)
        along_i = sh.change_i(jnp.where(low6, c48[0], c48[1]), v48, m_dn, m_up)
        m_dn, m_up = coefficient(coef, 2, 2, kt), coefficient(coef, 3, 2, kt)
        high = sh.change_j(c_high, c_low, c_in[3, kt], u_high, u_low, u1_in[3, kt], m_dn, None)
        low = sh.change_j(c_low, c_in[0, kt], c_high, u_low, u1_in[0, kt], u_high, None, m_up)
        chg[4, kt] = along_i + jnp.where(low5, high, low)
        chg[0, kt] = chg_in[0, kt] + sh.change_j(
            c_in[0, kt], c_in[1, kt], c_low, u1_in[0, kt], u1_in[1, kt], u_low,
            coefficient(coef, 2, 0, kt), None,
        )
        chg[3, kt] = chg_in[3, kt] + sh.change_j(
            c_in[3, kt], c_high, c_in[2, kt], u1_in[3, kt], u_high, u1_in[2, kt],
            None, coefficient(coef, 3, 1, kt),
        )
    kinds = (c40, u2, src, chg, prs)
    pack = KPack(gk, sh.lane)
    pack.block((3,), lambda kind, jq, kt, b: kinds[kind][jq, kt, pl.ds(8 * b, 8), :], ka, kb)
    pack.halo(lambda kind, kt, b: kinds[kind][4, kt, pl.ds(8 * b, 8), :], ka, kb)
    top = jnp.maximum(
        jnp.maximum(peak[0], x8[0]), jnp.maximum(ja[J_BLOCKS], jb[J_BLOCKS])
    )
    ka[K_BLOCKS] = top
    kb[K_BLOCKS] = top
    peak_out[0] = top


def main_kernel(
    c_in, u_in, s_in, p_in, chg_in, ka, kb, peak, x32, coef,
    out_adv, out_p, send_a, send_b,
    c_k, u2, src, p_k, chg_k, p0, p1, adv, mob, hgt, rhs, wts,
):
    d, tree, gi, gj, gk = where_am_i()
    sh = Shifts()
    sub, lane, lane5, k16 = sh.sub, sh.lane, sh.lane5, sh.k16
    near = lane % 16 < 8
    k_even = gk % 2 == 0
    dest = (c_k, u2, src, chg_k, p_k)

    def both_sides(n):
        a, e = ka[n], kb[n]
        return jnp.where(k_even, a, e), jnp.where(k_even, e, a)

    for kind in (0, 1, 3):
        turn = (0, 5, 0, 4)[kind]
        for b in range(5):
            rows = pl.ds(8 * b, 8)
            for n in range(1 if kind == 0 else 2):
                ref = dest[kind + n]
                for jt in range(2):
                    low, high = both_sides(k_place(kind, jt, b))
                    if n == 1:
                        low, high = rl(low, -turn), rl(high, turn)
                    ref[2 * jt, rows, :] = jnp.where(near, low, rl(high, 8))
                    ref[2 * jt + 1, rows, :] = jnp.where(near, rl(low, -8), high)
                m = (0, 1, 0, 2)[kind] * 5 + b
                low, high = both_sides(30 + m % 8)
                if m < 8:
                    high = rl(high, 8)
                else:
                    low = rl(low, -8)
                if n == 1:
                    low, high = rl(low, -turn), rl(high, turn)
                ref[4, rows, :] = jnp.where(near, low, high)

    def c40(jq, kt):
        return c_k[jq] if kt == 2 else c_in[jq, kt]

    def uk(jq, kt):
        return u2[jq] if kt == 2 else u_in[jq, kt]

    top = jnp.maximum(
        jnp.maximum(peak[0], x32[0]), jnp.maximum(ka[K_BLOCKS], kb[K_BLOCKS])
    )
    top = jnp.max(top, keepdims=True)
    step = jnp.broadcast_to(CFL / top, (8, 128))
    step = jnp.concatenate([step] * 5, axis=0)

    for jq in range(5):
        jt = jq // 2
        for kt in range(3):
            kn, kp = (kt + 1) % 3, (kt + 2) % 3
            change = chg_k[jq] if kt == 2 else chg_in[jq, kt]
            c = c40(jq, kt)
            m_dn, m_up = coefficient(coef, 4, jt, kt), coefficient(coef, 5, jt, kt)
            cn, cp = c40(jq, kn), c40(jq, kp)
            up1, up2 = sh.k_up(c, cn, 1, m_up), sh.k_up(c, cn, 2, m_up)
            dn1, dn2 = sh.k_dn(c, cp, 1, m_dn), sh.k_dn(c, cp, 2, m_dn)
            hgt[jq, kt] = dn2 + dn1 + c + up1 + up2
            u = uk(jq, kt)
            u_up, u_dn = sh.k_up(u, uk(jq, kn), 1, m_up), sh.k_dn(u, uk(jq, kp), 1, m_dn)
            change = change + face_change(c, up1, up2, dn1, dn2, u, u_up, u_dn)
            a = jnp.clip(c - step * coefficient(coef, 12, jt, kt) * change, 0.0, 1.0)
            adv[jq, kt] = a
            mob[jq, kt] = 1.0 / (RHO_GAS + (RHO_LIQ - RHO_GAS) * a)

    k_bot, k_top, j_bot, j_top = k16 < 1, k16 >= 15, lane5 < 16, lane5 >= 112
    for jq in range(5):
        jt, jn, jp = jq // 2, (jq + 1) % 5, (jq + 4) % 5
        edges = (
            sh.i_bot1, sh.i_top1,
            j_bot if jq % 2 == 0 else None, j_top if jq in (1, 3, 4) else None,
            k_bot, k_top,
        )
        for kt in range(3):
            kn, kp = (kt + 1) % 3, (kt + 2) % 3
            opened = [None if e is None else coefficient(coef, f, jt, kt) for f, e in enumerate(edges)]

            def masked(x, f):
                return x if edges[f] is None else x * jnp.where(edges[f], opened[f], 1.0)

            h = hgt[jq, kt]
            h_up, h_dn = masked(rs(h, -1), 1), masked(rs(h, 1), 0)
            gx, sx = 0.5 * (h_up - h_dn), h_up - 2.0 * h + h_dn
            h_up = masked(sh.j_up(h, hgt[jn, kt], 1), 3)
            h_dn = masked(sh.j_dn(h, hgt[jp, kt], 1), 2)
            gy, sy = 0.5 * (h_up - h_dn), h_up - 2.0 * h + h_dn
            gx2, gy2 = gx * gx, gy * gy
            root = lax.rsqrt(1.0 + gx2 + gy2)
            bend = (sx * (1.0 + gy2) + sy * (1.0 + gx2)) * coefficient(coef, 12, jt, kt)
            bend = bend * (root * root * root)
            right = (src[jq] if kt == 2 else s_in[jq, kt]) - SIGMA * bend * adv[jq, kt]
            m = mob[jq, kt]
            across = (
                rs(m, 1), rs(m, -1),
                sh.j_dn(m, mob[jp, kt], 1), sh.j_up(m, mob[jn, kt], 1),
                sh.k_dn(m, mob[jq, kp], 1), sh.k_up(m, mob[jq, kn], 1),
            )
            closed = jnp.zeros_like(m)
            diag = jnp.zeros_like(m)
            parts = []
            for f in range(6):
                part = m + across[f]
                if edges[f] is not None:
                    ratio = coefficient(coef, 6 + f, jt, kt)
                    part = part * jnp.where(edges[f], ratio * opened[f], 1.0)
                    closed = closed + jnp.where(edges[f], 1.0 - opened[f], 0.0)
                diag = diag + part
                parts.append(part)
            inv = 1.0 / (diag + closed * m)
            for f in range(6):
                wts[f, jq, kt] = parts[f] * inv
            rhs[jq, kt] = right * coefficient(coef, 13, jt, kt) * inv

    for sweep in range(SWEEPS):
        new = p0 if sweep % 2 == 0 else p1
        older = p1 if sweep % 2 == 0 else p0
        last = sweep == SWEEPS - 1

        def old(jq, kt):
            if sweep:
                return older[jq, kt]
            return p_k[jq] if kt == 2 else p_in[jq, kt]

        for jq in range(4 if last else 5):
            jn, jp = (jq + 1) % 5, (jq + 4) % 5
            for kt in range(2 if last or (sweep == SWEEPS - 2 and jq == 4) else 3):
                kn, kp = (kt + 1) % 3, (kt + 2) % 3
                p = old(jq, kt)
                total = wts[0, jq, kt] * rs(p, 1) + wts[1, jq, kt] * rs(p, -1)
                total = total + wts[2, jq, kt] * sh.j_dn(p, old(jp, kt), 1)
                total = total + wts[3, jq, kt] * sh.j_up(p, old(jn, kt), 1)
                total = total + wts[4, jq, kt] * sh.k_dn(p, old(jq, kp), 1)
                total = total + wts[5, jq, kt] * sh.k_up(p, old(jq, kn), 1)
                total = total - rhs[jq, kt]
                if last:
                    out_p[jq, kt] = total[:32]
                    out_adv[jq, kt] = adv[jq, kt][:32]
                else:
                    new[jq, kt] = total

    even = d % 2 == 0
    for h in range(2):
        for n, ref in enumerate((out_adv, out_p)):
            low, high = tile_half(ref, 0, h, tree), tile_half(ref, 7, h, tree)
            send_a[n, :, halves(h)] = jnp.where(even, high, low)
            send_b[n, :, halves(h)] = jnp.where(even, low, high)


def tile_half(ref, t, h, tree):
    row0 = pl.multiple_of(16 * ((t & 1) ^ tree), 16)
    return ref[2 * ((t >> 1) & 1) + h, (t >> 2) & 1, pl.ds(row0, 16), :]


def slots_kernel(adv, prs, bounds, vof, pres):
    d, tree, gi, gj, gk = where_am_i()
    start = bounds[d]
    count = bounds[d + 1] - start
    off = 8 * d - start
    vof[...] = jnp.zeros_like(vof)
    pres[...] = jnp.zeros_like(pres)
    for t in range(8):
        slot = t + off

        @pl.when((slot >= 0) & (slot < count))
        def _(t=t, slot=slot):
            for h in range(2):
                vof[slot, :, halves(h)] = tile_half(adv, t, h, tree)
                pres[slot, :, halves(h)] = tile_half(prs, t, h, tree)


VM = pl.BlockSpec(memory_space=pltpu.VMEM)
SM = pl.BlockSpec(memory_space=pltpu.SMEM)


def shape(*dims):
    return jax.ShapeDtypeStruct(dims, F32)


def blocks(n):
    return shape(n, 8, 128)


def call(kernel, specs, outs, args, scratch=(), micros=1, mib=8):
    return pl.pallas_call(
        kernel,
        out_shape=outs,
        in_specs=specs,
        out_specs=jax.tree.map(lambda _: VM, outs),
        scratch_shapes=list(scratch),
        compiler_params=pltpu.CompilerParams(vmem_limit_bytes=mib * 1024 * 1024),
        cost_estimate=pl.CostEstimate(
            flops=micros * 100000, bytes_accessed=micros * 100000, transcendentals=0
        ),
    )(*args)


def local(volume, velocity, source, pressure_prev, neighbours, levels, refine, bounds_old, bounds_new):
    d = lax.axis_index("row") * 16 + lax.axis_index("col")
    one = blocks(1)
    old = jnp.concatenate([volume[None], velocity, source[None], pressure_prev[None]], axis=0)
    ra, rb, peak = call(
        first_kernel, [VM, SM, SM], (blocks(57), blocks(24), one), (old, levels, bounds_old)
    )
    x16, x17 = send(peak, flip_pairs(16)), send(peak, flip_pairs(17))
    rb, ra = send(rb, ODD_PAIRS), send(ra, EVEN_PAIRS)
    own, mine, flags, ib = call(
        own_kernel,
        [VM, SM],
        (shape(6, 4, 2, 32, 128), blocks(8), blocks(FLAG_COUNT), blocks(32)),
        (old, bounds_old),
    )
    coef = call(
        coefficient_kernel,
        [SM] * 3,
        shape(14, 3, 3, 3, 8, 128),
        (neighbours.reshape(-1), levels, refine),
        [pltpu.SMEM((5 * 64,), F32)],
        5,
    )
    ib, peak = call(
        second_kernel,
        [VM] * 7 + [pl.BlockSpec(memory_space=pl.ANY)],
        (blocks(32), one),
        (ib, flags, rb, ra, peak, x16, x17, coef),
    )
    x64 = send(peak, flip_pairs(64))
    ib = send(ib, axis_pairs(0, 1))
    ext, ia = call(
        block_kernel,
        [VM] * 5,
        (shape(6, 4, 2, 32, 128), blocks(32)),
        (own, mine, flags, ra, rb),
    )
    ja, jb, peak = call(
        third_kernel,
        [VM] * 5,
        (blocks(J_BLOCKS + 1), blocks(J_BLOCKS + 1), one),
        (ext, ia, ib, peak, x64),
    )
    x8 = jnp.maximum(send(peak, flip_pairs(8)), send(peak, flip_pairs(10)))
    ja, jb = send(ja, axis_pairs(1, 0)), send(jb, axis_pairs(1, 1))
    inner = call(
        inner_kernel,
        [VM] * 4,
        (shape(4, 2, 40, 128),) * 6 + (blocks(20),) * 2,
        (ext, ia, ib, coef),
        (),
        2,
    )
    *early, ka, kb, peak = call(
        outer_kernel,
        [VM] * 13,
        (shape(5, 2, 40, 128),) * 5 + (blocks(K_BLOCKS + 1),) * 2 + (one,),
        (ja, jb, peak, x8, coef, *inner),
        (),
        1,
    )
    x32 = send(peak, flip_pairs(32))
    ka, kb = send(ka, axis_pairs(2, 0)), send(kb, axis_pairs(2, 1))
    halo, grid = (5, 40, 128), (5, 3, 40, 128)
    adv, prs, sa, sb = call(
        main_kernel,
        [VM] * 10,
        (shape(4, 2, 32, 128),) * 2 + (shape(2, 16, 256),) * 2,
        (*early, ka, kb, peak, x32, coef),
        [pltpu.VMEM(halo, F32)] * 5
        + [pltpu.VMEM(grid, F32)] * 6
        + [pltpu.VMEM((6, *grid), F32)],
        8,
        16,
    )
    sb, sa = send(sb, ODD_PAIRS), send(sa, EVEN_PAIRS)
    vof, pres = call(slots_kernel, [VM] * 2 + [SM], (shape(10, 16, 256),) * 2, (adv, prs, bounds_new))
    even = d % 2 == 0
    low, high = jnp.where(even, sb, sa), jnp.where(even, sa, sb)
    start, stop = bounds_new[d], bounds_new[d + 1]
    slots = jnp.arange(10, dtype=jnp.int32)
    at_low = ((slots == 0) & (start == 8 * d - 1))[:, None, None]
    at_high = ((slots == 8 * d + 8 - start) & (stop == 8 * d + 9))[:, None, None]
    outs = [
        jnp.where(at_low, low[n][None], jnp.where(at_high, high[n][None], x))
        for n, x in enumerate((vof, pres))
    ]
    return tuple(outs)


def solution(mesh):
    in_specs = (
        P(AXES, None, None),
        P(None, AXES, None, None),
        P(AXES, None, None),
        P(AXES, None, None),
        P(),
        P(),
        P(),
        P(),
        P(),
    )
    out_specs = (P(AXES, None, None), P(AXES, None, None))
    return jax.shard_map(local, mesh=mesh, in_specs=in_specs, out_specs=out_specs, check_vma=False)
```

```python
import jax
import jax.numpy as jnp
from jax import lax
from jax.experimental import pallas as pl
from jax.experimental.pallas import tpu as pltpu
from jax.sharding import PartitionSpec as P

SWEEPS = 4
CFL = 0.4
SIGMA = 0.05
RHO_GAS = 0.05
RHO_LIQ = 1.0
AXES = ("row", "col")
DEVS = 128
F32 = jnp.float32


def block_coords(d):
    tree, low = d >> 6, d & 63
    i = (low & 1) | (((low >> 3) & 1) << 1)
    j = ((low >> 1) & 1) | (((low >> 4) & 1) << 1)
    k = ((low >> 2) & 1) | (((low >> 5) & 1) << 1)
    return (7 - i if tree else i), j, k


PLACE = {block_coords(d): d for d in range(DEVS)}


def axis_pairs(axis, odd):
    count = (8, 4, 4)[axis]
    pairs = []
    for d in range(DEVS):
        c = list(block_coords(d))
        step = 1 if (c[axis] % 2 == 0) != bool(odd) else -1
        c[axis] = (c[axis] + step) % count
        pairs.append((d, PLACE[tuple(c)]))
    return pairs


def flip_pairs(bits):
    return [(d, d ^ bits) for d in range(DEVS)]


EVEN_PAIRS = flip_pairs(1)
ODD_PAIRS = [(d, d + 1 if d % 2 else d - 1) for d in range(1, DEVS - 1)]


def send(x, pairs):
    return lax.ppermute(x, AXES, pairs)


def where_is(d):
    tree = d >> 6
    i = (d & 1) | (((d >> 3) & 1) << 1)
    gi = jnp.where(tree == 1, 7 - i, i)
    gj = ((d >> 1) & 1) | (((d >> 4) & 1) << 1)
    gk = ((d >> 2) & 1) | (((d >> 5) & 1) << 1)
    return tree, gi, gj, gk


def where_am_i():
    d = lax.axis_index("row") * 16 + lax.axis_index("col")
    return d, *where_is(d)


def iotas():
    sub = lax.broadcasted_iota(jnp.int32, (8, 128), 0)
    lane = lax.broadcasted_iota(jnp.int32, (8, 128), 1)
    return sub, lane


def rl(x, shift):
    return pltpu.roll(x, shift % 128, 1)


def rs(x, shift):
    n = x.shape[0]
    return pltpu.roll(x, shift % n, 0)


def halves(h):
    return pl.ds(128 * h, 128)


def old_slice(old, f, slot, start, h):
    return old[f, slot, pl.ds(pl.multiple_of(start, 8), 8), halves(h)]


def slab_groups(get, high, sub):
    nat = (sub >= 4) == high
    return (
        get(0),
        get(1),
        jnp.where(nat, get(2), rs(get(3), 4)),
        jnp.where(nat, get(5), rs(get(4), 4)),
    )


def first_kernel(old, levels, bounds, ra, rb, peak):
    d, tree, gi, gj, gk = where_am_i()
    sub, lane = iotas()
    start = bounds[d]
    count = bounds[d + 1] - start
    off = 8 * d - start
    even = d % 2 == 0
    slot_a = jnp.where(even, 8 + off, 0)
    slot_b = jnp.where(even, 0, 8 + off)
    for f in range(6):
        for r in range(2):
            for h in range(2):
                ra[f * 4 + r * 2 + h] = old_slice(old, f, slot_a, 8 * r, h)
                rb[f * 4 + r * 2 + h] = old_slice(old, f, slot_b, 8 * r, h)
    high = gi % 2 == 0
    row0 = jnp.where(high, 8, 0)
    bit = jnp.where(even, 1, 0)
    for q in range(4):
        for h in range(2):
            slot = jnp.clip(bit + 2 * q + off, 0, 9)
            groups = slab_groups(lambda f: old_slice(old, f, slot, row0, h), high, sub)
            for g in range(4):
                ra[24 + (g * 4 + q) * 2 + h] = groups[g]
    top = jnp.zeros((8, 128), F32)
    for s in range(10):
        level = levels[jnp.minimum(start + s, 1023)]
        inv = jnp.where(s < count, jnp.left_shift(1, level), 0).astype(F32)
        part = jnp.zeros((8, 128), F32)
        for r in range(2):
            for h in range(2):
                u = [jnp.abs(old[1 + a, s, pl.ds(8 * r, 8), halves(h)]) for a in range(3)]
                part = jnp.maximum(part, u[0] + u[1] + u[2])
        top = jnp.maximum(top, part * inv)
    ra[56] = top
    peak[0] = top


FLAG_COUNT = 6


def own_kernel(old, bounds, ext, mine, flags, ib):
    d, tree, gi, gj, gk = where_am_i()
    sub, lane = iotas()
    off = 8 * d - bounds[d]
    even = d % 2 == 0
    for t in range(8):
        slot = jnp.clip(t + off, 0, 9)
        bj, bk = (t >> 1) & 1, (t >> 2) & 1
        row0 = 16 * ((t & 1) ^ tree)
        for f in range(6):
            for r in range(2):
                for h in range(2):
                    rows = pl.ds(pl.multiple_of(row0 + 8 * r, 8), 8)
                    ext[f, 2 * bj + h, bk, rows, :] = old_slice(old, f, slot, 8 * r, h)
    high = gi % 2 == 1
    row0 = jnp.where(high, 8, 0)
    slot_a = jnp.where(even, 8 + off, 0)
    bit = jnp.where(even, 0, 1)
    for h in range(2):
        groups = slab_groups(lambda f: old_slice(old, f, slot_a, row0, h), high, sub)
        for g in range(4):
            mine[g * 2 + h] = groups[g]
        for q in range(4):
            slot = jnp.clip(bit + 2 * q + off, 0, 9)
            groups = slab_groups(lambda f: old_slice(old, f, slot, row0, h), high, sub)
            for g in range(4):
                ib[(g * 4 + q) * 2 + h] = groups[g]
    odd = jnp.logical_not(even)
    first, last = bounds[d] == 8 * d + 1, bounds[d + 1] == 8 * d + 7
    values = (
        first,
        last,
        even & (bounds[d + 1] == 8 * d + 9),
        odd & (bounds[d] == 8 * d - 1),
        even & first,
        odd & last,
    )
    for n, value in enumerate(values):
        flags[n] = jnp.full((8, 128), jnp.where(value, 1.0, 0.0), F32)


def second_kernel(ib_in, flags, rb, ra, peak, x16, x17, coef, ib, peak_out):
    d, tree, gi, gj, gk = where_am_i()
    sub, lane = iotas()
    high = gi % 2 == 1
    block = jnp.where(high, 2, 0)
    for q in range(4):
        for h in range(2):
            if q in (0, 3):
                groups = slab_groups(lambda f: rb[f * 4 + block + h], high, sub)
                flag = flags[4 if q == 0 else 5] > 0.5
            for g in range(4):
                n = (g * 4 + q) * 2 + h
                ib[n] = jnp.where(flag, groups[g], ib_in[n]) if q in (0, 3) else ib_in[n]
    peak_out[0] = jnp.maximum(jnp.maximum(peak[0], ra[56]), jnp.maximum(x16[0], x17[0]))


def block_kernel(own, mine, flags, ra, rb, ext, ia):
    d, tree, gi, gj, gk = where_am_i()
    even = d % 2 == 0
    flag = [flags[n] > 0.5 for n in range(4)]
    ext[...] = own[...]
    for t, missing in ((0, flag[0]), (7, flag[1])):
        bj, bk = (t >> 1) & 1, (t >> 2) & 1
        row0 = 16 * ((t & 1) ^ tree)
        use_b = even if t == 0 else jnp.logical_not(even)
        for f in range(6):
            for r in range(2):
                for h in range(2):
                    n = f * 4 + r * 2 + h
                    rows = pl.ds(pl.multiple_of(row0 + 8 * r, 8), 8)
                    came = jnp.where(use_b, rb[n], ra[n])
                    ext[f, 2 * bj + h, bk, rows, :] = jnp.where(
                        missing, came, own[f, 2 * bj + h, bk, rows, :]
                    )
    for q in range(4):
        for h in range(2):
            for g in range(4):
                n = (g * 4 + q) * 2 + h
                x = ra[24 + n]
                if q == 0:
                    x = jnp.where(flag[2], mine[g * 2 + h], x)
                if q == 3:
                    x = jnp.where(flag[3], mine[g * 2 + h], x)
                ia[n] = x


def make_block(ext, ia, ib, gi, sub):
    first_high = gi % 2 == 0

    def pair(g, jq, kt):
        n = (g * 4 + jq // 2 + 2 * kt) * 2 + jq % 2
        a, b = ia[n], ib[n]
        return jnp.where(first_high, a, b), jnp.where(first_high, b, a)

    def rows(f, jq, kt, b):
        if b < 4:
            return ext[f, jq, kt, pl.ds(8 * b, 8), :]
        if f == 0:
            return pair(0, jq, kt)[b - 4]
        hi, lo = pair((1, 1, 2, 2, 3, 3)[f], jq, kt)
        if f in (3, 4):
            return rs(jnp.where(sub < 4, lo, hi), 4)
        return jnp.where(sub < 4, hi, lo)

    return rows, pair


J_BLOCKS = 37


def j_place(f, kt, b):
    if f == 0:
        return kt * 6 + b
    if f == 5:
        return 32 + b
    return (12 if f in (2, 4) else 22) + kt * 5 + b


def third_kernel(ext, ia, ib, peak, x64, ja, jb, peak_out):
    d, tree, gi, gj, gk = where_am_i()
    sub, lane = iotas()
    rows, _ = make_block(ext, ia, ib, gi, sub)
    even = gj % 2 == 0

    def put(f, kt, b, get):
        lo, hi = get(0), get(3)
        ja[j_place(f, kt, b)] = jnp.where(even, hi, lo)
        jb[j_place(f, kt, b)] = jnp.where(even, lo, hi)

    for b in range(6):
        for kt in range(2):
            put(0, kt, b, lambda jq: rows(0, jq, kt, b))
    for b in range(5):
        for kt in range(2):
            def five(jq):
                nat = lane < 80 if jq == 0 else lane >= 48
                turn = 80 if jq == 0 else -80
                return jnp.where(nat, rows(2, jq, kt, b), rl(rows(4, jq, kt, b), turn))

            def four(jq):
                nat = lane < 64 if jq == 0 else lane >= 64
                return jnp.where(nat, rows(1, jq, kt, b), rl(rows(3, jq, kt, b), 64))

            put(2, kt, b, five)
            put(1, kt, b, four)

        def both(jq):
            nat = lane < 64 if jq == 0 else lane >= 64
            return jnp.where(nat, rows(5, jq, 0, b), rl(rows(5, jq, 1, b), 64))

        put(5, 0, b, both)
    top = jnp.maximum(peak[0], x64[0])
    ja[J_BLOCKS] = top
    jb[J_BLOCKS] = top
    peak_out[0] = top


def make_wide(rows, ja, jb, gj):
    first_high = gj % 2 == 0

    def wide(f, jq, kt, b):
        if jq < 4:
            return rows(f, jq, kt, b)
        n = j_place(f, kt, b)
        if jq == 4:
            x = jnp.where(first_high, ja[n], jb[n])
        else:
            x = jnp.where(first_high, jb[n], ja[n])
        if f == 4:
            return rl(x, -80 if jq == 4 else 80)
        return rl(x, 64) if f == 3 or (f == 5 and kt == 1) else x

    return wide


K_BLOCKS = 38


def k_place(kind, jt, b):
    if jt == 2:
        return 30 + b
    return (0, 10, 10, 20, 20)[kind] + jt * 5 + b


class KPack:
    def __init__(self, gk, lane):
        self.even = gk % 2 == 0
        self.near = lane % 16 < 8
        self.k8 = lane % 8

    def put(self, ka, kb, n, lo, hi):
        ka[n] = jnp.where(self.even, hi, lo)
        kb[n] = jnp.where(self.even, lo, hi)

    def squeeze(self, first, last, kt):
        if kt == 0:
            return jnp.where(self.near, first, rl(last, 8))
        return jnp.where(self.near, rl(first, -8), last)

    def join(self, kind, value, kt):
        if kind == 0:
            return value(0)
        if kind == 1:
            nat, turn = (self.k8 < 5, 5) if kt == 0 else (self.k8 >= 3, -5)
        else:
            nat, turn = (self.k8 < 4, 4) if kt == 0 else (self.k8 >= 4, -4)
        return jnp.where(nat, value(kind), rl(value(kind + 1), turn))

    def block(self, kinds, get, ka, kb):
        for jt in range(2):
            for kind in kinds:
                for b in range(5):
                    sides = []
                    for kt in range(2):

                        def value(n):
                            one, two = get(n, 2 * jt, kt, b), get(n, 2 * jt + 1, kt, b)
                            return self.squeeze(one, two, kt)

                        sides.append(self.join(kind, value, kt))
                    self.put(ka, kb, k_place(kind, jt, b), *sides)

    def halo(self, get, ka, kb):
        for n in range(8):
            sides = []
            for kt in range(2):
                packs = []
                for m in (n, min(n + 8, 14)):
                    kind, b = (0, 1, 3)[m // 5], m % 5
                    packs.append(self.join(kind, lambda f: get(f, kt, b), kt))
                sides.append(self.squeeze(*packs, kt))
            self.put(ka, kb, 30 + n, *sides)


def coefficient_kernel(neighbours, levels, refine, out, table):
    d, tree, gi, gj, gk = where_am_i()
    sub, lane = iotas()

    def one(pos, carry):
        ip, jp, kp = pos >> 4, (pos >> 2) & 3, pos & 3
        x = 2 * gi + jnp.where(ip == 3, -1, ip)
        y = 2 * gj + jnp.where(jp == 3, -1, jp)
        z = 2 * gk + jnp.where(kp == 3, -1, kp)
        inside = (x >= 0) & (x < 16) & (y >= 0) & (y < 8) & (z >= 0) & (z < 8)
        upper = x >= 8
        lx = jnp.where(upper, 15 - x, x)
        code = jnp.where(upper, 512, 0)
        for bit in range(3):
            for axis, v in enumerate((lx, y, z)):
                code = code | (((v >> bit) & 1) << (3 * bit + axis))
        code = jnp.where(inside, code, 0)
        level = levels[code]
        depth = level + refine[code]
        for axis in range(3):
            opened = inside & (neighbours[code * 6 + 2 * axis + 1] >= 0)
            table[axis * 64 + pos] = jnp.where(opened, 1.0, 0.0)
        table[3 * 64 + pos] = jnp.left_shift(1, level).astype(F32)
        table[4 * 64 + pos] = jnp.left_shift(1, 3 - depth).astype(F32)
        return carry

    lax.fori_loop(0, 64, one, 0, unroll=4)
    turns = {0: (0, 1, 2, 3), -1: (3, 0, 1, 3), 1: (1, 2, 2, 0)}

    def spread(item, axis=0, step=0):
        maps = [turns[step if a == axis else 0] for a in range(3)]
        made = []
        for jp in range(4):
            vals = []
            for ip in range(4):
                n = item * 64 + maps[0][ip] * 16 + maps[1][jp] * 4
                v = [jnp.full((8, 128), table[n + maps[2][kp]], F32) for kp in range(4)]
                vals.append((v[0], v[1], jnp.where(lane % 16 < 8, v[2], v[3])))
            made.append(
                [
                    (vals[0][kt], vals[1][kt], jnp.where(sub < 4, vals[2][kt], vals[3][kt]))
                    for kt in range(3)
                ]
            )
        last = [
            [jnp.where(lane < 64, made[2][kt][n], made[3][kt][n]) for n in range(3)]
            for kt in range(3)
        ]
        return made[0], made[1], last

    places = [(jt, kt, n) for jt in range(3) for kt in range(3) for n in range(3)]
    size, inverse = spread(4), spread(3)
    for jt, kt, n in places:
        e = size[jt][kt][n]
        out[12, jt, kt, n] = inverse[jt][kt][n]
        out[13, jt, kt, n] = e * e * (1.0 / 32.0)
    for axis in range(3):
        for side, step in ((0, -1), (1, 1)):
            opened = spread(axis, axis, -1) if side == 0 else spread(axis)
            other = spread(4, axis, step)
            for jt, kt, n in places:
                e, m = size[jt][kt][n], opened[jt][kt][n]
                ratio = (2.0 * e) / (e + other[jt][kt][n])
                out[2 * axis + side, jt, kt, n] = m
                out[6 + 2 * axis + side, jt, kt, n] = jnp.where(m > 0.5, ratio, 1.0)


def coefficient(coef, item, jt, kt):
    a, b, c = (coef[item, jt, kt, n] for n in range(3))
    return jnp.concatenate([a, a, b, b, c], axis=0)


def minmod(a, b):
    return jnp.maximum(jnp.minimum(a, b), 0.0) + jnp.minimum(jnp.maximum(a, b), 0.0)


def face_change(c, up1, up2, dn1, dn2, u, u_up, u_dn):
    upper, lower = up1 - c, c - dn1
    half = 0.5 * minmod(upper, lower)
    half_up = 0.5 * minmod(up2 - up1, upper)
    half_dn = 0.5 * minmod(lower, dn1 - dn2)
    w_up, w_dn = 0.5 * (u + u_up), 0.5 * (u_dn + u)
    flux_up = jnp.maximum(w_up, 0.0) * (c + half) + jnp.minimum(w_up, 0.0) * (up1 - half_up)
    flux_dn = jnp.maximum(w_dn, 0.0) * (dn1 + half_dn) + jnp.minimum(w_dn, 0.0) * (c - half)
    return flux_up - flux_dn


def wrap48(x, sub):
    return jnp.concatenate([x[:32], jnp.where(sub < 4, x[32:40], x[40:48])], axis=0)


class Shifts:
    def __init__(self):
        self.sub, self.lane = iotas()
        self.row = lax.broadcasted_iota(jnp.int32, (40, 128), 0)
        self.lane5 = lax.broadcasted_iota(jnp.int32, (40, 128), 1)
        self.k16 = self.lane5 % 16
        row = self.row
        self.i_top1 = (row == 15) | (row == 31) | (row == 39)
        self.i_top2 = self.i_top1 | (row == 14) | (row == 30) | (row == 38)
        self.i_bot1 = (row == 0) | (row == 16) | (row == 32)
        self.i_bot2 = self.i_bot1 | (row == 1) | (row == 17) | (row == 33)

    def wrap(self, x):
        return wrap48(x, self.sub)

    def k_up(self, x, nxt, n, m=None):
        nxt = rl(nxt, 16 - n)
        return jnp.where(self.k16 < 16 - n, rl(x, -n), nxt if m is None else m * nxt)

    def k_dn(self, x, prv, n, m=None):
        prv = rl(prv, n - 16)
        return jnp.where(self.k16 >= n, rl(x, n), prv if m is None else m * prv)

    def j_up(self, x, nxt, n):
        return rl(jnp.where(self.lane5 < 16 * n, nxt, x), -16 * n)

    def j_dn(self, x, prv, n):
        return rl(jnp.where(self.lane5 >= 128 - 16 * n, prv, x), 16 * n)

    def change_j(self, c, cn, cp, u, un, up, m_dn, m_up):
        lane5 = self.lane5

        def masked(x, m, at):
            return x if m is None else x * jnp.where(at, m, 1.0)

        return face_change(
            c,
            masked(self.j_up(c, cn, 1), m_up, lane5 >= 112),
            masked(self.j_up(c, cn, 2), m_up, lane5 >= 96),
            masked(self.j_dn(c, cp, 1), m_dn, lane5 < 16),
            masked(self.j_dn(c, cp, 2), m_dn, lane5 < 32),
            u,
            masked(self.j_up(u, un, 1), m_up, lane5 >= 112),
            masked(self.j_dn(u, up, 1), m_dn, lane5 < 16),
        )

    def change_i(self, c48, v48, m_dn, m_up):
        up_m1, up_m2 = jnp.where(self.i_top1, m_up, 1.0), jnp.where(self.i_top2, m_up, 1.0)
        dn_m1, dn_m2 = jnp.where(self.i_bot1, m_dn, 1.0), jnp.where(self.i_bot2, m_dn, 1.0)
        wrap = self.wrap
        return face_change(
            wrap(c48), wrap(rs(c48, -1)) * up_m1, wrap(rs(c48, -2)) * up_m2,
            wrap(rs(c48, 1)) * dn_m1, wrap(rs(c48, 2)) * dn_m2,
            wrap(v48), wrap(rs(v48, -1)) * up_m1, wrap(rs(v48, 1)) * dn_m1,
        )


def inner_kernel(ext, ia, ib, coef, c40, u2, src, prs, u1, chg, ka, kb):
    d, tree, gi, gj, gk = where_am_i()
    sh = Shifts()
    rows, pair = make_block(ext, ia, ib, gi, sh.sub)
    dest = {0: c40, 2: u1, 3: u2, 4: src, 5: prs}
    for jq in range(4):
        for kt in range(2):
            jt = jq // 2
            c48 = jnp.concatenate([rows(0, jq, kt, b) for b in range(6)], axis=0)
            v48 = jnp.concatenate(
                [rows(1, jq, kt, b) for b in range(4)] + list(pair(1, jq, kt)), axis=0
            )
            for f, ref in dest.items():
                if f == 0:
                    ref[jq, kt] = sh.wrap(c48)
                else:
                    ref[jq, kt] = jnp.concatenate([rows(f, jq, kt, b) for b in range(5)], axis=0)
            m_dn, m_up = coefficient(coef, 0, jt, kt), coefficient(coef, 1, jt, kt)
            chg[jq, kt] = sh.change_i(c48, v48, m_dn, m_up)
    for jq in (1, 2):
        for kt in range(2):
            m_dn = coefficient(coef, 2, jq // 2, kt) if jq == 2 else None
            m_up = coefficient(coef, 3, jq // 2, kt) if jq == 1 else None
            chg[jq, kt] = chg[jq, kt] + sh.change_j(
                c40[jq, kt], c40[jq + 1, kt], c40[jq - 1, kt],
                u1[jq, kt], u1[jq + 1, kt], u1[jq - 1, kt], m_dn, m_up,
            )
    kinds = (c40, u2, src)
    KPack(gk, sh.lane).block(
        (0, 1), lambda kind, jq, kt, b: kinds[kind][jq, kt, pl.ds(8 * b, 8), :], ka, kb
    )


def outer_kernel(
    ja, jb, peak, x8, x10, coef, c_in, u2_in, src_in, prs_in, u1_in, chg_in, ka_in, kb_in,
    c40, u2, src, prs, chg, ka, kb, peak_out,
):
    d, tree, gi, gj, gk = where_am_i()
    sh = Shifts()
    wide = make_wide(None, ja, jb, gj)
    low5 = sh.lane5 < 64
    low6 = lax.broadcasted_iota(jnp.int32, (48, 128), 1) < 64
    for jq in range(4):
        for kt in range(2):
            c40[jq, kt], u2[jq, kt] = c_in[jq, kt], u2_in[jq, kt]
            src[jq, kt], prs[jq, kt] = src_in[jq, kt], prs_in[jq, kt]
            if jq in (1, 2):
                chg[jq, kt] = chg_in[jq, kt]
    for n in range(20):
        ka[n], kb[n] = ka_in[n], kb_in[n]

    def whole(f, jq, kt, count=5):
        return jnp.concatenate([wide(f, jq, kt, b) for b in range(count)], axis=0)

    for kt in range(2):
        for f, ref in ((3, u2), (4, src), (5, prs)):
            ref[4, kt] = jnp.where(low5, whole(f, 4, kt), whole(f, 5, kt))
        c48 = [whole(0, jq, kt, 6) for jq in (4, 5)]
        c_high, c_low = sh.wrap(c48[0]), sh.wrap(c48[1])
        c40[4, kt] = jnp.where(low5, c_high, c_low)
        u_high, u_low = whole(2, 4, kt), whole(2, 5, kt)
        m_dn, m_up = coefficient(coef, 0, 2, kt), coefficient(coef, 1, 2, kt)
        v40 = jnp.where(low5, whole(1, 4, kt), whole(1, 5, kt))
        v48 = jnp.concatenate([v40, v40[32:]], axis=0)
        along_i = sh.change_i(jnp.where(low6, c48[0], c48[1]), v48, m_dn, m_up)
        m_dn, m_up = coefficient(coef, 2, 2, kt), coefficient(coef, 3, 2, kt)
        high = sh.change_j(c_high, c_low, c_in[3, kt], u_high, u_low, u1_in[3, kt], m_dn, None)
        low = sh.change_j(c_low, c_in[0, kt], c_high, u_low, u1_in[0, kt], u_high, None, m_up)
        chg[4, kt] = along_i + jnp.where(low5, high, low)
        chg[0, kt] = chg_in[0, kt] + sh.change_j(
            c_in[0, kt], c_in[1, kt], c_low, u1_in[0, kt], u1_in[1, kt], u_low,
            coefficient(coef, 2, 0, kt), None,
        )
        chg[3, kt] = chg_in[3, kt] + sh.change_j(
            c_in[3, kt], c_high, c_in[2, kt], u1_in[3, kt], u_high, u1_in[2, kt],
            None, coefficient(coef, 3, 1, kt),
        )
    kinds = (c40, u2, src, chg, prs)
    pack = KPack(gk, sh.lane)
    pack.block((3,), lambda kind, jq, kt, b: kinds[kind][jq, kt, pl.ds(8 * b, 8), :], ka, kb)
    pack.halo(lambda kind, kt, b: kinds[kind][4, kt, pl.ds(8 * b, 8), :], ka, kb)
    top = jnp.maximum(
        jnp.maximum(jnp.maximum(peak[0], x8[0]), x10[0]),
        jnp.maximum(ja[J_BLOCKS], jb[J_BLOCKS]),
    )
    ka[K_BLOCKS] = top
    kb[K_BLOCKS] = top
    peak_out[0] = top


def main_kernel(
    c_in, u_in, s_in, p_in, chg_in, ka, kb, peak, x32, coef,
    out_adv, out_p, send_a, send_b,
    c_k, u2, src, p_k, chg_k, p0, p1, adv, mob, hgt, rhs, wts,
):
    d, tree, gi, gj, gk = where_am_i()
    sh = Shifts()
    sub, lane, lane5, k16 = sh.sub, sh.lane, sh.lane5, sh.k16
    near = lane % 16 < 8
    k_even = gk % 2 == 0
    dest = (c_k, u2, src, chg_k, p_k)

    def both_sides(n):
        a, e = ka[n], kb[n]
        return jnp.where(k_even, a, e), jnp.where(k_even, e, a)

    for kind in (0, 1, 3):
        turn = (0, 5, 0, 4)[kind]
        for b in range(5):
            rows = pl.ds(8 * b, 8)
            for n in range(1 if kind == 0 else 2):
                ref = dest[kind + n]
                for jt in range(2):
                    low, high = both_sides(k_place(kind, jt, b))
                    if n == 1:
                        low, high = rl(low, -turn), rl(high, turn)
                    ref[2 * jt, rows, :] = jnp.where(near, low, rl(high, 8))
                    ref[2 * jt + 1, rows, :] = jnp.where(near, rl(low, -8), high)
                m = (0, 1, 0, 2)[kind] * 5 + b
                low, high = both_sides(30 + m % 8)
                if m < 8:
                    high = rl(high, 8)
                else:
                    low = rl(low, -8)
                if n == 1:
                    low, high = rl(low, -turn), rl(high, turn)
                ref[4, rows, :] = jnp.where(near, low, high)

    def c40(jq, kt):
        return c_k[jq] if kt == 2 else c_in[jq, kt]

    def uk(jq, kt):
        return u2[jq] if kt == 2 else u_in[jq, kt]

    top = jnp.maximum(
        jnp.maximum(peak[0], x32[0]), jnp.maximum(ka[K_BLOCKS], kb[K_BLOCKS])
    )
    top = jnp.max(top, keepdims=True)
    step = jnp.broadcast_to(CFL / top, (8, 128))
    step = jnp.concatenate([step] * 5, axis=0)

    for jq in range(5):
        jt = jq // 2
        for kt in range(3):
            kn, kp = (kt + 1) % 3, (kt + 2) % 3
            change = chg_k[jq] if kt == 2 else chg_in[jq, kt]
            c = c40(jq, kt)
            m_dn, m_up = coefficient(coef, 4, jt, kt), coefficient(coef, 5, jt, kt)
            cn, cp = c40(jq, kn), c40(jq, kp)
            up1, up2 = sh.k_up(c, cn, 1, m_up), sh.k_up(c, cn, 2, m_up)
            dn1, dn2 = sh.k_dn(c, cp, 1, m_dn), sh.k_dn(c, cp, 2, m_dn)
            hgt[jq, kt] = dn2 + dn1 + c + up1 + up2
            u = uk(jq, kt)
            u_up, u_dn = sh.k_up(u, uk(jq, kn), 1, m_up), sh.k_dn(u, uk(jq, kp), 1, m_dn)
            change = change + face_change(c, up1, up2, dn1, dn2, u, u_up, u_dn)
            a = jnp.clip(c - step * coefficient(coef, 12, jt, kt) * change, 0.0, 1.0)
            adv[jq, kt] = a
            mob[jq, kt] = 1.0 / (RHO_GAS + (RHO_LIQ - RHO_GAS) * a)

    k_bot, k_top, j_bot, j_top = k16 < 1, k16 >= 15, lane5 < 16, lane5 >= 112
    for jq in range(5):
        jt, jn, jp = jq // 2, (jq + 1) % 5, (jq + 4) % 5
        edges = (
            sh.i_bot1, sh.i_top1,
            j_bot if jq % 2 == 0 else None, j_top if jq in (1, 3, 4) else None,
            k_bot, k_top,
        )
        for kt in range(3):
            kn, kp = (kt + 1) % 3, (kt + 2) % 3
            opened = [None if e is None else coefficient(coef, f, jt, kt) for f, e in enumerate(edges)]

            def masked(x, f):
                return x if edges[f] is None else x * jnp.where(edges[f], opened[f], 1.0)

            h = hgt[jq, kt]
            h_up, h_dn = masked(rs(h, -1), 1), masked(rs(h, 1), 0)
            gx, sx = 0.5 * (h_up - h_dn), h_up - 2.0 * h + h_dn
            h_up = masked(sh.j_up(h, hgt[jn, kt], 1), 3)
            h_dn = masked(sh.j_dn(h, hgt[jp, kt], 1), 2)
            gy, sy = 0.5 * (h_up - h_dn), h_up - 2.0 * h + h_dn
            gx2, gy2 = gx * gx, gy * gy
            root = lax.rsqrt(1.0 + gx2 + gy2)
            bend = (sx * (1.0 + gy2) + sy * (1.0 + gx2)) * coefficient(coef, 12, jt, kt)
            bend = bend * (root * root * root)
            right = (src[jq] if kt == 2 else s_in[jq, kt]) - SIGMA * bend * adv[jq, kt]
            m = mob[jq, kt]
            across = (
                rs(m, 1), rs(m, -1),
                sh.j_dn(m, mob[jp, kt], 1), sh.j_up(m, mob[jn, kt], 1),
                sh.k_dn(m, mob[jq, kp], 1), sh.k_up(m, mob[jq, kn], 1),
            )
            closed = jnp.zeros_like(m)
            diag = jnp.zeros_like(m)
            parts = []
            for f in range(6):
                part = m + across[f]
                if edges[f] is not None:
                    ratio = coefficient(coef, 6 + f, jt, kt)
                    part = part * jnp.where(edges[f], ratio * opened[f], 1.0)
                    closed = closed + jnp.where(edges[f], 1.0 - opened[f], 0.0)
                diag = diag + part
                parts.append(part)
            inv = 1.0 / (diag + closed * m)
            for f in range(6):
                wts[f, jq, kt] = parts[f] * inv
            rhs[jq, kt] = right * coefficient(coef, 13, jt, kt) * inv

    for sweep in range(SWEEPS):
        new = p0 if sweep % 2 == 0 else p1
        older = p1 if sweep % 2 == 0 else p0
        last = sweep == SWEEPS - 1

        def old(jq, kt):
            if sweep:
                return older[jq, kt]
            return p_k[jq] if kt == 2 else p_in[jq, kt]

        for jq in range(4 if last else 5):
            jn, jp = (jq + 1) % 5, (jq + 4) % 5
            for kt in range(2 if last or (sweep == SWEEPS - 2 and jq == 4) else 3):
                kn, kp = (kt + 1) % 3, (kt + 2) % 3
                p = old(jq, kt)
                total = wts[0, jq, kt] * rs(p, 1) + wts[1, jq, kt] * rs(p, -1)
                total = total + wts[2, jq, kt] * sh.j_dn(p, old(jp, kt), 1)
                total = total + wts[3, jq, kt] * sh.j_up(p, old(jn, kt), 1)
                total = total + wts[4, jq, kt] * sh.k_dn(p, old(jq, kp), 1)
                total = total + wts[5, jq, kt] * sh.k_up(p, old(jq, kn), 1)
                total = total - rhs[jq, kt]
                if last:
                    out_p[jq, kt] = total[:32]
                    out_adv[jq, kt] = adv[jq, kt][:32]
                else:
                    new[jq, kt] = total

    even = d % 2 == 0
    for h in range(2):
        for n, ref in enumerate((out_adv, out_p)):
            low, high = tile_half(ref, 0, h, tree), tile_half(ref, 7, h, tree)
            send_a[n, :, halves(h)] = jnp.where(even, high, low)
            send_b[n, :, halves(h)] = jnp.where(even, low, high)


def tile_half(ref, t, h, tree):
    row0 = pl.multiple_of(16 * ((t & 1) ^ tree), 16)
    return ref[2 * ((t >> 1) & 1) + h, (t >> 2) & 1, pl.ds(row0, 16), :]


def slots_kernel(adv, prs, bounds, vof, pres):
    d, tree, gi, gj, gk = where_am_i()
    start = bounds[d]
    count = bounds[d + 1] - start
    off = 8 * d - start
    vof[...] = jnp.zeros_like(vof)
    pres[...] = jnp.zeros_like(pres)
    for t in range(8):
        slot = t + off

        @pl.when((slot >= 0) & (slot < count))
        def _(t=t, slot=slot):
            for h in range(2):
                vof[slot, :, halves(h)] = tile_half(adv, t, h, tree)
                pres[slot, :, halves(h)] = tile_half(prs, t, h, tree)


VM = pl.BlockSpec(memory_space=pltpu.VMEM)
SM = pl.BlockSpec(memory_space=pltpu.SMEM)


def shape(*dims):
    return jax.ShapeDtypeStruct(dims, F32)


def blocks(n):
    return shape(n, 8, 128)


def call(kernel, specs, outs, args, scratch=(), micros=1, mib=8):
    return pl.pallas_call(
        kernel,
        out_shape=outs,
        in_specs=specs,
        out_specs=jax.tree.map(lambda _: VM, outs),
        scratch_shapes=list(scratch),
        compiler_params=pltpu.CompilerParams(vmem_limit_bytes=mib * 1024 * 1024),
        cost_estimate=pl.CostEstimate(
            flops=micros * 100000, bytes_accessed=micros * 100000, transcendentals=0
        ),
    )(*args)


def local(volume, velocity, source, pressure_prev, neighbours, levels, refine, bounds_old, bounds_new):
    d = lax.axis_index("row") * 16 + lax.axis_index("col")
    one = blocks(1)
    old = jnp.concatenate([volume[None], velocity, source[None], pressure_prev[None]], axis=0)
    ra, rb, peak = call(
        first_kernel, [VM, SM, SM], (blocks(57), blocks(24), one), (old, levels, bounds_old)
    )
    x16, x17 = send(peak, flip_pairs(16)), send(peak, flip_pairs(17))
    rb, ra = send(rb, ODD_PAIRS), send(ra, EVEN_PAIRS)
    own, mine, flags, ib = call(
        own_kernel,
        [VM, SM],
        (shape(6, 4, 2, 32, 128), blocks(8), blocks(FLAG_COUNT), blocks(32)),
        (old, bounds_old),
    )
    coef = call(
        coefficient_kernel,
        [SM] * 3,
        shape(14, 3, 3, 3, 8, 128),
        (neighbours.reshape(-1), levels, refine),
        [pltpu.SMEM((5 * 64,), F32)],
        5,
    )
    ib, peak = call(
        second_kernel,
        [VM] * 7 + [pl.BlockSpec(memory_space=pl.ANY)],
        (blocks(32), one),
        (ib, flags, rb, ra, peak, x16, x17, coef),
    )
    x64 = send(peak, flip_pairs(64))
    ib = send(ib, axis_pairs(0, 1))
    ext, ia = call(
        block_kernel,
        [VM] * 5,
        (shape(6, 4, 2, 32, 128), blocks(32)),
        (own, mine, flags, ra, rb),
    )
    ja, jb, peak = call(
        third_kernel,
        [VM] * 5,
        (blocks(J_BLOCKS + 1), blocks(J_BLOCKS + 1), one),
        (ext, ia, ib, peak, x64),
    )
    x8, x10 = send(peak, flip_pairs(8)), send(peak, flip_pairs(10))
    ja, jb = send(ja, axis_pairs(1, 0)), send(jb, axis_pairs(1, 1))
    inner = call(
        inner_kernel,
        [VM] * 4,
        (shape(4, 2, 40, 128),) * 6 + (blocks(20),) * 2,
        (ext, ia, ib, coef),
        (),
        2,
    )
    *early, ka, kb, peak = call(
        outer_kernel,
        [VM] * 14,
        (shape(5, 2, 40, 128),) * 5 + (blocks(K_BLOCKS + 1),) * 2 + (one,),
        (ja, jb, peak, x8, x10, coef, *inner),
        (),
        1,
    )
    x32 = send(peak, flip_pairs(32))
    ka, kb = send(ka, axis_pairs(2, 0)), send(kb, axis_pairs(2, 1))
    halo, grid = (5, 40, 128), (5, 3, 40, 128)
    adv, prs, sa, sb = call(
        main_kernel,
        [VM] * 10,
        (shape(4, 2, 32, 128),) * 2 + (shape(2, 16, 256),) * 2,
        (*early, ka, kb, peak, x32, coef),
        [pltpu.VMEM(halo, F32)] * 5
        + [pltpu.VMEM(grid, F32)] * 6
        + [pltpu.VMEM((6, *grid), F32)],
        8,
        16,
    )
    sb, sa = send(sb, ODD_PAIRS), send(sa, EVEN_PAIRS)
    vof, pres = call(slots_kernel, [VM] * 2 + [SM], (shape(10, 16, 256),) * 2, (adv, prs, bounds_new))
    even = d % 2 == 0
    low, high = jnp.where(even, sb, sa), jnp.where(even, sa, sb)
    start, stop = bounds_new[d], bounds_new[d + 1]
    slots = jnp.arange(10, dtype=jnp.int32)
    at_low = ((slots == 0) & (start == 8 * d - 1))[:, None, None]
    at_high = ((slots == 8 * d + 8 - start) & (stop == 8 * d + 9))[:, None, None]
    outs = [
        jnp.where(at_low, low[n][None], jnp.where(at_high, high[n][None], x))
        for n, x in enumerate((vof, pres))
    ]
    return tuple(outs)


def solution(mesh):
    in_specs = (
        P(AXES, None, None),
        P(None, AXES, None, None),
        P(AXES, None, None),
        P(AXES, None, None),
        P(),
        P(),
        P(),
        P(),
        P(),
    )
    out_specs = (P(AXES, None, None), P(AXES, None, None))
    return jax.shard_map(local, mesh=mesh, in_specs=in_specs, out_specs=out_specs, check_vma=False)
```
